32 devices in a mesh: lon: 16 (over z, y, core), lat: 2 (over x).
Axes of the slice: x: 2, y: 2, z: 4, core: 2. Of those that a mesh axis runs over, the one named last changes fastest.
Arguments:
- field: bfloat16 [96, 32, 2048], P(None, 'lat', 'lon'), may hold values from -6 to 6
- land_mask: int32 [32, 2048], P('lat', 'lon'), may hold values from 0 to 1, as said below
- depth_kernel: float32 [2, 96, 7, 7], replicated, may hold values from -0.875 to 0.875
- depth_bias: float32 [2, 96], replicated, may hold values from -3 to 3
- norm_gain: float32 [2, 96], replicated, may hold values from 0.1 to 1.9
- norm_bias: float32 [2, 96], replicated, may hold values from -3 to 3
- w_expand: bfloat16 [2, 384, 96], replicated, may hold values from -0.625 to 0.625
- b_expand: float32 [2, 384], replicated, may hold values from -3 to 3
- w_reduce: bfloat16 [2, 96, 384], replicated, may hold values from -0.3125 to 0.3125
- b_reduce: float32 [2, 96], replicated, may hold values from -3 to 3
Outputs:
- output_field: bfloat16 [96, 32, 2048], P(None, 'lat', 'lon')
The draws below stay inside these ranges and needn't reach their ends.
Inputs may be any that keep to these rules, and one draw needn't show every extreme that they name: `land_mask`: land and ocean come in regions; some aligned blocks of 8 rows and 128 columns are all land.
All inputs are finite; a program needn't handle non-finite values.
Results may differ from the reference program's by a relative error of at most 0.0058.
Values may be sent and summed in bfloat16 or wider, within the bound.
No kernel may reach another device: no remote copies, remote signals or barrier semaphores. Data moves between devices by JAX's collectives and lax.ppermute only.
A program may use at most 64 MiB of HBM per device.

```python
import jax
import jax.numpy as jnp
from jax import lax

C = 96
HID = 384
LAYERS = 2
CLON = 128
NLAT = 32
NLON = 2048


def draw_land_mask(key, part):
    key = jax.random.fold_in(key, 11)
    region_key, cell_key = jax.random.split(key)
    row_blocks = NLAT // 8
    col_blocks = NLON // CLON
    region_kind = jax.random.randint(region_key, (row_blocks, col_blocks), 0, 4)
    cell_draw = jax.random.randint(cell_key, (NLAT, NLON), 0, 4)
    region_full = jnp.repeat(jnp.repeat(region_kind, 8, axis=0), CLON, axis=1)
    ocean_cells = (region_full == 3) | (region_full > 0) & (cell_draw > 0)
    return ocean_cells.astype(jnp.int32)


def steps_of(rng, extent, cuts, least, high):
    gain, own = 1.0, jax.random.fold_in(rng, 6)
    for axis_at, parts in cuts:
        steps = jnp.exp(jax.random.uniform(jax.random.fold_in(own, axis_at), (parts,), jnp.float32, least / len(cuts), high / len(cuts)))
        gain = gain * jnp.repeat(steps, extent[axis_at] // parts).reshape([-1 if axis == axis_at else 1 for axis in range(len(extent))])
    return gain


def bell_draw(rng, extent, deviation, reach, pieces=(), held_as=jnp.bfloat16):
    values = jax.random.normal(rng, extent, jnp.float32) * deviation
    if len(pieces) > 0:
        values = steps_of(rng, extent, pieces, -0.22, 0.18) * values
    return jnp.clip(values, min=-reach, max=reach).astype(held_as)


def setup_inputs(seed: int = 0) -> dict:
    splits = jax.random.split(jax.random.key(seed), 11)
    field = bell_draw(splits[0], (C, NLAT, NLON), 1.0, 6.0, ((1, 2), (2, 16)))
    land_mask = draw_land_mask(jax.random.fold_in(splits[10], 71), 0)
    depth_kernel = bell_draw(splits[2], (LAYERS, C, 7, 7), 49 ** -0.5, 0.875, (), jnp.float32)
    depth_bias = bell_draw(splits[3], (LAYERS, C), 0.5, 3.0, (), jnp.float32)
    norm_gain = jnp.clip(1.0 + 0.18 * jax.random.normal(splits[4], (LAYERS, C), jnp.float32), 0.1, 1.9)
    norm_bias = bell_draw(splits[5], (LAYERS, C), 0.5, 3.0, (), jnp.float32)
    w_expand = bell_draw(splits[6], (LAYERS, HID, C), C ** -0.5, 0.625)
    b_expand = bell_draw(splits[7], (LAYERS, HID), 0.5, 3.0, (), jnp.float32)
    w_reduce = bell_draw(splits[8], (LAYERS, C, HID), HID ** -0.5, 0.3125)
    b_reduce = bell_draw(splits[9], (LAYERS, C), 0.5, 3.0, (), jnp.float32)
    return dict(field=field, land_mask=land_mask, depth_kernel=depth_kernel, depth_bias=depth_bias, norm_gain=norm_gain, norm_bias=norm_bias, w_expand=w_expand, b_expand=b_expand, w_reduce=w_reduce, b_reduce=b_reduce)


def extend(values):
    fold_rows = values[:, NLAT - 3:, :][:, ::-1, ::-1]
    bottom_rows = jnp.zeros((values.shape[0], 3, values.shape[2]), values.dtype)
    extended = jnp.concatenate([bottom_rows, values, fold_rows], axis=1)
    return jnp.concatenate([extended[:, :, -3:], extended, extended[:, :, :3]], axis=2)

def depthwise(band_rows, kernel, conv_bias):
    band_rows = band_rows.astype(jnp.float32)
    height = band_rows.shape[1] - 6
    width = band_rows.shape[2] - 6
    summed = jnp.zeros((band_rows.shape[0], height, width), jnp.float32) + conv_bias[:, None, None]
    for shift_row in range(7):
        for shift_col in range(7):
            summed = summed + kernel[:, shift_row, shift_col, None, None] * band_rows[:, shift_row:shift_row + height, shift_col:shift_col + width]
    return summed

def finish(mixed_cells, old_values, ocean_flags, norm_gain, norm_bias, w_expand, b_expand, w_reduce, b_reduce):
    channels, height, width = mixed_cells.shape
    flat_cells = mixed_cells.reshape(channels, height * width)
    average = lax.optimization_barrier(jnp.mean(flat_cells, axis=0))
    centered = flat_cells - average
    variance = lax.optimization_barrier(jnp.mean(centered * centered, axis=0))
    normed = (centered / jnp.sqrt(variance + 1e-06) * norm_gain[:, None] + norm_bias[:, None]).astype(jnp.bfloat16)
    hidden = jnp.dot(w_expand, normed, preferred_element_type=jnp.float32) + b_expand[:, None]
    hidden = jax.nn.gelu(hidden, approximate=False).astype(jnp.bfloat16)
    update = jnp.dot(w_reduce, hidden, preferred_element_type=jnp.float32) + b_reduce[:, None]
    flags = ocean_flags.reshape(height * width).astype(jnp.float32)
    result_band = flags[None, :] * (old_values.reshape(channels, height * width).astype(jnp.float32) + update)
    return result_band.astype(jnp.bfloat16).reshape(channels, height, width)

def convnext_layer(values, land_mask, kernel, conv_bias, norm_gain, norm_bias, w_expand, b_expand, w_reduce, b_reduce):
    extended = extend(values)

    def band_step(band):
        start = band * 8
        band_rows = lax.dynamic_slice_in_dim(extended, start, 14, 1)
        mixed_cells = depthwise(band_rows, kernel, conv_bias)
        old_values = lax.dynamic_slice_in_dim(values, start, 8, 1)
        ocean_flags = lax.dynamic_slice_in_dim(land_mask, start, 8, 0)
        return finish(mixed_cells, old_values, ocean_flags, norm_gain, norm_bias, w_expand, b_expand, w_reduce, b_reduce)
    bands = lax.map(band_step, jnp.arange(NLAT // 8, dtype=jnp.int32))
    return bands.transpose(1, 0, 2, 3).reshape(values.shape)

def reference(field, land_mask, depth_kernel, depth_bias, norm_gain, norm_bias, w_expand, b_expand, w_reduce, b_reduce):
    values = field
    for layer_index in range(LAYERS):
        values = convnext_layer(values, land_mask, depth_kernel[layer_index], depth_bias[layer_index], norm_gain[layer_index], norm_bias[layer_index], w_expand[layer_index], b_expand[layer_index], w_reduce[layer_index], b_reduce[layer_index])
    return values
```

```python
import functools

import jax
import jax.numpy as jnp
from jax import lax
from jax.experimental import pallas as pl
from jax.experimental.pallas import tpu as pltpu
from jax.sharding import PartitionSpec as P


HALO = 6
VMEM_LIMIT = 20 * 1024 * 1024


def params():
    return pltpu.CompilerParams(vmem_limit_bytes=VMEM_LIMIT)


def cost(flops):
    return pl.CostEstimate(flops=int(flops), bytes_accessed=1 << 20, transcendentals=0)


def vmem(count):
    return [pl.BlockSpec(memory_space=pltpu.VMEM)] * count


def lanes(shape):
    return lax.broadcasted_iota(jnp.int32, shape, len(shape) - 1)


def first_step(out_ref):
    out_ref[...] = jnp.zeros_like(out_ref)


def pack_rows(upper_if_even, field_ref, mask_ref, after_ref, out_ref, wide, wide_mask):
    del after_ref
    channels, rows, width = field_ref.shape
    even = lax.rem(lax.axis_index("lat"), 2) == 0
    take_upper = even if upper_if_even else jnp.logical_not(even)
    wide[...] = field_ref[...].astype(jnp.float32).reshape(channels * rows, width)
    wide_mask[...] = mask_ref[...].astype(jnp.float32)
    for k in range(HALO):
        lower = wide[pl.ds(k, channels, stride=rows), :]
        upper = wide[pl.ds(rows - HALO + k, channels, stride=rows), :]
        at = pl.ds(k * channels, channels)
        out_ref[at, :] = jnp.where(take_upper, upper, lower).astype(jnp.bfloat16)
    pad = jnp.zeros((16 - HALO, width), jnp.float32)
    lower = jnp.concatenate([wide_mask[0:HALO, :], pad], axis=0)
    upper = jnp.concatenate([wide_mask[rows - HALO : rows, :], pad], axis=0)
    at = pl.ds(HALO * channels, 16)
    out_ref[at, :] = jnp.where(take_upper, upper, lower).astype(jnp.bfloat16)


def south_place(k):
    return k - 3 if k >= 3 else 8 + k


def channel_of(channels, group, slot):
    return slot // 4 * (channels // 4) + group * 4 + slot % 4


def join_rows(
    field_ref,
    mask_ref,
    first_ref,
    second_ref,
    after_ref,
    halo_ref,
    halo_mask_ref,
    core_ref,
    cross_ref,
    wide,
):
    del after_ref
    channels, rows, width = field_ref.shape
    lat = lax.axis_index("lat")
    even = lax.rem(lat, 2) == 0
    folded = lat == lax.axis_size("lat") - 1
    lon_even = lax.rem(lax.axis_index("lon"), 2) == 0
    wide[...] = jnp.zeros_like(wide)
    halo_mask_ref[...] = jnp.zeros_like(halo_mask_ref)
    sub = lax.broadcasted_iota(jnp.int32, (width, width), 0)
    target = lanes((width, width))
    turn = sub == jnp.where(folded, width - 1 - target, target)
    turn = turn.astype(jnp.float32).astype(jnp.bfloat16)

    def split(one, two):
        north = jnp.where(even, one, two)
        south = jnp.where(even, two, one)
        north = jnp.dot(north, turn, preferred_element_type=jnp.float32)
        return north, south.astype(jnp.float32)

    at = slice(HALO * channels, HALO * channels + 16)
    mask_north, mask_south = split(first_ref[at, :], second_ref[at, :])
    for k in range(HALO):
        at = slice(k * channels, (k + 1) * channels)
        north, south = split(first_ref[at, :], second_ref[at, :])
        beyond = jnp.where(folded, HALO - 1 - k, k)
        place = jnp.where(beyond < 3, 4 + beyond, 9 + beyond)
        wide[pl.ds(place, channels, stride=16), :] = north
        wide[pl.ds(south_place(k), channels, stride=16), :] = south
        halo_mask_ref[pl.ds(place, 1), :] = mask_north[k : k + 1, :]
        halo_mask_ref[south_place(k) : south_place(k) + 1, :] = mask_south[k : k + 1, :]
    halo_ref[...] = wide[...].astype(jnp.bfloat16).reshape(channels, 16, width)

    lane = lanes((32, width))
    slots = [(lane >= 8 * q) & (lane < 8 * q + HALO) for q in range(16)]

    def group(blocks):
        west = jnp.zeros((32, width), jnp.bfloat16)
        east = jnp.zeros((32, width), jnp.bfloat16)
        for q, block in enumerate(blocks):
            west = jnp.where(slots[q], pltpu.roll(block, 8 * q, 1), west)
            east = jnp.where(slots[q], pltpu.roll(block, (8 * q + HALO) % width, 1), east)
        return jnp.where(lon_even, east, west), jnp.where(lon_even, west, east)

    for g in range(channels // 16):
        blocks = []
        for q in range(16):
            c = channel_of(channels, g, q)
            blocks.append(jnp.concatenate([field_ref[c], halo_ref[c]], axis=0))
        core_ref[g * 32 : g * 32 + 32, :], cross_ref[g * 32 : g * 32 + 32, :] = group(blocks)
    mask_block = jnp.concatenate(
        [mask_ref[...].astype(jnp.float32), halo_mask_ref[...]], axis=0
    ).astype(jnp.bfloat16)
    core_ref[channels * 2 :, :], cross_ref[channels * 2 :, :] = group([mask_block])


def in_row(place, first_layer):
    none = jnp.full_like(place, 1000)
    row = jnp.where(place < 16, place, none)
    row = jnp.where((place >= 16) & (place < 19), place - 19, row)
    row = jnp.where((place >= 20) & (place < 23), place - 4, row)
    if first_layer:
        row = jnp.where((place >= 24) & (place < 27), place - 30, row)
        row = jnp.where((place >= 28) & (place < 31), place - 9, row)
    return row


EDGE = (-3, -2, -1, 16, 17, 18, 0, 1, 2, 13, 14, 15)
INNER = (3, 4, 5, 6, 7, 8, 9, 10, 11, 12)


def place_of(row):
    if row < 0:
        return row + 19
    return row if row < 16 else row + 4


def conv_matrices(table, out_ref, left, right, row, rows_out):
    channels, taps = table.shape
    count = len(rows_out)
    folded = lax.axis_index("lat") == lax.axis_size("lat") - 1
    k = lanes((1, 256))
    shift = k // 32
    place = k - shift * 32
    tap = lax.broadcasted_iota(jnp.int32, (taps, 256), 0)
    row = row(place)
    for i, here in enumerate(rows_out):
        if here is None:
            wanted = jnp.full_like(k, -1)
        else:
            a = row - here + 3
            inside = (a >= 0) & (a <= 6) & (shift < 7)
            wanted = a * 7 + shift
            if here > 15:
                wanted = jnp.where(folded, 48 - wanted, wanted)
            wanted = jnp.where(inside, wanted, -1)
            wanted = jnp.where((shift == 7) & (place < 3), 49 + place, wanted)
        picks = (tap == wanted).astype(jnp.float32).astype(jnp.bfloat16)
        matrix = jnp.dot(table, picks, preferred_element_type=jnp.float32)
        left[pl.ds(i, channels, stride=count), :] = matrix[:, :128]
        right[pl.ds(i, channels, stride=count), :] = matrix[:, 128:]
    size = channels * count
    out_ref[:, :128] = left[:size, :].astype(jnp.bfloat16)
    out_ref[:, 128:] = right[:size, :].astype(jnp.bfloat16)


def split_bias(bias):
    high = bias.astype(jnp.bfloat16).astype(jnp.float32)
    rest = bias - high
    mid = rest.astype(jnp.bfloat16).astype(jnp.float32)
    return high, mid, rest - mid


def weights(
    kernel_ref,
    bias_ref,
    gain_ref,
    norm_bias_ref,
    expand_ref,
    expand_bias_ref,
    reduce_bias_ref,
    one_ref,
    two_ref,
    rows_ref,
    expand_out_ref,
    left,
    right,
    turn,
    tall,
):
    taps, layers, channels = kernel_ref.shape
    hidden = expand_ref.shape[2]
    turn[...] = jnp.zeros_like(turn)
    tall[...] = jnp.zeros_like(tall)
    for layer in range(layers):
        for tap in range(taps):
            turn[tap : tap + 1, :channels] = kernel_ref[tap, layer : layer + 1, :]
        parts = split_bias(bias_ref[layer : layer + 1, :])
        for n, part in enumerate(parts):
            turn[taps + n : taps + n + 1, :channels] = part
        table = turn[...].T[:channels, :64].astype(jnp.bfloat16)
        if layer == 0:
            every = EDGE + INNER + (None,) * 2
            row = functools.partial(in_row, first_layer=True)
            conv_matrices(table, one_ref, left, right, row, every)
        else:
            row = functools.partial(in_row, first_layer=False)
            conv_matrices(table, two_ref, left, right, row, tuple(range(16)))
    for layer in range(layers):
        for n, ref in enumerate((gain_ref, norm_bias_ref, reduce_bias_ref)):
            turn[:, :channels] = jnp.broadcast_to(ref[layer : layer + 1, :], (128, channels))
            rows_ref[layer, n] = turn[...].T[:channels, :]
        tall[:channels, :] = expand_ref[layer].astype(jnp.float32) * 0.5
        parts = split_bias(expand_bias_ref[layer : layer + 1, :] * 0.5)
        for n, part in enumerate(parts):
            tall[channels + n : channels + n + 1, :] = part
        for n in range(hidden // 128):
            piece = tall[:, n * 128 : (n + 1) * 128].T
            at = pl.ds(n * 128, 128)
            expand_out_ref[layer, at, :] = piece[:, : channels + 16].astype(jnp.bfloat16)


ERF = (7.97869712e-01, 3.63922860e-02, -8.78263977e-05, -3.66934787e-05, 1.42500782e-06)


def gelu_of_double(half):
    square = half * half
    total = jnp.full_like(half, 2.0 * 4.0 ** (len(ERF) - 1) * ERF[-1])
    for power in range(len(ERF) - 2, -1, -1):
        total = total * square + jnp.full_like(half, 2.0 * 4.0**power * ERF[power])
    return half * jnp.tanh(half * total) + half


def norm(rows_ref, layer, cells):
    average = jnp.mean(cells, axis=0, keepdims=True)
    centered = cells - average
    variance = jnp.mean(centered * centered, axis=0, keepdims=True)
    scaled = centered * lax.rsqrt(variance + 1e-06)
    return (scaled * rows_ref[layer, 0] + rows_ref[layer, 1]).astype(jnp.bfloat16)


def mlp(rows_ref, expand_ref, reduce_ref, layer, blocks, normed_ref, inner_ref, put):
    count = len(blocks)
    channels, width = rows_ref.shape[2:]
    hidden = inner_ref.shape[0]
    wide = count * width
    normed_ref[channels:, :wide] = jnp.ones((16, wide), jnp.bfloat16)
    for n, block in enumerate(blocks):
        at = slice(n * width, (n + 1) * width)
        normed_ref[:channels, at] = norm(rows_ref, layer, block())
    tiles = [slice(n, min(n + 2 * width, wide)) for n in range(0, wide, 2 * width)]
    for at in tiles:
        normed = normed_ref[:, at]
        for part in range(0, hidden, 128):
            matrix = expand_ref[layer, part : part + 128, :]
            half = jnp.dot(matrix, normed, preferred_element_type=jnp.float32)
            for k in range(0, 128, 16):
                values = gelu_of_double(half[k : k + 16, :].astype(jnp.bfloat16))
                inner_ref[part + k : part + k + 16, at] = values
    extra = rows_ref[layer, 2]
    for t, at in enumerate(tiles):
        change = jnp.dot(reduce_ref[layer], inner_ref[:, at], preferred_element_type=jnp.float32)
        for n in range((at.stop - at.start) // width):
            put(t * 2 + n, change[:, n * width : (n + 1) * width] + extra)


def columns_stack(block, ones):
    width = block.shape[1]
    stack = [block if s == 0 else pltpu.roll(block, (-s) % width, 1) for s in range(-3, 4)]
    return jnp.concatenate(stack + [ones], axis=0)


def conv_rows(matrix_ref, stack_of, conv, channels, stride, first, count):
    ones = jnp.ones((matrix_ref.shape[1] // 8, 128), jnp.bfloat16)

    def step(c, carry):
        matrix = matrix_ref[pl.ds(pl.multiple_of(c * stride + first, 8), count), :]
        result = jnp.dot(matrix, stack_of(c, ones), preferred_element_type=jnp.float32)
        conv[pl.ds(c, count, stride=channels), :] = result
        return carry

    lax.fori_loop(0, channels, step, 0, unroll=channels)


def conv_row(conv, channels, i):
    return lambda: conv[i * channels : (i + 1) * channels, :]


def inner_rows(
    field_ref, matrix_ref, rows_ref, expand_ref, reduce_ref, update_ref, conv, normed, inner
):
    channels, rows, width = field_ref.shape
    none = jnp.zeros((16, width), jnp.bfloat16)

    def stack_of(c, ones):
        return columns_stack(jnp.concatenate([field_ref[c], none], axis=0), ones)

    conv_rows(matrix_ref, stack_of, conv, channels, 24, 8, 16)

    def put(n, change):
        update_ref[pl.ds(INNER[n], channels, stride=24), :] = change

    blocks = [conv_row(conv, channels, i + len(EDGE) - 8) for i in range(len(INNER))]
    mlp(rows_ref, expand_ref, reduce_ref, 0, blocks, normed, inner, put)


def edge_rows(
    field_ref,
    halo_ref,
    matrix_ref,
    rows_ref,
    expand_ref,
    reduce_ref,
    old_ref,
    update_ref,
    conv,
    normed,
    inner,
):
    del old_ref
    channels, _, width = field_ref.shape

    def stack_of(c, ones):
        return columns_stack(jnp.concatenate([field_ref[c], halo_ref[c]], axis=0), ones)

    conv_rows(matrix_ref, stack_of, conv, channels, 24, 0, 16)
    for empty in (19, 23):
        update_ref[pl.ds(empty, channels, stride=24), :] = jnp.zeros((channels, width), jnp.float32)

    def put(n, change):
        update_ref[pl.ds(place_of(EDGE[n]), channels, stride=24), :] = change

    blocks = [conv_row(conv, channels, i) for i in range(len(EDGE))]
    mlp(rows_ref, expand_ref, reduce_ref, 0, blocks, normed, inner, put)


def by_side(core, cross):
    lon_even = lax.rem(lax.axis_index("lon"), 2) == 0
    return jnp.where(lon_even, core, cross), jnp.where(lon_even, cross, core)


def edge_columns(
    core_ref,
    cross_ref,
    core_sent_ref,
    cross_sent_ref,
    matrix_ref,
    rows_ref,
    expand_ref,
    reduce_ref,
    strips,
    conv,
    normed,
    inner,
):
    channels, width = rows_ref.shape[2:]
    quarter = channels // 4
    groups = channels // 16
    lane32 = lanes((32, width))
    within = lane32 % 32
    in_west, in_own_west, in_own_east = within < 6, within < 12, within < 18
    ones = jnp.ones((32, width), jnp.bfloat16)
    for g in range(groups):
        at = slice(g * 32, g * 32 + 32)
        east, west = by_side(core_ref[at, :], cross_ref[at, :])
        own_east, own_west = by_side(core_sent_ref[at, :], cross_sent_ref[at, :])
        for t in range(4):
            parts = [
                pltpu.roll(part, (6 * n - 8 * t) % width, 1)
                for n, part in enumerate((west, own_west, own_east, east))
            ]
            block = jnp.where(in_own_east, parts[2], parts[3])
            block = jnp.where(in_own_west, parts[1], block)
            block = jnp.where(in_west, parts[0], block)
            some = [channel_of(channels, g, 4 * n + t) for n in range(4)]
            matrix = jnp.concatenate(
                [matrix_ref[c * 24 : c * 24 + 24, :] for c in some], axis=0
            )
            stack = columns_stack(block, ones)
            result = jnp.dot(matrix, stack, preferred_element_type=jnp.float32)
            for n, c in enumerate(some):
                conv[pl.ds(c, 24, stride=channels), :] = result[n * 24 : n * 24 + 24, :]

    order = {place_of(row): i for i, row in enumerate(EDGE + INNER)}
    slot = lanes((quarter, width)) // 8
    packs = []
    for p in range(3):
        parts = []
        for n in range(4):
            packed = jnp.zeros((quarter, width), jnp.float32)
            for q in range(8):
                if p * 8 + q in order:
                    start = order[p * 8 + q] * channels + n * quarter
                    block = conv[start : start + quarter, :]
                    near = pltpu.roll(block, (53 - 8 * q - 32 * n) % width, 1)
                    far = pltpu.roll(block, (105 - 8 * q - 32 * n) % width, 1)
                    packed = jnp.where(slot == 7 - q, near, packed)
                    packed = jnp.where(slot == 15 - q, far, packed)
            parts.append(packed)
        packs.append(jnp.concatenate(parts, axis=0))

    def put(p, change):
        for q in range(8):
            near = pltpu.roll(change, (69 + 8 * q) % width, 1)
            strips[pl.ds(p * 8 + q, channels, stride=24), :] = near

    blocks = [functools.partial(lambda block: block, packed) for packed in packs]
    mlp(rows_ref, expand_ref, reduce_ref, 0, blocks, normed, inner, put)


def second_layer(
    field_ref,
    mask_ref,
    halo_ref,
    halo_mask_ref,
    core_ref,
    cross_ref,
    strips,
    update_ref,
    matrix_ref,
    rows_ref,
    expand_ref,
    reduce_ref,
    out_ref,
    main_ref,
    conv,
    normed,
    inner,
):
    channels, rows, width = out_ref.shape
    half = width // 2
    groups = channels // 16
    lane32 = lanes((32, width))
    lane24 = lanes((24, width))
    to_east = lane32 < half

    def beside_of(east, west, q):
        east = pltpu.roll(east, (width - 8 * q) % width, 1)
        west = pltpu.roll(west, width - HALO - 8 * q, 1)
        return jnp.where(to_east, east, west).astype(jnp.float32)[0:24, :]

    def received(g):
        at = slice(g * 32, g * 32 + 32)
        return by_side(core_ref[at, :], cross_ref[at, :])

    main_mask = jnp.concatenate(
        [mask_ref[...].astype(jnp.float32), halo_mask_ref[0:8, :]], axis=0
    )
    side_mask = beside_of(*received(groups), 0)
    low = lane24 < 3
    high = lane24 >= width - 3
    blank = jnp.zeros((8, width), jnp.float32)
    ones = jnp.ones((32, width), jnp.bfloat16)
    away = {s: lane32 < s if s > 0 else lane32 >= width + s for s in range(-3, 4) if s}
    for g in range(groups):
        east, west = received(g)
        for q in range(16):
            c = channel_of(channels, g, q)
            near = strips[c * 24 : c * 24 + 24, :]
            far = pltpu.roll(near, half, 1)
            change = update_ref[c * 24 : c * 24 + 24, :]
            change = jnp.where(low, near, jnp.where(high, far, change))
            old = jnp.concatenate([field_ref[c], halo_ref[c]], axis=0).astype(jnp.float32)
            main = main_mask * (old[:24, :] + change)
            main = jnp.concatenate([main, blank], axis=0).astype(jnp.bfloat16)
            main_ref[c] = main[:rows, :]
            change = jnp.where(high, near, far)
            beside = side_mask * (beside_of(east, west, q) + change)
            beside = jnp.concatenate([beside, blank], axis=0).astype(jnp.bfloat16)
            stack = []
            for s in range(-3, 4):
                moved = main
                if s:
                    moved = pltpu.roll(jnp.where(away[s], beside, main), (-s) % width, 1)
                stack.append(moved)
            stack = jnp.concatenate(stack + [ones], axis=0)
            matrix = matrix_ref[c * 16 : c * 16 + 16, :]
            result = jnp.dot(matrix, stack, preferred_element_type=jnp.float32)
            conv[pl.ds(c, 16, stride=channels), :] = result

    mask = mask_ref[...].astype(jnp.float32)
    changes = []

    def put(n, change):
        changes.append(change)
        if n < rows - 1:
            return
        for c in range(0, channels, 8):
            parts = []
            for half in range(0, rows, 8):
                part = [changes[i][c : c + 8, :] for i in range(half, half + 8)]
                parts.append(jnp.swapaxes(jnp.stack(part, axis=0), 0, 1))
            change = jnp.concatenate(parts, axis=1)
            old = main_ref[c : c + 8].astype(jnp.float32)
            out_ref[c : c + 8] = (mask[None] * (old + change)).astype(jnp.bfloat16)

    blocks = [conv_row(conv, channels, i) for i in range(rows)]
    mlp(rows_ref, expand_ref, reduce_ref, 1, blocks, normed, inner, put)


def per_device(
    nlat,
    nlon,
    field,
    land_mask,
    depth_kernel,
    depth_bias,
    norm_gain,
    norm_bias,
    w_expand,
    b_expand,
    w_reduce,
    b_reduce,
):
    channels, rows, width = field.shape
    layers, hidden = b_expand.shape
    bf16, f32 = jnp.bfloat16, jnp.float32
    edge = HALO * channels + 16

    def buffers(count):
        return [
            pltpu.VMEM((channels + 16, count * width), bf16),
            pltpu.VMEM((hidden, count * width), bf16),
        ]

    def pack(upper_if_even, after):
        return pl.pallas_call(
            functools.partial(pack_rows, upper_if_even),
            out_shape=jax.ShapeDtypeStruct((edge, width), bf16),
            in_specs=vmem(2) + [pl.BlockSpec(memory_space=pl.ANY)],
            out_specs=pl.BlockSpec(memory_space=pltpu.VMEM),
            scratch_shapes=[
                pltpu.VMEM((channels * rows, width), f32),
                pltpu.VMEM((rows, width), f32),
            ],
            compiler_params=params(),
            cost_estimate=cost(4e9),
        )(field, land_mask, after)

    begun = pl.pallas_call(
        first_step,
        out_shape=jax.ShapeDtypeStruct((8, 128), f32),
        out_specs=pl.BlockSpec(memory_space=pltpu.VMEM),
        compiler_params=params(),
        cost_estimate=cost(4e9),
    )()
    first = pack(True, begun)
    second = pack(False, first)

    pairs = []
    for d in range(nlon):
        at = d * nlat
        for low in range(1, nlat - 1, 2):
            pairs += [(at + low, at + low + 1), (at + low + 1, at + low)]
        pairs.append((at + nlat - 1, (nlon - 1 - d) * nlat + nlat - 1))
    second = lax.ppermute(second, ("lon", "lat"), pairs)
    pairs = []
    for low in range(0, nlat - 1, 2):
        pairs += [(low, low + 1), (low + 1, low)]
    first = lax.ppermute(first, "lat", pairs)

    kernel = depth_kernel.transpose(2, 3, 0, 1).reshape(49, layers, channels)
    matrix_one, matrix_two, by_channel, expand = pl.pallas_call(
        weights,
        out_shape=[
            jax.ShapeDtypeStruct((channels * 24, 256), bf16),
            jax.ShapeDtypeStruct((channels * 16, 256), bf16),
            jax.ShapeDtypeStruct((layers, 3, channels, 128), f32),
            jax.ShapeDtypeStruct((layers, hidden, channels + 16), bf16),
        ],
        in_specs=vmem(7),
        out_specs=vmem(4),
        scratch_shapes=[
            pltpu.VMEM((channels * 24, 128), f32),
            pltpu.VMEM((channels * 24, 128), f32),
            pltpu.VMEM((128, 128), f32),
            pltpu.VMEM((128, hidden), f32),
        ],
        compiler_params=params(),
        cost_estimate=cost(2e9),
    )(
        kernel,
        depth_bias,
        norm_gain,
        norm_bias,
        w_expand.transpose(0, 2, 1),
        b_expand,
        b_reduce,
    )
    update = pl.pallas_call(
        inner_rows,
        out_shape=jax.ShapeDtypeStruct((channels * 24, width), f32),
        in_specs=vmem(5),
        out_specs=pl.BlockSpec(memory_space=pltpu.VMEM),
        scratch_shapes=[pltpu.VMEM((channels * 16, width), f32)] + buffers(len(INNER)),
        compiler_params=params(),
        cost_estimate=cost(4e9),
    )(field, matrix_one, by_channel, expand, w_reduce)

    strip_rows = (channels // 16 + 1) * 32
    halo, halo_mask, core, cross = pl.pallas_call(
        join_rows,
        out_shape=[
            jax.ShapeDtypeStruct((channels, 16, width), bf16),
            jax.ShapeDtypeStruct((16, width), f32),
            jax.ShapeDtypeStruct((strip_rows, width), bf16),
            jax.ShapeDtypeStruct((strip_rows, width), bf16),
        ],
        in_specs=vmem(4) + [pl.BlockSpec(memory_space=pl.ANY)],
        out_specs=vmem(4),
        scratch_shapes=[pltpu.VMEM((channels * 16, width), f32)],
        compiler_params=params(),
    )(field, land_mask, first, second, update)

    pairs = []
    for low in range(0, nlon, 2):
        pairs += [(low, low + 1), (low + 1, low)]
    core_sent, cross_sent = core, cross
    core = lax.ppermute(core, "lon", pairs)
    pairs = []
    for low in range(1, nlon, 2):
        after = (low + 1) % nlon
        pairs += [(low, after), (after, low)]
    cross = lax.ppermute(cross, "lon", pairs)

    update = pl.pallas_call(
        edge_rows,
        out_shape=jax.ShapeDtypeStruct((channels * 24, width), f32),
        in_specs=vmem(7),
        out_specs=pl.BlockSpec(memory_space=pltpu.VMEM),
        scratch_shapes=[pltpu.VMEM((channels * 16, width), f32)] + buffers(len(EDGE)),
        input_output_aliases={6: 0},
        compiler_params=params(),
        cost_estimate=cost(4e9),
    )(field, halo, matrix_one, by_channel, expand, w_reduce, update)

    strips = pl.pallas_call(
        edge_columns,
        out_shape=jax.ShapeDtypeStruct((channels * 24, width), f32),
        in_specs=vmem(8),
        out_specs=pl.BlockSpec(memory_space=pltpu.VMEM),
        scratch_shapes=[pltpu.VMEM((channels * 24, width), f32)] + buffers(3),
        compiler_params=params(),
    )(core, cross, core_sent, cross_sent, matrix_one, by_channel, expand, w_reduce)

    return pl.pallas_call(
        second_layer,
        out_shape=jax.ShapeDtypeStruct((channels, rows, width), bf16),
        in_specs=vmem(12),
        out_specs=pl.BlockSpec(memory_space=pltpu.VMEM),
        scratch_shapes=[
            pltpu.VMEM((channels, rows, width), bf16),
            pltpu.VMEM((channels * 16, width), f32),
        ]
        + buffers(rows),
        compiler_params=params(),
    )(
        field,
        land_mask,
        halo,
        halo_mask,
        core,
        cross,
        strips,
        update,
        matrix_two,
        by_channel,
        expand,
        w_reduce,
    )


def solution(mesh):
    placed = (P(None, "lat", "lon"), P("lat", "lon"), P(), P(), P(), P(), P(), P(), P(), P())
    return jax.shard_map(
        functools.partial(per_device, mesh.shape["lat"], mesh.shape["lon"]),
        mesh=mesh,
        in_specs=placed,
        out_specs=P(None, "lat", "lon"),
        check_vma=False,
    )
```

```python
import functools

import jax
import jax.numpy as jnp
from jax import lax
from jax.experimental import pallas as pl
from jax.experimental.pallas import tpu as pltpu
from jax.sharding import PartitionSpec as P


HALO = 6
VMEM_LIMIT = 20 * 1024 * 1024


def params():
    return pltpu.CompilerParams(vmem_limit_bytes=VMEM_LIMIT)


def cost(flops):
    return pl.CostEstimate(flops=int(flops), bytes_accessed=1 << 20, transcendentals=0)


def vmem(count):
    return [pl.BlockSpec(memory_space=pltpu.VMEM)] * count


def lanes(shape):
    return lax.broadcasted_iota(jnp.int32, shape, len(shape) - 1)


def first_step(out_ref):
    out_ref[...] = jnp.zeros_like(out_ref)


def pack_rows(upper_if_even, field_ref, mask_ref, after_ref, out_ref, wide, wide_mask):
    del after_ref
    channels, rows, width = field_ref.shape
    even = lax.rem(lax.axis_index("lat"), 2) == 0
    take_upper = even if upper_if_even else jnp.logical_not(even)
    wide[...] = field_ref[...].astype(jnp.float32).reshape(channels * rows, width)
    wide_mask[...] = mask_ref[...].astype(jnp.float32)
    for k in range(HALO):
        lower = wide[pl.ds(k, channels, stride=rows), :]
        upper = wide[pl.ds(rows - HALO + k, channels, stride=rows), :]
        at = pl.ds(k * channels, channels)
        out_ref[at, :] = jnp.where(take_upper, upper, lower).astype(jnp.bfloat16)
    pad = jnp.zeros((16 - HALO, width), jnp.float32)
    lower = jnp.concatenate([wide_mask[0:HALO, :], pad], axis=0)
    upper = jnp.concatenate([wide_mask[rows - HALO : rows, :], pad], axis=0)
    at = pl.ds(HALO * channels, 16)
    out_ref[at, :] = jnp.where(take_upper, upper, lower).astype(jnp.bfloat16)


def south_place(k):
    return k - 3 if k >= 3 else 8 + k


def channel_of(channels, group, slot):
    return slot // 2 * (channels // 4) + group * 2 + slot % 2


def join_rows(
    field_ref,
    mask_ref,
    first_ref,
    second_ref,
    after_ref,
    halo_ref,
    halo_mask_ref,
    ends_ref,
    wide,
):
    del after_ref
    channels, rows, width = field_ref.shape
    lat = lax.axis_index("lat")
    even = lax.rem(lat, 2) == 0
    folded = lat == lax.axis_size("lat") - 1
    wide[...] = jnp.zeros_like(wide)
    halo_mask_ref[...] = jnp.zeros_like(halo_mask_ref)
    sub = lax.broadcasted_iota(jnp.int32, (width, width), 0)
    target = lanes((width, width))
    turn = sub == jnp.where(folded, width - 1 - target, target)
    turn = turn.astype(jnp.float32).astype(jnp.bfloat16)

    def split(one, two):
        north = jnp.where(even, one, two)
        south = jnp.where(even, two, one)
        north = jnp.dot(north, turn, preferred_element_type=jnp.float32)
        return north, south.astype(jnp.float32)

    at = slice(HALO * channels, HALO * channels + 16)
    mask_north, mask_south = split(first_ref[at, :], second_ref[at, :])
    for k in range(HALO):
        at = slice(k * channels, (k + 1) * channels)
        north, south = split(first_ref[at, :], second_ref[at, :])
        beyond = jnp.where(folded, HALO - 1 - k, k)
        place = jnp.where(beyond < 3, 4 + beyond, 9 + beyond)
        wide[pl.ds(place, channels, stride=16), :] = north
        wide[pl.ds(south_place(k), channels, stride=16), :] = south
        halo_mask_ref[pl.ds(place, 1), :] = mask_north[k : k + 1, :]
        halo_mask_ref[south_place(k) : south_place(k) + 1, :] = mask_south[k : k + 1, :]
    halo_ref[...] = wide[...].astype(jnp.bfloat16).reshape(channels, 16, width)

    slot = lanes((32, width)) // 16

    def ends(blocks):
        packed = jnp.zeros((32, width), jnp.bfloat16)
        for j, block in enumerate(blocks):
            packed = jnp.where(slot == j, pltpu.roll(block, 16 * j + HALO, 1), packed)
        return packed

    groups = channels // 8
    for g in range(groups):
        some = [channel_of(channels, g, j) for j in range(8)]
        blocks = [jnp.concatenate([field_ref[c], halo_ref[c]], axis=0) for c in some]
        ends_ref[g * 32 : g * 32 + 32, :] = ends(blocks)
    mask_block = jnp.concatenate(
        [mask_ref[...].astype(jnp.float32), halo_mask_ref[...]], axis=0
    ).astype(jnp.bfloat16)
    ends_ref[groups * 32 :, :] = ends([mask_block])


def in_row(place, first_layer):
    none = jnp.full_like(place, 1000)
    row = jnp.where(place < 16, place, none)
    row = jnp.where((place >= 16) & (place < 19), place - 19, row)
    row = jnp.where((place >= 20) & (place < 23), place - 4, row)
    if first_layer:
        row = jnp.where((place >= 24) & (place < 27), place - 30, row)
        row = jnp.where((place >= 28) & (place < 31), place - 9, row)
    return row


EDGE = (-3, -2, -1, 16, 17, 18, 0, 1, 2, 13, 14, 15)
INNER = (3, 4, 5, 6, 7, 8, 9, 10, 11, 12)


def place_of(row):
    if row < 0:
        return row + 19
    return row if row < 16 else row + 4


def conv_matrices(table, out_ref, left, right, row, rows_out):
    channels, taps = table.shape
    count = len(rows_out)
    folded = lax.axis_index("lat") == lax.axis_size("lat") - 1
    k = lanes((1, 256))
    shift = k // 32
    place = k - shift * 32
    tap = lax.broadcasted_iota(jnp.int32, (taps, 256), 0)
    row = row(place)
    for i, here in enumerate(rows_out):
        if here is None:
            wanted = jnp.full_like(k, -1)
        else:
            a = row - here + 3
            inside = (a >= 0) & (a <= 6) & (shift < 7)
            wanted = a * 7 + shift
            if here > 15:
                wanted = jnp.where(folded, 48 - wanted, wanted)
            wanted = jnp.where(inside, wanted, -1)
            wanted = jnp.where((shift == 7) & (place < 3), 49 + place, wanted)
        picks = (tap == wanted).astype(jnp.float32).astype(jnp.bfloat16)
        matrix = jnp.dot(table, picks, preferred_element_type=jnp.float32)
        left[pl.ds(i, channels, stride=count), :] = matrix[:, :128]
        right[pl.ds(i, channels, stride=count), :] = matrix[:, 128:]
    size = channels * count
    out_ref[:, :128] = left[:size, :].astype(jnp.bfloat16)
    out_ref[:, 128:] = right[:size, :].astype(jnp.bfloat16)


def split_bias(bias):
    high = bias.astype(jnp.bfloat16).astype(jnp.float32)
    rest = bias - high
    mid = rest.astype(jnp.bfloat16).astype(jnp.float32)
    return high, mid, rest - mid


def weights(
    kernel_ref,
    bias_ref,
    gain_ref,
    norm_bias_ref,
    expand_ref,
    expand_bias_ref,
    reduce_bias_ref,
    one_ref,
    two_ref,
    rows_ref,
    expand_out_ref,
    left,
    right,
    turn,
    tall,
):
    taps, layers, channels = kernel_ref.shape
    hidden = expand_ref.shape[2]
    turn[...] = jnp.zeros_like(turn)
    tall[...] = jnp.zeros_like(tall)
    for layer in range(layers):
        for tap in range(taps):
            turn[tap : tap + 1, :channels] = kernel_ref[tap, layer : layer + 1, :]
        parts = split_bias(bias_ref[layer : layer + 1, :])
        for n, part in enumerate(parts):
            turn[taps + n : taps + n + 1, :channels] = part
        table = turn[...].T[:channels, :64].astype(jnp.bfloat16)
        if layer == 0:
            every = EDGE + INNER + (None,) * 2
            row = functools.partial(in_row, first_layer=True)
            conv_matrices(table, one_ref, left, right, row, every)
        else:
            row = functools.partial(in_row, first_layer=False)
            conv_matrices(table, two_ref, left, right, row, tuple(range(16)))
    for layer in range(layers):
        for n, ref in enumerate((gain_ref, norm_bias_ref, reduce_bias_ref)):
            turn[:, :channels] = jnp.broadcast_to(ref[layer : layer + 1, :], (128, channels))
            rows_ref[layer, n] = turn[...].T[:channels, :]
        tall[:channels, :] = expand_ref[layer].astype(jnp.float32) * 0.5
        parts = split_bias(expand_bias_ref[layer : layer + 1, :] * 0.5)
        for n, part in enumerate(parts):
            tall[channels + n : channels + n + 1, :] = part
        for n in range(hidden // 128):
            piece = tall[:, n * 128 : (n + 1) * 128].T
            at = pl.ds(n * 128, 128)
            expand_out_ref[layer, at, :] = piece[:, : channels + 16].astype(jnp.bfloat16)


ERF = (7.97869712e-01, 3.63922860e-02, -8.78263977e-05, -3.66934787e-05, 1.42500782e-06)


def gelu_of_double(half):
    square = half * half
    total = jnp.full_like(half, 2.0 * 4.0 ** (len(ERF) - 1) * ERF[-1])
    for power in range(len(ERF) - 2, -1, -1):
        total = total * square + jnp.full_like(half, 2.0 * 4.0**power * ERF[power])
    return half * jnp.tanh(half * total) + half


def norm(rows_ref, layer, cells):
    average = jnp.mean(cells, axis=0, keepdims=True)
    centered = cells - average
    variance = jnp.mean(centered * centered, axis=0, keepdims=True)
    scaled = centered * lax.rsqrt(variance + 1e-06)
    return (scaled * rows_ref[layer, 0] + rows_ref[layer, 1]).astype(jnp.bfloat16)


def mlp(rows_ref, expand_ref, reduce_ref, layer, blocks, normed_ref, inner_ref, put):
    count = len(blocks)
    channels, width = rows_ref.shape[2:]
    hidden = inner_ref.shape[0]
    wide = count * width
    normed_ref[channels:, :wide] = jnp.ones((16, wide), jnp.bfloat16)
    for n, block in enumerate(blocks):
        at = slice(n * width, (n + 1) * width)
        normed_ref[:channels, at] = norm(rows_ref, layer, block())
    tiles = [slice(n, min(n + 2 * width, wide)) for n in range(0, wide, 2 * width)]
    for at in tiles:
        normed = normed_ref[:, at]
        for part in range(0, hidden, 128):
            matrix = expand_ref[layer, part : part + 128, :]
            half = jnp.dot(matrix, normed, preferred_element_type=jnp.float32)
            for k in range(0, 128, 16):
                values = gelu_of_double(half[k : k + 16, :].astype(jnp.bfloat16))
                inner_ref[part + k : part + k + 16, at] = values
    extra = rows_ref[layer, 2]
    for t, at in enumerate(tiles):
        change = jnp.dot(reduce_ref[layer], inner_ref[:, at], preferred_element_type=jnp.float32)
        for n in range((at.stop - at.start) // width):
            put(t * 2 + n, change[:, n * width : (n + 1) * width] + extra)


def columns_stack(block, ones):
    width = block.shape[1]
    stack = [block if s == 0 else pltpu.roll(block, (-s) % width, 1) for s in range(-3, 4)]
    return jnp.concatenate(stack + [ones], axis=0)


def conv_rows(matrix_ref, stack_of, conv, channels, stride, first, count):
    ones = jnp.ones((matrix_ref.shape[1] // 8, 128), jnp.bfloat16)

    def step(c, carry):
        matrix = matrix_ref[pl.ds(pl.multiple_of(c * stride + first, 8), count), :]
        result = jnp.dot(matrix, stack_of(c, ones), preferred_element_type=jnp.float32)
        conv[pl.ds(c, count, stride=channels), :] = result
        return carry

    lax.fori_loop(0, channels, step, 0, unroll=channels)


def conv_row(conv, channels, i):
    return lambda: conv[i * channels : (i + 1) * channels, :]


def inner_rows(
    field_ref, matrix_ref, rows_ref, expand_ref, reduce_ref, update_ref, conv, normed, inner
):
    channels, rows, width = field_ref.shape
    none = jnp.zeros((16, width), jnp.bfloat16)

    def stack_of(c, ones):
        return columns_stack(jnp.concatenate([field_ref[c], none], axis=0), ones)

    conv_rows(matrix_ref, stack_of, conv, channels, 24, 8, 16)

    def put(n, change):
        update_ref[pl.ds(INNER[n], channels, stride=24), :] = change

    blocks = [conv_row(conv, channels, i + len(EDGE) - 8) for i in range(len(INNER))]
    mlp(rows_ref, expand_ref, reduce_ref, 0, blocks, normed, inner, put)


def edge_rows(
    field_ref,
    halo_ref,
    matrix_ref,
    rows_ref,
    expand_ref,
    reduce_ref,
    old_ref,
    update_ref,
    conv,
    normed,
    inner,
):
    del old_ref
    channels, _, width = field_ref.shape

    def stack_of(c, ones):
        return columns_stack(jnp.concatenate([field_ref[c], halo_ref[c]], axis=0), ones)

    conv_rows(matrix_ref, stack_of, conv, channels, 24, 0, 16)
    for empty in (19, 23):
        update_ref[pl.ds(empty, channels, stride=24), :] = jnp.zeros((channels, width), jnp.float32)

    def put(n, change):
        update_ref[pl.ds(place_of(EDGE[n]), channels, stride=24), :] = change

    blocks = [conv_row(conv, channels, i) for i in range(len(EDGE))]
    mlp(rows_ref, expand_ref, reduce_ref, 0, blocks, normed, inner, put)


def by_side(core, cross):
    lon_even = lax.rem(lax.axis_index("lon"), 2) == 0
    return jnp.where(lon_even, core, cross), jnp.where(lon_even, cross, core)


def edge_columns(
    core_ref,
    cross_ref,
    ends_ref,
    matrix_ref,
    rows_ref,
    expand_ref,
    reduce_ref,
    strips,
    conv,
    normed,
    inner,
):
    channels, width = rows_ref.shape[2:]
    quarter = channels // 4
    groups = channels // 8
    lane32 = lanes((32, width))
    first_six = lane32 % 16 < HALO
    first_twelve = lane32 % 32 < 2 * HALO
    ones = jnp.ones((32, width), jnp.bfloat16)
    for g in range(groups):
        at = slice(g * 32, g * 32 + 32)
        east, west = by_side(core_ref[at, :], cross_ref[at, :])
        own = ends_ref[at, :]
        at_west = jnp.where(first_six, west, own)
        at_east = jnp.where(first_six, own, east)
        for t in range(2):
            left = pltpu.roll(at_west, width - 16, 1) if t else at_west
            right = pltpu.roll(at_east, (2 * HALO - 16 * t) % width, 1)
            block = jnp.where(first_twelve, left, right)
            some = [channel_of(channels, g, 2 * n + t) for n in range(4)]
            matrix = jnp.concatenate(
                [matrix_ref[c * 24 : c * 24 + 24, :] for c in some], axis=0
            )
            stack = columns_stack(block, ones)
            result = jnp.dot(matrix, stack, preferred_element_type=jnp.float32)
            for n, c in enumerate(some):
                conv[pl.ds(c, 24, stride=channels), :] = result[n * 24 : n * 24 + 24, :]

    order = {place_of(row): i for i, row in enumerate(EDGE + INNER)}
    lane = lanes((quarter, width))
    starts = [32 * (q // 2) + 6 * (q % 2) for q in range(8)]
    inside = [
        ((lane >= s + 3) & (lane < s + 9)) | ((lane >= s + 15) & (lane < s + 21)) for s in starts
    ]
    packs = []
    for p in range(3):
        parts = []
        for n in range(4):
            packed = jnp.zeros((quarter, width), jnp.float32)
            for q, start in enumerate(starts):
                if p * 8 + q in order:
                    row = order[p * 8 + q] * channels + n * quarter
                    block = conv[row : row + quarter, :]
                    block = pltpu.roll(block, (start - 32 * n) % width, 1)
                    packed = jnp.where(inside[q], block, packed)
            parts.append(packed)
        packs.append(jnp.concatenate(parts, axis=0))

    def put(p, change):
        for q, start in enumerate(starts):
            near = pltpu.roll(change, (width - 6 - start) % width, 1)
            strips[pl.ds(p * 8 + q, channels, stride=24), :] = near

    blocks = [functools.partial(lambda block: block, packed) for packed in packs]
    mlp(rows_ref, expand_ref, reduce_ref, 0, blocks, normed, inner, put)


def second_layer(
    field_ref,
    mask_ref,
    halo_ref,
    halo_mask_ref,
    core_ref,
    cross_ref,
    strips,
    update_ref,
    matrix_ref,
    rows_ref,
    expand_ref,
    reduce_ref,
    out_ref,
    main_ref,
    conv,
    normed,
    inner,
):
    channels, rows, width = out_ref.shape
    groups = channels // 8
    lane32 = lanes((32, width))
    lane24 = lanes((24, width))
    first_six = lane32 % 16 < HALO

    def beside_of(received, slot):
        beside = pltpu.roll(received, (width - HALO - 16 * slot) % width, 1)
        return beside.astype(jnp.float32)[0:24, :]

    def received(g):
        at = slice(g * 32, g * 32 + 32)
        east, west = by_side(core_ref[at, :], cross_ref[at, :])
        return jnp.where(first_six, west, east)

    main_mask = jnp.concatenate(
        [mask_ref[...].astype(jnp.float32), halo_mask_ref[0:8, :]], axis=0
    )
    side_mask = beside_of(received(groups), 0)
    low = lane24 < 3
    high = lane24 >= width - 3
    blank = jnp.zeros((8, width), jnp.float32)
    ones = jnp.ones((32, width), jnp.bfloat16)
    away = {s: lane32 < s if s > 0 else lane32 >= width + s for s in range(-3, 4) if s}
    for g in range(groups):
        both = received(g)
        for j in range(8):
            c = channel_of(channels, g, j)
            near = strips[c * 24 : c * 24 + 24, :]
            far = pltpu.roll(near, width - 2 * HALO, 1)
            change = update_ref[c * 24 : c * 24 + 24, :]
            change = jnp.where(low, near, jnp.where(high, far, change))
            old = jnp.concatenate([field_ref[c], halo_ref[c]], axis=0).astype(jnp.float32)
            main = main_mask * (old[:24, :] + change)
            main = jnp.concatenate([main, blank], axis=0).astype(jnp.bfloat16)
            main_ref[c] = main[:rows, :]
            change = jnp.where(high, near, far)
            beside = side_mask * (beside_of(both, j) + change)
            beside = jnp.concatenate([beside, blank], axis=0).astype(jnp.bfloat16)
            stack = []
            for s in range(-3, 4):
                moved = main
                if s:
                    moved = pltpu.roll(jnp.where(away[s], beside, main), (-s) % width, 1)
                stack.append(moved)
            stack = jnp.concatenate(stack + [ones], axis=0)
            matrix = matrix_ref[c * 16 : c * 16 + 16, :]
            result = jnp.dot(matrix, stack, preferred_element_type=jnp.float32)
            conv[pl.ds(c, 16, stride=channels), :] = result

    mask = mask_ref[...].astype(jnp.float32)
    changes = []

    def put(n, change):
        changes.append(change)
        if n < rows - 1:
            return
        for c in range(0, channels, 8):
            parts = []
            for half in range(0, rows, 8):
                part = [changes[i][c : c + 8, :] for i in range(half, half + 8)]
                parts.append(jnp.swapaxes(jnp.stack(part, axis=0), 0, 1))
            change = jnp.concatenate(parts, axis=1)
            old = main_ref[c : c + 8].astype(jnp.float32)
            out_ref[c : c + 8] = (mask[None] * (old + change)).astype(jnp.bfloat16)

    blocks = [conv_row(conv, channels, i) for i in range(rows)]
    mlp(rows_ref, expand_ref, reduce_ref, 1, blocks, normed, inner, put)


def per_device(
    nlat,
    nlon,
    field,
    land_mask,
    depth_kernel,
    depth_bias,
    norm_gain,
    norm_bias,
    w_expand,
    b_expand,
    w_reduce,
    b_reduce,
):
    channels, rows, width = field.shape
    layers, hidden = b_expand.shape
    bf16, f32 = jnp.bfloat16, jnp.float32
    edge = HALO * channels + 16

    def buffers(count):
        return [
            pltpu.VMEM((channels + 16, count * width), bf16),
            pltpu.VMEM((hidden, count * width), bf16),
        ]

    def pack(upper_if_even, after):
        return pl.pallas_call(
            functools.partial(pack_rows, upper_if_even),
            out_shape=jax.ShapeDtypeStruct((edge, width), bf16),
            in_specs=vmem(2) + [pl.BlockSpec(memory_space=pl.ANY)],
            out_specs=pl.BlockSpec(memory_space=pltpu.VMEM),
            scratch_shapes=[
                pltpu.VMEM((channels * rows, width), f32),
                pltpu.VMEM((rows, width), f32),
            ],
            compiler_params=params(),
            cost_estimate=cost(4e9),
        )(field, land_mask, after)

    begun = pl.pallas_call(
        first_step,
        out_shape=jax.ShapeDtypeStruct((8, 128), f32),
        out_specs=pl.BlockSpec(memory_space=pltpu.VMEM),
        compiler_params=params(),
        cost_estimate=cost(4e9),
    )()
    first = pack(True, begun)
    second = pack(False, first)

    pairs = []
    for d in range(nlon):
        at = d * nlat
        for low in range(1, nlat - 1, 2):
            pairs += [(at + low, at + low + 1), (at + low + 1, at + low)]
        pairs.append((at + nlat - 1, (nlon - 1 - d) * nlat + nlat - 1))
    second = lax.ppermute(second, ("lon", "lat"), pairs)
    pairs = []
    for low in range(0, nlat - 1, 2):
        pairs += [(low, low + 1), (low + 1, low)]
    first = lax.ppermute(first, "lat", pairs)

    kernel = depth_kernel.transpose(2, 3, 0, 1).reshape(49, layers, channels)
    matrix_one, matrix_two, by_channel, expand = pl.pallas_call(
        weights,
        out_shape=[
            jax.ShapeDtypeStruct((channels * 24, 256), bf16),
            jax.ShapeDtypeStruct((channels * 16, 256), bf16),
            jax.ShapeDtypeStruct((layers, 3, channels, 128), f32),
            jax.ShapeDtypeStruct((layers, hidden, channels + 16), bf16),
        ],
        in_specs=vmem(7),
        out_specs=vmem(4),
        scratch_shapes=[
            pltpu.VMEM((channels * 24, 128), f32),
            pltpu.VMEM((channels * 24, 128), f32),
            pltpu.VMEM((128, 128), f32),
            pltpu.VMEM((128, hidden), f32),
        ],
        compiler_params=params(),
        cost_estimate=cost(2e9),
    )(
        kernel,
        depth_bias,
        norm_gain,
        norm_bias,
        w_expand.transpose(0, 2, 1),
        b_expand,
        b_reduce,
    )
    update = pl.pallas_call(
        inner_rows,
        out_shape=jax.ShapeDtypeStruct((channels * 24, width), f32),
        in_specs=vmem(5),
        out_specs=pl.BlockSpec(memory_space=pltpu.VMEM),
        scratch_shapes=[pltpu.VMEM((channels * 16, width), f32)] + buffers(len(INNER)),
        compiler_params=params(),
        cost_estimate=cost(4e9),
    )(field, matrix_one, by_channel, expand, w_reduce)

    strip_rows = (channels // 8 + 1) * 32
    halo, halo_mask, ends = pl.pallas_call(
        join_rows,
        out_shape=[
            jax.ShapeDtypeStruct((channels, 16, width), bf16),
            jax.ShapeDtypeStruct((16, width), f32),
            jax.ShapeDtypeStruct((strip_rows, width), bf16),
        ],
        in_specs=vmem(4) + [pl.BlockSpec(memory_space=pl.ANY)],
        out_specs=vmem(3),
        scratch_shapes=[pltpu.VMEM((channels * 16, width), f32)],
        compiler_params=params(),
    )(field, land_mask, first, second, update)

    pairs = []
    for low in range(0, nlon, 2):
        pairs += [(low, low + 1), (low + 1, low)]
    core = lax.ppermute(ends, "lon", pairs)
    pairs = []
    for low in range(1, nlon, 2):
        after = (low + 1) % nlon
        pairs += [(low, after), (after, low)]
    cross = lax.ppermute(ends, "lon", pairs)

    update = pl.pallas_call(
        edge_rows,
        out_shape=jax.ShapeDtypeStruct((channels * 24, width), f32),
        in_specs=vmem(7),
        out_specs=pl.BlockSpec(memory_space=pltpu.VMEM),
        scratch_shapes=[pltpu.VMEM((channels * 16, width), f32)] + buffers(len(EDGE)),
        input_output_aliases={6: 0},
        compiler_params=params(),
        cost_estimate=cost(4e9),
    )(field, halo, matrix_one, by_channel, expand, w_reduce, update)

    strips = pl.pallas_call(
        edge_columns,
        out_shape=jax.ShapeDtypeStruct((channels * 24, width), f32),
        in_specs=vmem(7),
        out_specs=pl.BlockSpec(memory_space=pltpu.VMEM),
        scratch_shapes=[pltpu.VMEM((channels * 24, width), f32)] + buffers(3),
        compiler_params=params(),
    )(core, cross, ends, matrix_one, by_channel, expand, w_reduce)

    return pl.pallas_call(
        second_layer,
        out_shape=jax.ShapeDtypeStruct((channels, rows, width), bf16),
        in_specs=vmem(12),
        out_specs=pl.BlockSpec(memory_space=pltpu.VMEM),
        scratch_shapes=[
            pltpu.VMEM((channels, rows, width), bf16),
            pltpu.VMEM((channels * 16, width), f32),
        ]
        + buffers(rows),
        compiler_params=params(),
    )(
        field,
        land_mask,
        halo,
        halo_mask,
        core,
        cross,
        strips,
        update,
        matrix_two,
        by_channel,
        expand,
        w_reduce,
    )


def solution(mesh):
    placed = (P(None, "lat", "lon"), P("lat", "lon"), P(), P(), P(), P(), P(), P(), P(), P())
    return jax.shard_map(
        functools.partial(per_device, mesh.shape["lat"], mesh.shape["lon"]),
        mesh=mesh,
        in_specs=placed,
        out_specs=P(None, "lat", "lon"),
        check_vma=False,
    )
```

```python
import functools

import jax
import jax.numpy as jnp
from jax import lax
from jax.experimental import pallas as pl
from jax.experimental.pallas import tpu as pltpu
from jax.sharding import PartitionSpec as P


HALO = 6
VMEM_LIMIT = 20 * 1024 * 1024


def params():
    return pltpu.CompilerParams(vmem_limit_bytes=VMEM_LIMIT)


def cost(flops):
    return pl.CostEstimate(flops=int(flops), bytes_accessed=1 << 20, transcendentals=0)


def vmem(count):
    return [pl.BlockSpec(memory_space=pltpu.VMEM)] * count


def lanes(shape):
    return lax.broadcasted_iota(jnp.int32, shape, len(shape) - 1)


def first_step(out_ref):
    out_ref[...] = jnp.zeros_like(out_ref)


def pack_rows(upper_if_even, field_ref, mask_ref, after_ref, out_ref, wide, wide_mask):
    del after_ref
    channels, rows, width = field_ref.shape
    even = lax.rem(lax.axis_index("lat"), 2) == 0
    take_upper = even if upper_if_even else jnp.logical_not(even)
    wide[...] = field_ref[...].astype(jnp.float32).reshape(channels * rows, width)
    wide_mask[...] = mask_ref[...].astype(jnp.float32)
    for k in range(HALO):
        lower = wide[pl.ds(k, channels, stride=rows), :]
        upper = wide[pl.ds(rows - HALO + k, channels, stride=rows), :]
        at = pl.ds(k * channels, channels)
        out_ref[at, :] = jnp.where(take_upper, upper, lower).astype(jnp.bfloat16)
    pad = jnp.zeros((16 - HALO, width), jnp.float32)
    lower = jnp.concatenate([wide_mask[0:HALO, :], pad], axis=0)
    upper = jnp.concatenate([wide_mask[rows - HALO : rows, :], pad], axis=0)
    at = pl.ds(HALO * channels, 16)
    out_ref[at, :] = jnp.where(take_upper, upper, lower).astype(jnp.bfloat16)


def north_place(row):
    return jnp.where(row < 3, 4 + row, 9 + row)


def south_place(k):
    return k - 3 if k >= 3 else 8 + k


def place_rows(received_ref, is_north, turned, wide, mask_rows, channels):
    width = received_ref.shape[1]
    wide[...] = jnp.zeros_like(wide)
    mask_rows[...] = jnp.zeros_like(mask_rows)
    turn = None
    if turned is not None:
        sub = lax.broadcasted_iota(jnp.int32, (width, width), 0)
        target = lanes((width, width))
        turn = sub == jnp.where(turned, width - 1 - target, target)
        turn = turn.astype(jnp.float32).astype(jnp.bfloat16)

    def rows_at(start, count):
        block = received_ref[start : start + count, :]
        if turn is None:
            return block.astype(jnp.float32)
        return jnp.dot(block, turn, preferred_element_type=jnp.float32)

    masks = rows_at(HALO * channels, 16)
    for k in range(HALO):
        row = k if turned is None else jnp.where(turned, HALO - 1 - k, k)
        place = jnp.where(is_north, north_place(row), south_place(k))
        wide[pl.ds(place, channels, stride=16), :] = rows_at(k * channels, channels)
        mask_rows[pl.ds(place, 1), :] = masks[k : k + 1, :]


def pack_ends(blocks):
    rows, width = blocks[0].shape
    slot = lanes((rows, width)) // 16
    packed = jnp.zeros((rows, width), jnp.bfloat16)
    for j, block in enumerate(blocks):
        packed = jnp.where(slot == j, pltpu.roll(block, 16 * j + HALO, 1), packed)
    return packed


def channel_of(channels, group, slot):
    return slot // 2 * (channels // 4) + group * 2 + slot % 2


def near_rows(field_ref, mask_ref, first_ref, halo_ref, mask_rows, ends_ref, wide):
    channels, rows, width = field_ref.shape
    even = lax.rem(lax.axis_index("lat"), 2) == 0
    place_rows(first_ref, even, None, wide, mask_rows, channels)
    halo_ref[...] = wide[...].astype(jnp.bfloat16).reshape(channels, 16, width)
    groups = channels // 8
    for g in range(groups):
        blocks = [field_ref[channel_of(channels, g, j)] for j in range(8)]
        ends_ref[g * 16 : g * 16 + 16, :] = pack_ends(blocks)
    mask = mask_ref[...].astype(jnp.float32).astype(jnp.bfloat16)
    ends_ref[groups * 16 :, :] = pack_ends([mask])


def pack_side(ends_ref, out_ref, to_east):
    width = ends_ref.shape[1]
    groups = ends_ref.shape[0] // 32 - 1
    lower = lanes((32, width)) % 16 < 8
    for m in range(groups // 2 + 1):
        n = m if m < groups // 2 else groups
        one = ends_ref[n * 32 : n * 32 + 32, :]
        one = jnp.where(to_east, one, pltpu.roll(one, width - HALO, 1))
        if n < groups:
            two = ends_ref[(n + groups // 2) * 32 : (n + groups // 2) * 32 + 32, :]
            two = jnp.where(to_east, pltpu.roll(two, 8, 1), pltpu.roll(two, 8 - HALO, 1))
            one = jnp.where(lower, one, two)
        out_ref[m * 32 : m * 32 + 32, :] = one


def far_rows(
    second_ref,
    near_halo_ref,
    near_mask_ref,
    own_ends_ref,
    after_ref,
    halo_ref,
    halo_mask_ref,
    ends_ref,
    cross_ref,
    wide,
    mask_rows,
):
    del after_ref
    channels, _, width = halo_ref.shape
    lat = lax.axis_index("lat")
    odd = lax.rem(lat, 2) == 1
    folded = lat == lax.axis_size("lat") - 1
    place_rows(second_ref, odd, folded, wide, mask_rows, channels)
    far = wide[...].astype(jnp.bfloat16).reshape(channels, 16, width)
    halo_ref[...] = near_halo_ref[...] + far
    halo_mask = near_mask_ref[...] + mask_rows[...]
    halo_mask_ref[...] = halo_mask
    groups = channels // 8
    for g in range(groups + 1):
        if g < groups:
            blocks = [halo_ref[channel_of(channels, g, j)] for j in range(8)]
        else:
            blocks = [halo_mask.astype(jnp.bfloat16)]
        ends_ref[g * 32 : g * 32 + 16, :] = own_ends_ref[g * 16 : g * 16 + 16, :]
        ends_ref[g * 32 + 16 : g * 32 + 32, :] = pack_ends(blocks)
    pack_side(ends_ref, cross_ref, lax.rem(lax.axis_index("lon"), 2) == 1)


def core_columns(ends_ref, after_ref, core_ref):
    del after_ref
    pack_side(ends_ref, core_ref, lax.rem(lax.axis_index("lon"), 2) == 0)


def in_row(place, first_layer):
    none = jnp.full_like(place, 1000)
    row = jnp.where(place < 16, place, none)
    row = jnp.where((place >= 16) & (place < 19), place - 19, row)
    row = jnp.where((place >= 20) & (place < 23), place - 4, row)
    if first_layer:
        row = jnp.where((place >= 24) & (place < 27), place - 30, row)
        row = jnp.where((place >= 28) & (place < 31), place - 9, row)
    return row


EDGE = (-3, -2, -1, 16, 17, 18, 0, 1, 2, 13, 14, 15)
INNER = (3, 4, 5, 6, 7, 8, 9, 10, 11, 12)


def place_of(row):
    if row < 0:
        return row + 19
    return row if row < 16 else row + 4


def conv_matrices(table, out_ref, left, right, row, rows_out):
    channels, taps = table.shape
    count = len(rows_out)
    folded = lax.axis_index("lat") == lax.axis_size("lat") - 1
    k = lanes((1, 256))
    shift = k // 32
    place = k - shift * 32
    tap = lax.broadcasted_iota(jnp.int32, (taps, 256), 0)
    row = row(place)
    for i, here in enumerate(rows_out):
        if here is None:
            wanted = jnp.full_like(k, -1)
        else:
            a = row - here + 3
            inside = (a >= 0) & (a <= 6) & (shift < 7)
            wanted = a * 7 + shift
            if here > 15:
                wanted = jnp.where(folded, 48 - wanted, wanted)
            wanted = jnp.where(inside, wanted, -1)
            wanted = jnp.where((shift == 7) & (place < 3), 49 + place, wanted)
        picks = (tap == wanted).astype(jnp.float32).astype(jnp.bfloat16)
        matrix = jnp.dot(table, picks, preferred_element_type=jnp.float32)
        left[pl.ds(i, channels, stride=count), :] = matrix[:, :128]
        right[pl.ds(i, channels, stride=count), :] = matrix[:, 128:]
    size = channels * count
    out_ref[:, :128] = left[:size, :].astype(jnp.bfloat16)
    out_ref[:, 128:] = right[:size, :].astype(jnp.bfloat16)


def split_bias(bias):
    high = bias.astype(jnp.bfloat16).astype(jnp.float32)
    rest = bias - high
    mid = rest.astype(jnp.bfloat16).astype(jnp.float32)
    return high, mid, rest - mid


def weights(
    kernel_ref,
    bias_ref,
    gain_ref,
    norm_bias_ref,
    expand_ref,
    expand_bias_ref,
    reduce_bias_ref,
    one_ref,
    two_ref,
    rows_ref,
    expand_out_ref,
    left,
    right,
    turn,
    tall,
):
    taps, layers, channels = kernel_ref.shape
    hidden = expand_ref.shape[2]
    turn[...] = jnp.zeros_like(turn)
    tall[...] = jnp.zeros_like(tall)
    for layer in range(layers):
        for tap in range(taps):
            turn[tap : tap + 1, :channels] = kernel_ref[tap, layer : layer + 1, :]
        parts = split_bias(bias_ref[layer : layer + 1, :])
        for n, part in enumerate(parts):
            turn[taps + n : taps + n + 1, :channels] = part
        table = turn[...].T[:channels, :64].astype(jnp.bfloat16)
        if layer == 0:
            every = EDGE + INNER + (None,) * 2
            row = functools.partial(in_row, first_layer=True)
            conv_matrices(table, one_ref, left, right, row, every)
        else:
            row = functools.partial(in_row, first_layer=False)
            conv_matrices(table, two_ref, left, right, row, tuple(range(16)))
    for layer in range(layers):
        for n, ref in enumerate((gain_ref, norm_bias_ref, reduce_bias_ref)):
            turn[:, :channels] = jnp.broadcast_to(ref[layer : layer + 1, :], (128, channels))
            rows_ref[layer, n] = turn[...].T[:channels, :]
        tall[:channels, :] = expand_ref[layer].astype(jnp.float32) * 0.5
        parts = split_bias(expand_bias_ref[layer : layer + 1, :] * 0.5)
        for n, part in enumerate(parts):
            tall[channels + n : channels + n + 1, :] = part
        for n in range(hidden // 128):
            piece = tall[:, n * 128 : (n + 1) * 128].T
            at = pl.ds(n * 128, 128)
            expand_out_ref[layer, at, :] = piece[:, : channels + 16].astype(jnp.bfloat16)


ERF = (7.97869712e-01, 3.63922860e-02, -8.78263977e-05, -3.66934787e-05, 1.42500782e-06)


def gelu_of_double(half):
    square = half * half
    total = jnp.full_like(half, 2.0 * 4.0 ** (len(ERF) - 1) * ERF[-1])
    for power in range(len(ERF) - 2, -1, -1):
        total = total * square + jnp.full_like(half, 2.0 * 4.0**power * ERF[power])
    return half * jnp.tanh(half * total) + half


def norm(rows_ref, layer, cells):
    average = jnp.mean(cells, axis=0, keepdims=True)
    centered = cells - average
    variance = jnp.mean(centered * centered, axis=0, keepdims=True)
    scaled = centered * lax.rsqrt(variance + 1e-06)
    return (scaled * rows_ref[layer, 0] + rows_ref[layer, 1]).astype(jnp.bfloat16)


def mlp(rows_ref, expand_ref, reduce_ref, layer, blocks, normed_ref, inner_ref, put):
    count = len(blocks)
    channels, width = rows_ref.shape[2:]
    hidden = inner_ref.shape[0]
    wide = count * width
    normed_ref[channels:, :wide] = jnp.ones((16, wide), jnp.bfloat16)
    for n, block in enumerate(blocks):
        at = slice(n * width, (n + 1) * width)
        normed_ref[:channels, at] = norm(rows_ref, layer, block())
    tiles = [slice(n, min(n + 2 * width, wide)) for n in range(0, wide, 2 * width)]
    for at in tiles:
        normed = normed_ref[:, at]
        for part in range(0, hidden, 128):
            matrix = expand_ref[layer, part : part + 128, :]
            half = jnp.dot(matrix, normed, preferred_element_type=jnp.float32)
            for k in range(0, 128, 16):
                values = gelu_of_double(half[k : k + 16, :].astype(jnp.bfloat16))
                inner_ref[part + k : part + k + 16, at] = values
    extra = rows_ref[layer, 2]
    for t, at in enumerate(tiles):
        change = jnp.dot(reduce_ref[layer], inner_ref[:, at], preferred_element_type=jnp.float32)
        for n in range((at.stop - at.start) // width):
            put(t * 2 + n, change[:, n * width : (n + 1) * width] + extra)


def columns_stack(block, ones):
    width = block.shape[1]
    stack = [block if s == 0 else pltpu.roll(block, (-s) % width, 1) for s in range(-3, 4)]
    return jnp.concatenate(stack + [ones], axis=0)


def conv_rows(matrix_ref, stack_of, conv, channels, stride, first, count):
    ones = jnp.ones((matrix_ref.shape[1] // 8, 128), jnp.bfloat16)

    def step(c, carry):
        matrix = matrix_ref[pl.ds(pl.multiple_of(c * stride + first, 8), count), :]
        result = jnp.dot(matrix, stack_of(c, ones), preferred_element_type=jnp.float32)
        conv[pl.ds(c, count, stride=channels), :] = result
        return carry

    lax.fori_loop(0, channels, step, 0, unroll=channels)


def conv_row(conv, channels, i):
    return lambda: conv[i * channels : (i + 1) * channels, :]


def inner_rows(
    field_ref, matrix_ref, rows_ref, expand_ref, reduce_ref, update_ref, conv, normed, inner
):
    channels, rows, width = field_ref.shape
    none = jnp.zeros((16, width), jnp.bfloat16)

    def stack_of(c, ones):
        return columns_stack(jnp.concatenate([field_ref[c], none], axis=0), ones)

    conv_rows(matrix_ref, stack_of, conv, channels, 24, 8, 16)

    def put(n, change):
        update_ref[pl.ds(INNER[n], channels, stride=24), :] = change

    blocks = [conv_row(conv, channels, i + len(EDGE) - 8) for i in range(len(INNER))]
    mlp(rows_ref, expand_ref, reduce_ref, 0, blocks, normed, inner, put)


def edge_rows(
    field_ref,
    halo_ref,
    matrix_ref,
    rows_ref,
    expand_ref,
    reduce_ref,
    old_ref,
    update_ref,
    conv,
    normed,
    inner,
):
    del old_ref
    channels, _, width = field_ref.shape

    def stack_of(c, ones):
        return columns_stack(jnp.concatenate([field_ref[c], halo_ref[c]], axis=0), ones)

    conv_rows(matrix_ref, stack_of, conv, channels, 24, 0, 16)
    for empty in (19, 23):
        update_ref[pl.ds(empty, channels, stride=24), :] = jnp.zeros((channels, width), jnp.float32)

    def put(n, change):
        update_ref[pl.ds(place_of(EDGE[n]), channels, stride=24), :] = change

    blocks = [conv_row(conv, channels, i) for i in range(len(EDGE))]
    mlp(rows_ref, expand_ref, reduce_ref, 0, blocks, normed, inner, put)


def neighbours(core_ref, cross_ref, group, groups):
    width = core_ref.shape[1]
    half = groups // 2
    m, upper = (half, 0) if group == groups else (group % half, group // half)
    core = core_ref[m * 32 : m * 32 + 32, :]
    cross = cross_ref[m * 32 : m * 32 + 32, :]
    lon_even = lax.rem(lax.axis_index("lon"), 2) == 0
    east = jnp.where(lon_even, core, cross)
    west = jnp.where(lon_even, cross, core)
    east = pltpu.roll(east, (HALO - 8 * upper) % width, 1)
    return east, pltpu.roll(west, width - 8, 1) if upper else west


def edge_columns(
    core_ref,
    cross_ref,
    ends_ref,
    matrix_ref,
    rows_ref,
    expand_ref,
    reduce_ref,
    strips,
    conv,
    normed,
    inner,
):
    channels, width = rows_ref.shape[2:]
    quarter = channels // 4
    groups = channels // 8
    lane32 = lanes((32, width))
    first_six = lane32 % 16 < HALO
    first_twelve = lane32 % 32 < 2 * HALO
    ones = jnp.ones((32, width), jnp.bfloat16)
    for g in range(groups):
        at = slice(g * 32, g * 32 + 32)
        east, west = neighbours(core_ref, cross_ref, g, groups)
        own = ends_ref[at, :]
        at_west = jnp.where(first_six, west, own)
        at_east = jnp.where(first_six, own, east)
        for t in range(2):
            left = pltpu.roll(at_west, width - 16, 1) if t else at_west
            right = pltpu.roll(at_east, (2 * HALO - 16 * t) % width, 1)
            block = jnp.where(first_twelve, left, right)
            some = [channel_of(channels, g, 2 * n + t) for n in range(4)]
            matrix = jnp.concatenate(
                [matrix_ref[c * 24 : c * 24 + 24, :] for c in some], axis=0
            )
            stack = columns_stack(block, ones)
            result = jnp.dot(matrix, stack, preferred_element_type=jnp.float32)
            for n, c in enumerate(some):
                conv[pl.ds(c, 24, stride=channels), :] = result[n * 24 : n * 24 + 24, :]

    order = {place_of(row): i for i, row in enumerate(EDGE + INNER)}
    lane = lanes((quarter, width))
    starts = [32 * (q // 2) + 6 * (q % 2) for q in range(8)]
    inside = [
        ((lane >= s + 3) & (lane < s + 9)) | ((lane >= s + 15) & (lane < s + 21)) for s in starts
    ]
    packs = []
    for p in range(3):
        parts = []
        for n in range(4):
            packed = jnp.zeros((quarter, width), jnp.float32)
            for q, start in enumerate(starts):
                if p * 8 + q in order:
                    row = order[p * 8 + q] * channels + n * quarter
                    block = conv[row : row + quarter, :]
                    block = pltpu.roll(block, (start - 32 * n) % width, 1)
                    packed = jnp.where(inside[q], block, packed)
            parts.append(packed)
        packs.append(jnp.concatenate(parts, axis=0))

    def put(p, change):
        for q, start in enumerate(starts):
            near = pltpu.roll(change, (width - 6 - start) % width, 1)
            strips[pl.ds(p * 8 + q, channels, stride=24), :] = near

    blocks = [functools.partial(lambda block: block, packed) for packed in packs]
    mlp(rows_ref, expand_ref, reduce_ref, 0, blocks, normed, inner, put)


def second_layer(
    field_ref,
    mask_ref,
    halo_ref,
    halo_mask_ref,
    core_ref,
    cross_ref,
    strips,
    update_ref,
    matrix_ref,
    rows_ref,
    expand_ref,
    reduce_ref,
    out_ref,
    main_ref,
    conv,
    normed,
    inner,
):
    channels, rows, width = out_ref.shape
    groups = channels // 8
    lane32 = lanes((32, width))
    lane24 = lanes((24, width))
    first_six = lane32 % 16 < HALO

    def beside_of(received, slot):
        beside = pltpu.roll(received, (width - HALO - 16 * slot) % width, 1)
        return beside.astype(jnp.float32)[0:24, :]

    def received(g):
        east, west = neighbours(core_ref, cross_ref, g, groups)
        return jnp.where(first_six, west, east)

    main_mask = jnp.concatenate(
        [mask_ref[...].astype(jnp.float32), halo_mask_ref[0:8, :]], axis=0
    )
    side_mask = beside_of(received(groups), 0)
    low = lane24 < 3
    high = lane24 >= width - 3
    blank = jnp.zeros((8, width), jnp.float32)
    ones = jnp.ones((32, width), jnp.bfloat16)
    away = {s: lane32 < s if s > 0 else lane32 >= width + s for s in range(-3, 4) if s}
    for g in range(groups):
        both = received(g)
        for j in range(8):
            c = channel_of(channels, g, j)
            near = strips[c * 24 : c * 24 + 24, :]
            far = pltpu.roll(near, width - 2 * HALO, 1)
            change = update_ref[c * 24 : c * 24 + 24, :]
            change = jnp.where(low, near, jnp.where(high, far, change))
            old = jnp.concatenate([field_ref[c], halo_ref[c]], axis=0).astype(jnp.float32)
            main = main_mask * (old[:24, :] + change)
            main = jnp.concatenate([main, blank], axis=0).astype(jnp.bfloat16)
            main_ref[c] = main[:rows, :]
            change = jnp.where(high, near, far)
            beside = side_mask * (beside_of(both, j) + change)
            beside = jnp.concatenate([beside, blank], axis=0).astype(jnp.bfloat16)
            stack = []
            for s in range(-3, 4):
                moved = main
                if s:
                    moved = pltpu.roll(jnp.where(away[s], beside, main), (-s) % width, 1)
                stack.append(moved)
            stack = jnp.concatenate(stack + [ones], axis=0)
            matrix = matrix_ref[c * 16 : c * 16 + 16, :]
            result = jnp.dot(matrix, stack, preferred_element_type=jnp.float32)
            conv[pl.ds(c, 16, stride=channels), :] = result

    mask = mask_ref[...].astype(jnp.float32)
    changes = []

    def put(n, change):
        changes.append(change)
        if n < rows - 1:
            return
        for c in range(0, channels, 8):
            parts = []
            for half in range(0, rows, 8):
                part = [changes[i][c : c + 8, :] for i in range(half, half + 8)]
                parts.append(jnp.swapaxes(jnp.stack(part, axis=0), 0, 1))
            change = jnp.concatenate(parts, axis=1)
            old = main_ref[c : c + 8].astype(jnp.float32)
            out_ref[c : c + 8] = (mask[None] * (old + change)).astype(jnp.bfloat16)

    blocks = [conv_row(conv, channels, i) for i in range(rows)]
    mlp(rows_ref, expand_ref, reduce_ref, 1, blocks, normed, inner, put)


def per_device(
    nlat,
    nlon,
    field,
    land_mask,
    depth_kernel,
    depth_bias,
    norm_gain,
    norm_bias,
    w_expand,
    b_expand,
    w_reduce,
    b_reduce,
):
    channels, rows, width = field.shape
    layers, hidden = b_expand.shape
    bf16, f32 = jnp.bfloat16, jnp.float32
    edge = HALO * channels + 16

    def buffers(count):
        return [
            pltpu.VMEM((channels + 16, count * width), bf16),
            pltpu.VMEM((hidden, count * width), bf16),
        ]

    def pack(upper_if_even, after):
        return pl.pallas_call(
            functools.partial(pack_rows, upper_if_even),
            out_shape=jax.ShapeDtypeStruct((edge, width), bf16),
            in_specs=vmem(2) + [pl.BlockSpec(memory_space=pl.ANY)],
            out_specs=pl.BlockSpec(memory_space=pltpu.VMEM),
            scratch_shapes=[
                pltpu.VMEM((channels * rows, width), f32),
                pltpu.VMEM((rows, width), f32),
            ],
            compiler_params=params(),
            cost_estimate=cost(4e9),
        )(field, land_mask, after)

    begun = pl.pallas_call(
        first_step,
        out_shape=jax.ShapeDtypeStruct((8, 128), f32),
        out_specs=pl.BlockSpec(memory_space=pltpu.VMEM),
        compiler_params=params(),
        cost_estimate=cost(4e9),
    )()
    first = pack(True, begun)
    second = pack(False, first)

    pairs = []
    for d in range(nlon):
        at = d * nlat
        for low in range(1, nlat - 1, 2):
            pairs += [(at + low, at + low + 1), (at + low + 1, at + low)]
        pairs.append((at + nlat - 1, (nlon - 1 - d) * nlat + nlat - 1))
    second = lax.ppermute(second, ("lon", "lat"), pairs)
    pairs = []
    for low in range(0, nlat - 1, 2):
        pairs += [(low, low + 1), (low + 1, low)]
    first = lax.ppermute(first, "lat", pairs)

    kernel = depth_kernel.transpose(2, 3, 0, 1).reshape(49, layers, channels)
    matrix_one, matrix_two, by_channel, expand = pl.pallas_call(
        weights,
        out_shape=[
            jax.ShapeDtypeStruct((channels * 24, 256), bf16),
            jax.ShapeDtypeStruct((channels * 16, 256), bf16),
            jax.ShapeDtypeStruct((layers, 3, channels, 128), f32),
            jax.ShapeDtypeStruct((layers, hidden, channels + 16), bf16),
        ],
        in_specs=vmem(7),
        out_specs=vmem(4),
        scratch_shapes=[
            pltpu.VMEM((channels * 24, 128), f32),
            pltpu.VMEM((channels * 24, 128), f32),
            pltpu.VMEM((128, 128), f32),
            pltpu.VMEM((128, hidden), f32),
        ],
        compiler_params=params(),
        cost_estimate=cost(2e9),
    )(
        kernel,
        depth_bias,
        norm_gain,
        norm_bias,
        w_expand.transpose(0, 2, 1),
        b_expand,
        b_reduce,
    )
    update = pl.pallas_call(
        inner_rows,
        out_shape=jax.ShapeDtypeStruct((channels * 24, width), f32),
        in_specs=vmem(5),
        out_specs=pl.BlockSpec(memory_space=pltpu.VMEM),
        scratch_shapes=[pltpu.VMEM((channels * 16, width), f32)] + buffers(len(INNER)),
        compiler_params=params(),
        cost_estimate=cost(4e9),
    )(field, matrix_one, by_channel, expand, w_reduce)

    groups = channels // 8 + 1
    sent_rows = (channels // 16 + 1) * 32
    near_halo, near_mask, own_ends = pl.pallas_call(
        near_rows,
        out_shape=[
            jax.ShapeDtypeStruct((channels, 16, width), bf16),
            jax.ShapeDtypeStruct((16, width), f32),
            jax.ShapeDtypeStruct((groups * 16, width), bf16),
        ],
        in_specs=vmem(3),
        out_specs=vmem(3),
        scratch_shapes=[pltpu.VMEM((channels * 16, width), f32)],
        compiler_params=params(),
        cost_estimate=cost(1e9),
    )(field, land_mask, first)
    halo, halo_mask, ends, cross = pl.pallas_call(
        far_rows,
        out_shape=[
            jax.ShapeDtypeStruct((channels, 16, width), bf16),
            jax.ShapeDtypeStruct((16, width), f32),
            jax.ShapeDtypeStruct((groups * 32, width), bf16),
            jax.ShapeDtypeStruct((sent_rows, width), bf16),
        ],
        in_specs=vmem(4) + [pl.BlockSpec(memory_space=pl.ANY)],
        out_specs=vmem(4),
        scratch_shapes=[
            pltpu.VMEM((channels * 16, width), f32),
            pltpu.VMEM((16, width), f32),
        ],
        compiler_params=params(),
    )(second, near_halo, near_mask, own_ends, update)
    core = pl.pallas_call(
        core_columns,
        out_shape=jax.ShapeDtypeStruct((sent_rows, width), bf16),
        in_specs=vmem(1) + [pl.BlockSpec(memory_space=pl.ANY)],
        out_specs=pl.BlockSpec(memory_space=pltpu.VMEM),
        compiler_params=params(),
    )(ends, cross)

    pairs = []
    for low in range(0, nlon, 2):
        pairs += [(low, low + 1), (low + 1, low)]
    core = lax.ppermute(core, "lon", pairs)
    pairs = []
    for low in range(1, nlon, 2):
        after = (low + 1) % nlon
        pairs += [(low, after), (after, low)]
    cross = lax.ppermute(cross, "lon", pairs)

    update = pl.pallas_call(
        edge_rows,
        out_shape=jax.ShapeDtypeStruct((channels * 24, width), f32),
        in_specs=vmem(7),
        out_specs=pl.BlockSpec(memory_space=pltpu.VMEM),
        scratch_shapes=[pltpu.VMEM((channels * 16, width), f32)] + buffers(len(EDGE)),
        input_output_aliases={6: 0},
        compiler_params=params(),
        cost_estimate=cost(4e9),
    )(field, halo, matrix_one, by_channel, expand, w_reduce, update)

    strips = pl.pallas_call(
        edge_columns,
        out_shape=jax.ShapeDtypeStruct((channels * 24, width), f32),
        in_specs=vmem(7),
        out_specs=pl.BlockSpec(memory_space=pltpu.VMEM),
        scratch_shapes=[pltpu.VMEM((channels * 24, width), f32)] + buffers(3),
        compiler_params=params(),
    )(core, cross, ends, matrix_one, by_channel, expand, w_reduce)

    return pl.pallas_call(
        second_layer,
        out_shape=jax.ShapeDtypeStruct((channels, rows, width), bf16),
        in_specs=vmem(12),
        out_specs=pl.BlockSpec(memory_space=pltpu.VMEM),
        scratch_shapes=[
            pltpu.VMEM((channels, rows, width), bf16),
            pltpu.VMEM((channels * 16, width), f32),
        ]
        + buffers(rows),
        compiler_params=params(),
    )(
        field,
        land_mask,
        halo,
        halo_mask,
        core,
        cross,
        strips,
        update,
        matrix_two,
        by_channel,
        expand,
        w_reduce,
    )


def solution(mesh):
    placed = (P(None, "lat", "lon"), P("lat", "lon"), P(), P(), P(), P(), P(), P(), P(), P())
    return jax.shard_map(
        functools.partial(per_device, mesh.shape["lat"], mesh.shape["lon"]),
        mesh=mesh,
        in_specs=placed,
        out_specs=P(None, "lat", "lon"),
        check_vma=False,
    )
```

```python
import functools

import jax
import jax.numpy as jnp
from jax import lax
from jax.experimental import pallas as pl
from jax.experimental.pallas import tpu as pltpu
from jax.sharding import PartitionSpec as P


HALO = 6
VMEM_LIMIT = 20 * 1024 * 1024


def params():
    return pltpu.CompilerParams(vmem_limit_bytes=VMEM_LIMIT)


def cost(flops):
    return pl.CostEstimate(flops=int(flops), bytes_accessed=1 << 20, transcendentals=0)


def vmem(count):
    return [pl.BlockSpec(memory_space=pltpu.VMEM)] * count


def lanes(shape):
    return lax.broadcasted_iota(jnp.int32, shape, len(shape) - 1)


def first_step(out_ref):
    out_ref[...] = jnp.zeros_like(out_ref)


def pack_rows(upper_if_even, field_ref, mask_ref, after_ref, out_ref, wide, wide_mask):
    del after_ref
    channels, rows, width = field_ref.shape
    even = lax.rem(lax.axis_index("lat"), 2) == 0
    take_upper = even if upper_if_even else jnp.logical_not(even)
    wide[...] = field_ref[...].astype(jnp.float32).reshape(channels * rows, width)
    wide_mask[...] = mask_ref[...].astype(jnp.float32)
    for k in range(HALO):
        lower = wide[pl.ds(k, channels, stride=rows), :]
        upper = wide[pl.ds(rows - HALO + k, channels, stride=rows), :]
        at = pl.ds(k * channels, channels)
        out_ref[at, :] = jnp.where(take_upper, upper, lower).astype(jnp.bfloat16)
    pad = jnp.zeros((16 - HALO, width), jnp.float32)
    lower = jnp.concatenate([wide_mask[0:HALO, :], pad], axis=0)
    upper = jnp.concatenate([wide_mask[rows - HALO : rows, :], pad], axis=0)
    at = pl.ds(HALO * channels, 16)
    out_ref[at, :] = jnp.where(take_upper, upper, lower).astype(jnp.bfloat16)


def north_place(row):
    return jnp.where(row < 3, 4 + row, 9 + row)


def south_place(k):
    return k - 3 if k >= 3 else 8 + k


def place_rows(received_ref, is_north, turned, wide, mask_rows, channels):
    width = received_ref.shape[1]
    wide[...] = jnp.zeros_like(wide)
    mask_rows[...] = jnp.zeros_like(mask_rows)
    turn = None
    if turned is not None:
        sub = lax.broadcasted_iota(jnp.int32, (width, width), 0)
        target = lanes((width, width))
        turn = sub == jnp.where(turned, width - 1 - target, target)
        turn = turn.astype(jnp.float32).astype(jnp.bfloat16)

    def rows_at(start, count):
        block = received_ref[start : start + count, :]
        if turn is None:
            return block.astype(jnp.float32)
        return jnp.dot(block, turn, preferred_element_type=jnp.float32)

    masks = rows_at(HALO * channels, 16)
    for k in range(HALO):
        row = k if turned is None else jnp.where(turned, HALO - 1 - k, k)
        place = jnp.where(is_north, north_place(row), south_place(k))
        wide[pl.ds(place, channels, stride=16), :] = rows_at(k * channels, channels)
        mask_rows[pl.ds(place, 1), :] = masks[k : k + 1, :]


def pack_ends(blocks):
    rows, width = blocks[0].shape
    slot = lanes((rows, width)) // 16
    packed = jnp.zeros((rows, width), jnp.bfloat16)
    for j, block in enumerate(blocks):
        packed = jnp.where(slot == j, pltpu.roll(block, 16 * j + HALO, 1), packed)
    return packed


def channel_of(channels, group, slot):
    return slot // 2 * (channels // 4) + group * 2 + slot % 2


def over_wrap():
    lon = lax.axis_index("lon")
    return (lon == 0) | (lon == lax.axis_size("lon") - 1)


def near_rows(
    field_ref, mask_ref, first_ref, halo_ref, mask_rows, ends_ref, wrap_ref, wide, all_ends
):
    channels, rows, width = field_ref.shape
    even = lax.rem(lax.axis_index("lat"), 2) == 0
    place_rows(first_ref, even, None, wide, mask_rows, channels)
    halo_ref[...] = wide[...].astype(jnp.bfloat16).reshape(channels, 16, width)
    groups = channels // 8
    for g in range(groups):
        blocks = [field_ref[channel_of(channels, g, j)] for j in range(8)]
        ends_ref[g * 16 : g * 16 + 16, :] = pack_ends(blocks)
    mask = mask_ref[...].astype(jnp.float32).astype(jnp.bfloat16)
    ends_ref[groups * 16 :, :] = pack_ends([mask])
    wrap_ref[...] = jnp.zeros_like(wrap_ref)

    @pl.when(over_wrap())
    def _():
        join_ends(ends_ref, halo_ref, mask_rows, all_ends)
        pack_side(all_ends, wrap_ref, lax.rem(lax.axis_index("lon"), 2) == 1)


def join_ends(own_ends_ref, halo_ref, mask_rows, ends_ref):
    channels = halo_ref.shape[0]
    groups = channels // 8
    for g in range(groups + 1):
        if g < groups:
            blocks = [halo_ref[channel_of(channels, g, j)] for j in range(8)]
        else:
            blocks = [mask_rows[...].astype(jnp.bfloat16)]
        own = jnp.zeros((16, halo_ref.shape[2]), jnp.bfloat16)
        if own_ends_ref is not None:
            own = own_ends_ref[g * 16 : g * 16 + 16, :]
        ends_ref[g * 32 : g * 32 + 16, :] = own
        ends_ref[g * 32 + 16 : g * 32 + 32, :] = pack_ends(blocks)


def pack_side(ends_ref, out_ref, to_east):
    width = ends_ref.shape[1]
    groups = ends_ref.shape[0] // 32 - 1
    lower = lanes((32, width)) % 16 < 8
    for m in range(groups // 2 + 1):
        n = m if m < groups // 2 else groups
        one = ends_ref[n * 32 : n * 32 + 32, :]
        one = jnp.where(to_east, one, pltpu.roll(one, width - HALO, 1))
        if n < groups:
            two = ends_ref[(n + groups // 2) * 32 : (n + groups // 2) * 32 + 32, :]
            two = jnp.where(to_east, pltpu.roll(two, 8, 1), pltpu.roll(two, 8 - HALO, 1))
            one = jnp.where(lower, one, two)
        out_ref[m * 32 : m * 32 + 32, :] = one


def far_rows(
    mirrored,
    second_ref,
    sent_ref,
    near_halo_ref,
    near_mask_ref,
    own_ends_ref,
    after_ref,
    halo_ref,
    halo_mask_ref,
    ends_ref,
    cross_ref,
    own_ref,
    wide,
    mask_rows,
):
    del after_ref
    channels, _, width = halo_ref.shape
    lat = lax.axis_index("lat")
    odd = lax.rem(lat, 2) == 1
    lon_odd = lax.rem(lax.axis_index("lon"), 2) == 1
    folded = lat == lax.axis_size("lat") - 1
    own_ref[...] = jnp.zeros_like(own_ref)
    if mirrored:

        @pl.when(folded & over_wrap())
        def _():
            place_rows(sent_ref, odd, folded, wide, mask_rows, channels)
            halo_ref[...] = wide[...].astype(jnp.bfloat16).reshape(channels, 16, width)
            join_ends(None, halo_ref, mask_rows, ends_ref)
            pack_side(ends_ref, own_ref, jnp.logical_not(lon_odd))

    place_rows(second_ref, odd, folded, wide, mask_rows, channels)
    far = wide[...].astype(jnp.bfloat16).reshape(channels, 16, width)
    halo_ref[...] = near_halo_ref[...] + far
    halo_mask_ref[...] = near_mask_ref[...] + mask_rows[...]
    join_ends(own_ends_ref, halo_ref, halo_mask_ref, ends_ref)
    pack_side(ends_ref, cross_ref, lon_odd)


def core_columns(ends_ref, after_ref, core_ref):
    del after_ref
    pack_side(ends_ref, core_ref, lax.rem(lax.axis_index("lon"), 2) == 0)


def in_row(place, first_layer):
    none = jnp.full_like(place, 1000)
    row = jnp.where(place < 16, place, none)
    row = jnp.where((place >= 16) & (place < 19), place - 19, row)
    row = jnp.where((place >= 20) & (place < 23), place - 4, row)
    if first_layer:
        row = jnp.where((place >= 24) & (place < 27), place - 30, row)
        row = jnp.where((place >= 28) & (place < 31), place - 9, row)
    return row


EDGE = (-3, -2, -1, 16, 17, 18, 0, 1, 2, 13, 14, 15)
INNER = (3, 4, 5, 6, 7, 8, 9, 10, 11, 12)


def place_of(row):
    if row < 0:
        return row + 19
    return row if row < 16 else row + 4


def conv_matrices(table, out_ref, left, right, row, rows_out):
    channels, taps = table.shape
    count = len(rows_out)
    folded = lax.axis_index("lat") == lax.axis_size("lat") - 1
    k = lanes((1, 256))
    shift = k // 32
    place = k - shift * 32
    tap = lax.broadcasted_iota(jnp.int32, (taps, 256), 0)
    row = row(place)
    for i, here in enumerate(rows_out):
        if here is None:
            wanted = jnp.full_like(k, -1)
        else:
            a = row - here + 3
            inside = (a >= 0) & (a <= 6) & (shift < 7)
            wanted = a * 7 + shift
            if here > 15:
                wanted = jnp.where(folded, 48 - wanted, wanted)
            wanted = jnp.where(inside, wanted, -1)
            wanted = jnp.where((shift == 7) & (place < 3), 49 + place, wanted)
        picks = (tap == wanted).astype(jnp.float32).astype(jnp.bfloat16)
        matrix = jnp.dot(table, picks, preferred_element_type=jnp.float32)
        left[pl.ds(i, channels, stride=count), :] = matrix[:, :128]
        right[pl.ds(i, channels, stride=count), :] = matrix[:, 128:]
    size = channels * count
    out_ref[:, :128] = left[:size, :].astype(jnp.bfloat16)
    out_ref[:, 128:] = right[:size, :].astype(jnp.bfloat16)


def split_bias(bias):
    high = bias.astype(jnp.bfloat16).astype(jnp.float32)
    rest = bias - high
    mid = rest.astype(jnp.bfloat16).astype(jnp.float32)
    return high, mid, rest - mid


def weights(
    kernel_ref,
    bias_ref,
    gain_ref,
    norm_bias_ref,
    expand_ref,
    expand_bias_ref,
    reduce_bias_ref,
    one_ref,
    two_ref,
    rows_ref,
    expand_out_ref,
    left,
    right,
    turn,
    tall,
):
    taps, layers, channels = kernel_ref.shape
    hidden = expand_ref.shape[2]
    turn[...] = jnp.zeros_like(turn)
    tall[...] = jnp.zeros_like(tall)
    for layer in range(layers):
        for tap in range(taps):
            turn[tap : tap + 1, :channels] = kernel_ref[tap, layer : layer + 1, :]
        parts = split_bias(bias_ref[layer : layer + 1, :])
        for n, part in enumerate(parts):
            turn[taps + n : taps + n + 1, :channels] = part
        table = turn[...].T[:channels, :64].astype(jnp.bfloat16)
        if layer == 0:
            every = EDGE + INNER + (None,) * 2
            row = functools.partial(in_row, first_layer=True)
            conv_matrices(table, one_ref, left, right, row, every)
        else:
            row = functools.partial(in_row, first_layer=False)
            conv_matrices(table, two_ref, left, right, row, tuple(range(16)))
    for layer in range(layers):
        for n, ref in enumerate((gain_ref, norm_bias_ref, reduce_bias_ref)):
            turn[:, :channels] = jnp.broadcast_to(ref[layer : layer + 1, :], (128, channels))
            rows_ref[layer, n] = turn[...].T[:channels, :]
        tall[:channels, :] = expand_ref[layer].astype(jnp.float32) * 0.5
        parts = split_bias(expand_bias_ref[layer : layer + 1, :] * 0.5)
        for n, part in enumerate(parts):
            tall[channels + n : channels + n + 1, :] = part
        for n in range(hidden // 128):
            piece = tall[:, n * 128 : (n + 1) * 128].T
            at = pl.ds(n * 128, 128)
            expand_out_ref[layer, at, :] = piece[:, : channels + 16].astype(jnp.bfloat16)


ERF = (7.97869712e-01, 3.63922860e-02, -8.78263977e-05, -3.66934787e-05, 1.42500782e-06)


def gelu_of_double(half):
    square = half * half
    total = jnp.full_like(half, 2.0 * 4.0 ** (len(ERF) - 1) * ERF[-1])
    for power in range(len(ERF) - 2, -1, -1):
        total = total * square + jnp.full_like(half, 2.0 * 4.0**power * ERF[power])
    return half * jnp.tanh(half * total) + half


def norm(rows_ref, layer, cells):
    average = jnp.mean(cells, axis=0, keepdims=True)
    centered = cells - average
    variance = jnp.mean(centered * centered, axis=0, keepdims=True)
    scaled = centered * lax.rsqrt(variance + 1e-06)
    return (scaled * rows_ref[layer, 0] + rows_ref[layer, 1]).astype(jnp.bfloat16)


def mlp(rows_ref, expand_ref, reduce_ref, layer, blocks, normed_ref, inner_ref, put):
    count = len(blocks)
    channels, width = rows_ref.shape[2:]
    hidden = inner_ref.shape[0]
    wide = count * width
    normed_ref[channels:, :wide] = jnp.ones((16, wide), jnp.bfloat16)
    for n, block in enumerate(blocks):
        at = slice(n * width, (n + 1) * width)
        normed_ref[:channels, at] = norm(rows_ref, layer, block())
    tiles = [slice(n, min(n + 2 * width, wide)) for n in range(0, wide, 2 * width)]
    for at in tiles:
        normed = normed_ref[:, at]
        for part in range(0, hidden, 128):
            matrix = expand_ref[layer, part : part + 128, :]
            half = jnp.dot(matrix, normed, preferred_element_type=jnp.float32)
            for k in range(0, 128, 16):
                values = gelu_of_double(half[k : k + 16, :].astype(jnp.bfloat16))
                inner_ref[part + k : part + k + 16, at] = values
    extra = rows_ref[layer, 2]
    for t, at in enumerate(tiles):
        change = jnp.dot(reduce_ref[layer], inner_ref[:, at], preferred_element_type=jnp.float32)
        for n in range((at.stop - at.start) // width):
            put(t * 2 + n, change[:, n * width : (n + 1) * width] + extra)


def columns_stack(block, ones):
    width = block.shape[1]
    stack = [block if s == 0 else pltpu.roll(block, (-s) % width, 1) for s in range(-3, 4)]
    return jnp.concatenate(stack + [ones], axis=0)


def conv_rows(matrix_ref, stack_of, conv, channels, stride, first, count):
    ones = jnp.ones((matrix_ref.shape[1] // 8, 128), jnp.bfloat16)

    def step(c, carry):
        matrix = matrix_ref[pl.ds(pl.multiple_of(c * stride + first, 8), count), :]
        result = jnp.dot(matrix, stack_of(c, ones), preferred_element_type=jnp.float32)
        conv[pl.ds(c, count, stride=channels), :] = result
        return carry

    lax.fori_loop(0, channels, step, 0, unroll=channels)


def conv_row(conv, channels, i):
    return lambda: conv[i * channels : (i + 1) * channels, :]


def inner_rows(
    field_ref, matrix_ref, rows_ref, expand_ref, reduce_ref, update_ref, conv, normed, inner
):
    channels, rows, width = field_ref.shape
    none = jnp.zeros((16, width), jnp.bfloat16)

    def stack_of(c, ones):
        return columns_stack(jnp.concatenate([field_ref[c], none], axis=0), ones)

    conv_rows(matrix_ref, stack_of, conv, channels, 24, 8, 16)

    def put(n, change):
        update_ref[pl.ds(INNER[n], channels, stride=24), :] = change

    blocks = [conv_row(conv, channels, i + len(EDGE) - 8) for i in range(len(INNER))]
    mlp(rows_ref, expand_ref, reduce_ref, 0, blocks, normed, inner, put)


def edge_rows(
    field_ref,
    halo_ref,
    matrix_ref,
    rows_ref,
    expand_ref,
    reduce_ref,
    old_ref,
    update_ref,
    conv,
    normed,
    inner,
):
    del old_ref
    channels, _, width = field_ref.shape

    def stack_of(c, ones):
        return columns_stack(jnp.concatenate([field_ref[c], halo_ref[c]], axis=0), ones)

    conv_rows(matrix_ref, stack_of, conv, channels, 24, 0, 16)
    for empty in (19, 23):
        update_ref[pl.ds(empty, channels, stride=24), :] = jnp.zeros((channels, width), jnp.float32)

    def put(n, change):
        update_ref[pl.ds(place_of(EDGE[n]), channels, stride=24), :] = change

    blocks = [conv_row(conv, channels, i) for i in range(len(EDGE))]
    mlp(rows_ref, expand_ref, reduce_ref, 0, blocks, normed, inner, put)


def neighbours(core_ref, cross_refs, group, groups):
    width = core_ref.shape[1]
    half = groups // 2
    m, upper = (half, 0) if group == groups else (group % half, group // half)
    core = core_ref[m * 32 : m * 32 + 32, :]
    cross = sum(ref[m * 32 : m * 32 + 32, :] for ref in cross_refs)
    lon_even = lax.rem(lax.axis_index("lon"), 2) == 0
    east = jnp.where(lon_even, core, cross)
    west = jnp.where(lon_even, cross, core)
    east = pltpu.roll(east, (HALO - 8 * upper) % width, 1)
    return east, pltpu.roll(west, width - 8, 1) if upper else west


def edge_columns(
    core_ref,
    cross_ref,
    wrap_ref,
    own_ref,
    ends_ref,
    matrix_ref,
    rows_ref,
    expand_ref,
    reduce_ref,
    strips,
    conv,
    normed,
    inner,
):
    channels, width = rows_ref.shape[2:]
    quarter = channels // 4
    groups = channels // 8
    lane32 = lanes((32, width))
    first_six = lane32 % 16 < HALO
    first_twelve = lane32 % 32 < 2 * HALO
    ones = jnp.ones((32, width), jnp.bfloat16)
    for g in range(groups):
        at = slice(g * 32, g * 32 + 32)
        east, west = neighbours(core_ref, (cross_ref, wrap_ref, own_ref), g, groups)
        own = ends_ref[at, :]
        at_west = jnp.where(first_six, west, own)
        at_east = jnp.where(first_six, own, east)
        for t in range(2):
            left = pltpu.roll(at_west, width - 16, 1) if t else at_west
            right = pltpu.roll(at_east, (2 * HALO - 16 * t) % width, 1)
            block = jnp.where(first_twelve, left, right)
            some = [channel_of(channels, g, 2 * n + t) for n in range(4)]
            matrix = jnp.concatenate(
                [matrix_ref[c * 24 : c * 24 + 24, :] for c in some], axis=0
            )
            stack = columns_stack(block, ones)
            result = jnp.dot(matrix, stack, preferred_element_type=jnp.float32)
            for n, c in enumerate(some):
                conv[pl.ds(c, 24, stride=channels), :] = result[n * 24 : n * 24 + 24, :]

    order = {place_of(row): i for i, row in enumerate(EDGE + INNER)}
    lane = lanes((quarter, width))
    starts = [32 * (q // 2) + 6 * (q % 2) for q in range(8)]
    inside = [
        ((lane >= s + 3) & (lane < s + 9)) | ((lane >= s + 15) & (lane < s + 21)) for s in starts
    ]
    packs = []
    for p in range(3):
        parts = []
        for n in range(4):
            packed = jnp.zeros((quarter, width), jnp.float32)
            for q, start in enumerate(starts):
                if p * 8 + q in order:
                    row = order[p * 8 + q] * channels + n * quarter
                    block = conv[row : row + quarter, :]
                    block = pltpu.roll(block, (start - 32 * n) % width, 1)
                    packed = jnp.where(inside[q], block, packed)
            parts.append(packed)
        packs.append(jnp.concatenate(parts, axis=0))

    def put(p, change):
        for q, start in enumerate(starts):
            near = pltpu.roll(change, (width - 6 - start) % width, 1)
            strips[pl.ds(p * 8 + q, channels, stride=24), :] = near

    blocks = [functools.partial(lambda block: block, packed) for packed in packs]
    mlp(rows_ref, expand_ref, reduce_ref, 0, blocks, normed, inner, put)


def second_layer(
    field_ref,
    mask_ref,
    halo_ref,
    halo_mask_ref,
    core_ref,
    cross_ref,
    wrap_ref,
    own_ref,
    strips,
    update_ref,
    matrix_ref,
    rows_ref,
    expand_ref,
    reduce_ref,
    out_ref,
    main_ref,
    conv,
    normed,
    inner,
):
    channels, rows, width = out_ref.shape
    groups = channels // 8
    lane32 = lanes((32, width))
    lane24 = lanes((24, width))
    first_six = lane32 % 16 < HALO

    def beside_of(received, slot):
        beside = pltpu.roll(received, (width - HALO - 16 * slot) % width, 1)
        return beside.astype(jnp.float32)[0:24, :]

    def received(g):
        east, west = neighbours(core_ref, (cross_ref, wrap_ref, own_ref), g, groups)
        return jnp.where(first_six, west, east)

    main_mask = jnp.concatenate(
        [mask_ref[...].astype(jnp.float32), halo_mask_ref[0:8, :]], axis=0
    )
    side_mask = beside_of(received(groups), 0)
    low = lane24 < 3
    high = lane24 >= width - 3
    blank = jnp.zeros((8, width), jnp.float32)
    ones = jnp.ones((32, width), jnp.bfloat16)
    away = {s: lane32 < s if s > 0 else lane32 >= width + s for s in range(-3, 4) if s}
    for g in range(groups):
        both = received(g)
        for j in range(8):
            c = channel_of(channels, g, j)
            near = strips[c * 24 : c * 24 + 24, :]
            far = pltpu.roll(near, width - 2 * HALO, 1)
            change = update_ref[c * 24 : c * 24 + 24, :]
            change = jnp.where(low, near, jnp.where(high, far, change))
            old = jnp.concatenate([field_ref[c], halo_ref[c]], axis=0).astype(jnp.float32)
            main = main_mask * (old[:24, :] + change)
            main = jnp.concatenate([main, blank], axis=0).astype(jnp.bfloat16)
            main_ref[c] = main[:rows, :]
            change = jnp.where(high, near, far)
            beside = side_mask * (beside_of(both, j) + change)
            beside = jnp.concatenate([beside, blank], axis=0).astype(jnp.bfloat16)
            stack = []
            for s in range(-3, 4):
                moved = main
                if s:
                    moved = pltpu.roll(jnp.where(away[s], beside, main), (-s) % width, 1)
                stack.append(moved)
            stack = jnp.concatenate(stack + [ones], axis=0)
            matrix = matrix_ref[c * 16 : c * 16 + 16, :]
            result = jnp.dot(matrix, stack, preferred_element_type=jnp.float32)
            conv[pl.ds(c, 16, stride=channels), :] = result

    mask = mask_ref[...].astype(jnp.float32)
    changes = []

    def put(n, change):
        changes.append(change)
        if n < rows - 1:
            return
        for c in range(0, channels, 8):
            parts = []
            for half in range(0, rows, 8):
                part = [changes[i][c : c + 8, :] for i in range(half, half + 8)]
                parts.append(jnp.swapaxes(jnp.stack(part, axis=0), 0, 1))
            change = jnp.concatenate(parts, axis=1)
            old = main_ref[c : c + 8].astype(jnp.float32)
            out_ref[c : c + 8] = (mask[None] * (old + change)).astype(jnp.bfloat16)

    blocks = [conv_row(conv, channels, i) for i in range(rows)]
    mlp(rows_ref, expand_ref, reduce_ref, 1, blocks, normed, inner, put)


def per_device(
    nlat,
    nlon,
    field,
    land_mask,
    depth_kernel,
    depth_bias,
    norm_gain,
    norm_bias,
    w_expand,
    b_expand,
    w_reduce,
    b_reduce,
):
    channels, rows, width = field.shape
    layers, hidden = b_expand.shape
    bf16, f32 = jnp.bfloat16, jnp.float32
    edge = HALO * channels + 16

    def buffers(count):
        return [
            pltpu.VMEM((channels + 16, count * width), bf16),
            pltpu.VMEM((hidden, count * width), bf16),
        ]

    def pack(upper_if_even, after):
        return pl.pallas_call(
            functools.partial(pack_rows, upper_if_even),
            out_shape=jax.ShapeDtypeStruct((edge, width), bf16),
            in_specs=vmem(2) + [pl.BlockSpec(memory_space=pl.ANY)],
            out_specs=pl.BlockSpec(memory_space=pltpu.VMEM),
            scratch_shapes=[
                pltpu.VMEM((channels * rows, width), f32),
                pltpu.VMEM((rows, width), f32),
            ],
            compiler_params=params(),
            cost_estimate=cost(4e9),
        )(field, land_mask, after)

    begun = pl.pallas_call(
        first_step,
        out_shape=jax.ShapeDtypeStruct((8, 128), f32),
        out_specs=pl.BlockSpec(memory_space=pltpu.VMEM),
        compiler_params=params(),
        cost_estimate=cost(4e9),
    )()
    first = pack(True, begun)
    second_sent = pack(False, first)

    alone = nlat == 2

    def at(d, lat):
        return d * nlat + lat

    pairs = []
    for d in range(nlon):
        for low in range(1, nlat - 1, 2):
            pairs += [(at(d, low), at(d, low + 1)), (at(d, low + 1), at(d, low))]
        pairs.append((at(d, nlat - 1), at(nlon - 1 - d, nlat - 1)))
    second = lax.ppermute(second_sent, ("lon", "lat"), pairs)
    pairs = []
    for low in range(0, nlat - 1, 2):
        pairs += [(low, low + 1), (low + 1, low)]
    first = lax.ppermute(first, "lat", pairs)

    kernel = depth_kernel.transpose(2, 3, 0, 1).reshape(49, layers, channels)
    matrix_one, matrix_two, by_channel, expand = pl.pallas_call(
        weights,
        out_shape=[
            jax.ShapeDtypeStruct((channels * 24, 256), bf16),
            jax.ShapeDtypeStruct((channels * 16, 256), bf16),
            jax.ShapeDtypeStruct((layers, 3, channels, 128), f32),
            jax.ShapeDtypeStruct((layers, hidden, channels + 16), bf16),
        ],
        in_specs=vmem(7),
        out_specs=vmem(4),
        scratch_shapes=[
            pltpu.VMEM((channels * 24, 128), f32),
            pltpu.VMEM((channels * 24, 128), f32),
            pltpu.VMEM((128, 128), f32),
            pltpu.VMEM((128, hidden), f32),
        ],
        compiler_params=params(),
        cost_estimate=cost(2e9),
    )(
        kernel,
        depth_bias,
        norm_gain,
        norm_bias,
        w_expand.transpose(0, 2, 1),
        b_expand,
        b_reduce,
    )
    update = pl.pallas_call(
        inner_rows,
        out_shape=jax.ShapeDtypeStruct((channels * 24, width), f32),
        in_specs=vmem(5),
        out_specs=pl.BlockSpec(memory_space=pltpu.VMEM),
        scratch_shapes=[pltpu.VMEM((channels * 16, width), f32)] + buffers(len(INNER)),
        compiler_params=params(),
        cost_estimate=cost(4e9),
    )(field, matrix_one, by_channel, expand, w_reduce)

    groups = channels // 8 + 1
    sent_rows = (channels // 16 + 1) * 32
    near_halo, near_mask, own_ends, wrap = pl.pallas_call(
        near_rows,
        out_shape=[
            jax.ShapeDtypeStruct((channels, 16, width), bf16),
            jax.ShapeDtypeStruct((16, width), f32),
            jax.ShapeDtypeStruct((groups * 16, width), bf16),
            jax.ShapeDtypeStruct((sent_rows, width), bf16),
        ],
        in_specs=vmem(3),
        out_specs=vmem(4),
        scratch_shapes=[
            pltpu.VMEM((channels * 16, width), f32),
            pltpu.VMEM((groups * 32, width), bf16),
        ],
        compiler_params=params(),
        cost_estimate=cost(1e9),
    )(field, land_mask, first)
    if alone:
        pairs = []
        for lat in range(nlat):
            pairs += [(lat, at(nlon - 1, lat)), (at(nlon - 1, lat), lat)]
        wrap = lax.ppermute(wrap, ("lon", "lat"), pairs)
    else:
        wrap = jnp.zeros_like(wrap)
    halo, halo_mask, ends, cross, own = pl.pallas_call(
        functools.partial(far_rows, alone),
        out_shape=[
            jax.ShapeDtypeStruct((channels, 16, width), bf16),
            jax.ShapeDtypeStruct((16, width), f32),
            jax.ShapeDtypeStruct((groups * 32, width), bf16),
            jax.ShapeDtypeStruct((sent_rows, width), bf16),
            jax.ShapeDtypeStruct((sent_rows, width), bf16),
        ],
        in_specs=vmem(5) + [pl.BlockSpec(memory_space=pl.ANY)],
        out_specs=vmem(5),
        scratch_shapes=[
            pltpu.VMEM((channels * 16, width), f32),
            pltpu.VMEM((16, width), f32),
        ],
        compiler_params=params(),
    )(second, second_sent, near_halo, near_mask, own_ends, update)
    core = pl.pallas_call(
        core_columns,
        out_shape=jax.ShapeDtypeStruct((sent_rows, width), bf16),
        in_specs=vmem(1) + [pl.BlockSpec(memory_space=pl.ANY)],
        out_specs=pl.BlockSpec(memory_space=pltpu.VMEM),
        compiler_params=params(),
    )(ends, cross)

    pairs = []
    for low in range(0, nlon, 2):
        pairs += [(low, low + 1), (low + 1, low)]
    core = lax.ppermute(core, "lon", pairs)
    pairs = []
    for low in range(1, nlon, 2):
        after = (low + 1) % nlon
        if after or not alone:
            pairs += [(low, after), (after, low)]
    cross = lax.ppermute(cross, "lon", pairs)

    update = pl.pallas_call(
        edge_rows,
        out_shape=jax.ShapeDtypeStruct((channels * 24, width), f32),
        in_specs=vmem(7),
        out_specs=pl.BlockSpec(memory_space=pltpu.VMEM),
        scratch_shapes=[pltpu.VMEM((channels * 16, width), f32)] + buffers(len(EDGE)),
        input_output_aliases={6: 0},
        compiler_params=params(),
        cost_estimate=cost(4e9),
    )(field, halo, matrix_one, by_channel, expand, w_reduce, update)

    strips = pl.pallas_call(
        edge_columns,
        out_shape=jax.ShapeDtypeStruct((channels * 24, width), f32),
        in_specs=vmem(9),
        out_specs=pl.BlockSpec(memory_space=pltpu.VMEM),
        scratch_shapes=[pltpu.VMEM((channels * 24, width), f32)] + buffers(3),
        compiler_params=params(),
    )(core, cross, wrap, own, ends, matrix_one, by_channel, expand, w_reduce)

    return pl.pallas_call(
        second_layer,
        out_shape=jax.ShapeDtypeStruct((channels, rows, width), bf16),
        in_specs=vmem(14),
        out_specs=pl.BlockSpec(memory_space=pltpu.VMEM),
        scratch_shapes=[
            pltpu.VMEM((channels, rows, width), bf16),
            pltpu.VMEM((channels * 16, width), f32),
        ]
        + buffers(rows),
        compiler_params=params(),
    )(
        field,
        land_mask,
        halo,
        halo_mask,
        core,
        cross,
        wrap,
        own,
        strips,
        update,
        matrix_two,
        by_channel,
        expand,
        w_reduce,
    )


def solution(mesh):
    placed = (P(None, "lat", "lon"), P("lat", "lon"), P(), P(), P(), P(), P(), P(), P(), P())
    return jax.shard_map(
        functools.partial(per_device, mesh.shape["lat"], mesh.shape["lon"]),
        mesh=mesh,
        in_specs=placed,
        out_specs=P(None, "lat", "lon"),
        check_vma=False,
    )
```

```python
import functools

import jax
import jax.numpy as jnp
from jax import lax
from jax.experimental import pallas as pl
from jax.experimental.pallas import tpu as pltpu
from jax.sharding import PartitionSpec as P


HALO = 6
VMEM_LIMIT = 20 * 1024 * 1024


def params():
    return pltpu.CompilerParams(vmem_limit_bytes=VMEM_LIMIT)


def cost(flops):
    return pl.CostEstimate(flops=int(flops), bytes_accessed=1 << 20, transcendentals=0)


def vmem(count):
    return [pl.BlockSpec(memory_space=pltpu.VMEM)] * count


def lanes(shape):
    return lax.broadcasted_iota(jnp.int32, shape, len(shape) - 1)


def first_step(out_ref):
    out_ref[...] = jnp.zeros_like(out_ref)


def pack_rows(upper_if_even, field_ref, mask_ref, after_ref, out_ref, wide, wide_mask):
    del after_ref
    kept = 1.0 if upper_if_even else (lax.axis_index("lat") > 0).astype(jnp.float32)
    channels, rows, width = field_ref.shape
    even = lax.rem(lax.axis_index("lat"), 2) == 0
    take_upper = even if upper_if_even else jnp.logical_not(even)
    wide[...] = field_ref[...].astype(jnp.float32).reshape(channels * rows, width)
    wide_mask[...] = mask_ref[...].astype(jnp.float32)
    for k in range(HALO):
        lower = wide[pl.ds(k, channels, stride=rows), :]
        upper = wide[pl.ds(rows - HALO + k, channels, stride=rows), :]
        at = pl.ds(k * channels, channels)
        out_ref[at, :] = (kept * jnp.where(take_upper, upper, lower)).astype(jnp.bfloat16)
    pad = jnp.zeros((16 - HALO, width), jnp.float32)
    lower = jnp.concatenate([wide_mask[0:HALO, :], pad], axis=0)
    upper = jnp.concatenate([wide_mask[rows - HALO : rows, :], pad], axis=0)
    at = pl.ds(HALO * channels, 16)
    out_ref[at, :] = (kept * jnp.where(take_upper, upper, lower)).astype(jnp.bfloat16)


def north_place(row):
    return jnp.where(row < 3, 4 + row, 9 + row)


def south_place(k):
    return k - 3 if k >= 3 else 8 + k


def place_rows(received_ref, is_north, turned, wide, mask_rows, channels):
    width = received_ref.shape[1]
    wide[...] = jnp.zeros_like(wide)
    mask_rows[...] = jnp.zeros_like(mask_rows)
    turn = None
    if turned is not None:
        sub = lax.broadcasted_iota(jnp.int32, (width, width), 0)
        target = lanes((width, width))
        turn = sub == jnp.where(turned, width - 1 - target, target)
        turn = turn.astype(jnp.float32).astype(jnp.bfloat16)

    def rows_at(start, count):
        block = received_ref[start : start + count, :]
        if turn is None:
            return block.astype(jnp.float32)
        return jnp.dot(block, turn, preferred_element_type=jnp.float32)

    masks = rows_at(HALO * channels, 16)
    for k in range(HALO):
        row = k if turned is None else jnp.where(turned, HALO - 1 - k, k)
        place = jnp.where(is_north, north_place(row), south_place(k))
        wide[pl.ds(place, channels, stride=16), :] = rows_at(k * channels, channels)
        mask_rows[pl.ds(place, 1), :] = masks[k : k + 1, :]


def pack_ends(blocks):
    rows, width = blocks[0].shape
    slot = lanes((rows, width)) // 16
    packed = jnp.zeros((rows, width), jnp.bfloat16)
    for j, block in enumerate(blocks):
        packed = jnp.where(slot == j, pltpu.roll(block, 16 * j + HALO, 1), packed)
    return packed


def channel_of(channels, group, slot):
    return slot // 2 * (channels // 4) + group * 2 + slot % 2


def over_wrap():
    lon = lax.axis_index("lon")
    return (lon == 0) | (lon == lax.axis_size("lon") - 1)


def near_rows(
    field_ref, mask_ref, first_ref, halo_ref, mask_rows, ends_ref, wrap_ref, wide, all_ends
):
    channels, rows, width = field_ref.shape
    even = lax.rem(lax.axis_index("lat"), 2) == 0
    place_rows(first_ref, even, None, wide, mask_rows, channels)
    halo_ref[...] = wide[...].astype(jnp.bfloat16).reshape(channels, 16, width)
    groups = channels // 8
    for g in range(groups):
        blocks = [field_ref[channel_of(channels, g, j)] for j in range(8)]
        ends_ref[g * 16 : g * 16 + 16, :] = pack_ends(blocks)
    mask = mask_ref[...].astype(jnp.float32).astype(jnp.bfloat16)
    ends_ref[groups * 16 :, :] = pack_ends([mask])
    wrap_ref[...] = jnp.zeros_like(wrap_ref)

    @pl.when(over_wrap())
    def _():
        join_ends(ends_ref, halo_ref, mask_rows, all_ends)
        pack_side(all_ends, wrap_ref, lax.rem(lax.axis_index("lon"), 2) == 1)


def join_ends(own_ends_ref, halo_ref, mask_rows, ends_ref):
    channels = halo_ref.shape[0]
    groups = channels // 8
    for g in range(groups + 1):
        if g < groups:
            blocks = [halo_ref[channel_of(channels, g, j)] for j in range(8)]
        else:
            blocks = [mask_rows[...].astype(jnp.bfloat16)]
        own = jnp.zeros((16, halo_ref.shape[2]), jnp.bfloat16)
        if own_ends_ref is not None:
            own = own_ends_ref[g * 16 : g * 16 + 16, :]
        ends_ref[g * 32 : g * 32 + 16, :] = own
        ends_ref[g * 32 + 16 : g * 32 + 32, :] = pack_ends(blocks)


def pack_side(ends_ref, out_ref, to_east):
    width = ends_ref.shape[1]
    groups = ends_ref.shape[0] // 32 - 1
    lower = lanes((32, width)) % 16 < 8
    for m in range(groups // 2 + 1):
        n = m if m < groups // 2 else groups
        one = ends_ref[n * 32 : n * 32 + 32, :]
        one = jnp.where(to_east, one, pltpu.roll(one, width - HALO, 1))
        if n < groups:
            two = ends_ref[(n + groups // 2) * 32 : (n + groups // 2) * 32 + 32, :]
            two = jnp.where(to_east, pltpu.roll(two, 8, 1), pltpu.roll(two, 8 - HALO, 1))
            one = jnp.where(lower, one, two)
        out_ref[m * 32 : m * 32 + 32, :] = one


def far_rows(
    mirrored,
    second_ref,
    sent_ref,
    near_halo_ref,
    near_mask_ref,
    own_ends_ref,
    after_ref,
    halo_ref,
    halo_mask_ref,
    ends_ref,
    cross_ref,
    own_ref,
    wide,
    mask_rows,
):
    del after_ref
    channels, _, width = halo_ref.shape
    lat = lax.axis_index("lat")
    odd = lax.rem(lat, 2) == 1
    lon_odd = lax.rem(lax.axis_index("lon"), 2) == 1
    folded = lat == lax.axis_size("lat") - 1
    own_ref[...] = jnp.zeros_like(own_ref)
    if mirrored:

        @pl.when(folded & over_wrap())
        def _():
            place_rows(sent_ref, odd, folded, wide, mask_rows, channels)
            halo_ref[...] = wide[...].astype(jnp.bfloat16).reshape(channels, 16, width)
            join_ends(None, halo_ref, mask_rows, ends_ref)
            pack_side(ends_ref, own_ref, jnp.logical_not(lon_odd))

    place_rows(second_ref, odd, folded, wide, mask_rows, channels)
    far = wide[...].astype(jnp.bfloat16).reshape(channels, 16, width)
    halo_ref[...] = near_halo_ref[...] + far
    halo_mask_ref[...] = near_mask_ref[...] + mask_rows[...]
    join_ends(own_ends_ref, halo_ref, halo_mask_ref, ends_ref)
    pack_side(ends_ref, cross_ref, lon_odd)
    if mirrored:

        @pl.when(over_wrap())
        def _():
            cross_ref[...] = jnp.zeros_like(cross_ref)


def core_columns(ends_ref, after_ref, core_ref):
    del after_ref
    pack_side(ends_ref, core_ref, lax.rem(lax.axis_index("lon"), 2) == 0)


def in_row(place, first_layer):
    none = jnp.full_like(place, 1000)
    row = jnp.where(place < 16, place, none)
    row = jnp.where((place >= 16) & (place < 19), place - 19, row)
    row = jnp.where((place >= 20) & (place < 23), place - 4, row)
    if first_layer:
        row = jnp.where((place >= 24) & (place < 27), place - 30, row)
        row = jnp.where((place >= 28) & (place < 31), place - 9, row)
    return row


EDGE = (-3, -2, -1, 16, 17, 18, 0, 1, 2, 13, 14, 15)
INNER = (3, 4, 5, 6, 7, 8, 9, 10, 11, 12)


def place_of(row):
    if row < 0:
        return row + 19
    return row if row < 16 else row + 4


def conv_matrices(table, out_ref, left, right, row, rows_out):
    channels, taps = table.shape
    count = len(rows_out)
    folded = lax.axis_index("lat") == lax.axis_size("lat") - 1
    k = lanes((1, 256))
    shift = k // 32
    place = k - shift * 32
    tap = lax.broadcasted_iota(jnp.int32, (taps, 256), 0)
    row = row(place)
    for i, here in enumerate(rows_out):
        if here is None:
            wanted = jnp.full_like(k, -1)
        else:
            a = row - here + 3
            inside = (a >= 0) & (a <= 6) & (shift < 7)
            wanted = a * 7 + shift
            if here > 15:
                wanted = jnp.where(folded, 48 - wanted, wanted)
            wanted = jnp.where(inside, wanted, -1)
            wanted = jnp.where((shift == 7) & (place < 3), 49 + place, wanted)
        picks = (tap == wanted).astype(jnp.float32).astype(jnp.bfloat16)
        matrix = jnp.dot(table, picks, preferred_element_type=jnp.float32)
        left[pl.ds(i, channels, stride=count), :] = matrix[:, :128]
        right[pl.ds(i, channels, stride=count), :] = matrix[:, 128:]
    size = channels * count
    out_ref[:, :128] = left[:size, :].astype(jnp.bfloat16)
    out_ref[:, 128:] = right[:size, :].astype(jnp.bfloat16)


def split_bias(bias):
    high = bias.astype(jnp.bfloat16).astype(jnp.float32)
    rest = bias - high
    mid = rest.astype(jnp.bfloat16).astype(jnp.float32)
    return high, mid, rest - mid


def weights(
    kernel_ref,
    bias_ref,
    gain_ref,
    norm_bias_ref,
    expand_ref,
    expand_bias_ref,
    reduce_bias_ref,
    one_ref,
    two_ref,
    rows_ref,
    expand_out_ref,
    left,
    right,
    turn,
    tall,
):
    taps, layers, channels = kernel_ref.shape
    hidden = expand_ref.shape[2]
    turn[...] = jnp.zeros_like(turn)
    tall[...] = jnp.zeros_like(tall)
    for layer in range(layers):
        for tap in range(taps):
            turn[tap : tap + 1, :channels] = kernel_ref[tap, layer : layer + 1, :]
        parts = split_bias(bias_ref[layer : layer + 1, :])
        for n, part in enumerate(parts):
            turn[taps + n : taps + n + 1, :channels] = part
        table = turn[...].T[:channels, :64].astype(jnp.bfloat16)
        if layer == 0:
            every = EDGE + INNER + (None,) * 2
            row = functools.partial(in_row, first_layer=True)
            conv_matrices(table, one_ref, left, right, row, every)
        else:
            row = functools.partial(in_row, first_layer=False)
            conv_matrices(table, two_ref, left, right, row, tuple(range(16)))
    for layer in range(layers):
        for n, ref in enumerate((gain_ref, norm_bias_ref, reduce_bias_ref)):
            turn[:, :channels] = jnp.broadcast_to(ref[layer : layer + 1, :], (128, channels))
            rows_ref[layer, n] = turn[...].T[:channels, :]
        tall[:channels, :] = expand_ref[layer].astype(jnp.float32) * 0.5
        parts = split_bias(expand_bias_ref[layer : layer + 1, :] * 0.5)
        for n, part in enumerate(parts):
            tall[channels + n : channels + n + 1, :] = part
        for n in range(hidden // 128):
            piece = tall[:, n * 128 : (n + 1) * 128].T
            at = pl.ds(n * 128, 128)
            expand_out_ref[layer, at, :] = piece[:, : channels + 16].astype(jnp.bfloat16)


ERF = (7.97869712e-01, 3.63922860e-02, -8.78263977e-05, -3.66934787e-05, 1.42500782e-06)


def gelu_of_double(half):
    square = half * half
    total = jnp.full_like(half, 2.0 * 4.0 ** (len(ERF) - 1) * ERF[-1])
    for power in range(len(ERF) - 2, -1, -1):
        total = total * square + jnp.full_like(half, 2.0 * 4.0**power * ERF[power])
    return half * jnp.tanh(half * total) + half


def norm(rows_ref, layer, cells):
    average = jnp.mean(cells, axis=0, keepdims=True)
    centered = cells - average
    variance = jnp.mean(centered * centered, axis=0, keepdims=True)
    scaled = centered * lax.rsqrt(variance + 1e-06)
    return (scaled * rows_ref[layer, 0] + rows_ref[layer, 1]).astype(jnp.bfloat16)


def mlp(rows_ref, expand_ref, reduce_ref, layer, blocks, normed_ref, inner_ref, put):
    count = len(blocks)
    channels, width = rows_ref.shape[2:]
    hidden = inner_ref.shape[0]
    wide = count * width
    normed_ref[channels:, :wide] = jnp.ones((16, wide), jnp.bfloat16)
    for n, block in enumerate(blocks):
        at = slice(n * width, (n + 1) * width)
        normed_ref[:channels, at] = norm(rows_ref, layer, block())
    tiles = [slice(n, min(n + 2 * width, wide)) for n in range(0, wide, 2 * width)]
    for at in tiles:
        normed = normed_ref[:, at]
        for part in range(0, hidden, 128):
            matrix = expand_ref[layer, part : part + 128, :]
            half = jnp.dot(matrix, normed, preferred_element_type=jnp.float32)
            for k in range(0, 128, 16):
                values = gelu_of_double(half[k : k + 16, :].astype(jnp.bfloat16))
                inner_ref[part + k : part + k + 16, at] = values
    extra = rows_ref[layer, 2]
    for t, at in enumerate(tiles):
        change = jnp.dot(reduce_ref[layer], inner_ref[:, at], preferred_element_type=jnp.float32)
        for n in range((at.stop - at.start) // width):
            put(t * 2 + n, change[:, n * width : (n + 1) * width] + extra)


def columns_stack(block, ones):
    width = block.shape[1]
    stack = [block if s == 0 else pltpu.roll(block, (-s) % width, 1) for s in range(-3, 4)]
    return jnp.concatenate(stack + [ones], axis=0)


def conv_rows(matrix_ref, stack_of, conv, channels, stride, first, count):
    ones = jnp.ones((matrix_ref.shape[1] // 8, 128), jnp.bfloat16)

    def step(c, carry):
        matrix = matrix_ref[pl.ds(pl.multiple_of(c * stride + first, 8), count), :]
        result = jnp.dot(matrix, stack_of(c, ones), preferred_element_type=jnp.float32)
        conv[pl.ds(c, count, stride=channels), :] = result
        return carry

    lax.fori_loop(0, channels, step, 0, unroll=channels)


def conv_row(conv, channels, i):
    return lambda: conv[i * channels : (i + 1) * channels, :]


def inner_rows(
    field_ref, matrix_ref, rows_ref, expand_ref, reduce_ref, update_ref, conv, normed, inner
):
    channels, rows, width = field_ref.shape
    none = jnp.zeros((16, width), jnp.bfloat16)

    def stack_of(c, ones):
        return columns_stack(jnp.concatenate([field_ref[c], none], axis=0), ones)

    conv_rows(matrix_ref, stack_of, conv, channels, 24, 8, 16)

    def put(n, change):
        update_ref[pl.ds(INNER[n], channels, stride=24), :] = change

    blocks = [conv_row(conv, channels, i + len(EDGE) - 8) for i in range(len(INNER))]
    mlp(rows_ref, expand_ref, reduce_ref, 0, blocks, normed, inner, put)


def edge_rows(
    field_ref,
    halo_ref,
    matrix_ref,
    rows_ref,
    expand_ref,
    reduce_ref,
    old_ref,
    update_ref,
    conv,
    normed,
    inner,
):
    del old_ref
    channels, _, width = field_ref.shape

    def stack_of(c, ones):
        return columns_stack(jnp.concatenate([field_ref[c], halo_ref[c]], axis=0), ones)

    conv_rows(matrix_ref, stack_of, conv, channels, 24, 0, 16)
    for empty in (19, 23):
        update_ref[pl.ds(empty, channels, stride=24), :] = jnp.zeros((channels, width), jnp.float32)

    def put(n, change):
        update_ref[pl.ds(place_of(EDGE[n]), channels, stride=24), :] = change

    blocks = [conv_row(conv, channels, i) for i in range(len(EDGE))]
    mlp(rows_ref, expand_ref, reduce_ref, 0, blocks, normed, inner, put)


def neighbours(core_ref, cross_refs, group, groups):
    width = core_ref.shape[1]
    half = groups // 2
    m, upper = (half, 0) if group == groups else (group % half, group // half)
    core = core_ref[m * 32 : m * 32 + 32, :]
    cross = sum(ref[m * 32 : m * 32 + 32, :] for ref in cross_refs)
    lon_even = lax.rem(lax.axis_index("lon"), 2) == 0
    east = jnp.where(lon_even, core, cross)
    west = jnp.where(lon_even, cross, core)
    east = pltpu.roll(east, (HALO - 8 * upper) % width, 1)
    return east, pltpu.roll(west, width - 8, 1) if upper else west


def edge_columns(
    core_ref,
    cross_ref,
    wrap_ref,
    own_ref,
    ends_ref,
    matrix_ref,
    rows_ref,
    expand_ref,
    reduce_ref,
    strips,
    conv,
    normed,
    inner,
):
    channels, width = rows_ref.shape[2:]
    quarter = channels // 4
    groups = channels // 8
    lane32 = lanes((32, width))
    first_six = lane32 % 16 < HALO
    first_twelve = lane32 % 32 < 2 * HALO
    ones = jnp.ones((32, width), jnp.bfloat16)
    for g in range(groups):
        at = slice(g * 32, g * 32 + 32)
        east, west = neighbours(core_ref, (cross_ref, wrap_ref, own_ref), g, groups)
        own = ends_ref[at, :]
        at_west = jnp.where(first_six, west, own)
        at_east = jnp.where(first_six, own, east)
        for t in range(2):
            left = pltpu.roll(at_west, width - 16, 1) if t else at_west
            right = pltpu.roll(at_east, (2 * HALO - 16 * t) % width, 1)
            block = jnp.where(first_twelve, left, right)
            some = [channel_of(channels, g, 2 * n + t) for n in range(4)]
            matrix = jnp.concatenate(
                [matrix_ref[c * 24 : c * 24 + 24, :] for c in some], axis=0
            )
            stack = columns_stack(block, ones)
            result = jnp.dot(matrix, stack, preferred_element_type=jnp.float32)
            for n, c in enumerate(some):
                conv[pl.ds(c, 24, stride=channels), :] = result[n * 24 : n * 24 + 24, :]

    order = {place_of(row): i for i, row in enumerate(EDGE + INNER)}
    lane = lanes((quarter, width))
    starts = [32 * (q // 2) + 6 * (q % 2) for q in range(8)]
    inside = [
        ((lane >= s + 3) & (lane < s + 9)) | ((lane >= s + 15) & (lane < s + 21)) for s in starts
    ]
    packs = []
    for p in range(3):
        parts = []
        for n in range(4):
            packed = jnp.zeros((quarter, width), jnp.float32)
            for q, start in enumerate(starts):
                if p * 8 + q in order:
                    row = order[p * 8 + q] * channels + n * quarter
                    block = conv[row : row + quarter, :]
                    block = pltpu.roll(block, (start - 32 * n) % width, 1)
                    packed = jnp.where(inside[q], block, packed)
            parts.append(packed)
        packs.append(jnp.concatenate(parts, axis=0))

    def put(p, change):
        for q, start in enumerate(starts):
            near = pltpu.roll(change, (width - 6 - start) % width, 1)
            strips[pl.ds(p * 8 + q, channels, stride=24), :] = near

    blocks = [functools.partial(lambda block: block, packed) for packed in packs]
    mlp(rows_ref, expand_ref, reduce_ref, 0, blocks, normed, inner, put)


def second_layer(
    field_ref,
    mask_ref,
    halo_ref,
    halo_mask_ref,
    core_ref,
    cross_ref,
    wrap_ref,
    own_ref,
    strips,
    update_ref,
    matrix_ref,
    rows_ref,
    expand_ref,
    reduce_ref,
    out_ref,
    main_ref,
    conv,
    normed,
    inner,
):
    channels, rows, width = out_ref.shape
    groups = channels // 8
    lane32 = lanes((32, width))
    lane24 = lanes((24, width))
    first_six = lane32 % 16 < HALO

    def beside_of(received, slot):
        beside = pltpu.roll(received, (width - HALO - 16 * slot) % width, 1)
        return beside.astype(jnp.float32)[0:24, :]

    def received(g):
        east, west = neighbours(core_ref, (cross_ref, wrap_ref, own_ref), g, groups)
        return jnp.where(first_six, west, east)

    main_mask = jnp.concatenate(
        [mask_ref[...].astype(jnp.float32), halo_mask_ref[0:8, :]], axis=0
    )
    side_mask = beside_of(received(groups), 0)
    low = lane24 < 3
    high = lane24 >= width - 3
    blank = jnp.zeros((8, width), jnp.float32)
    ones = jnp.ones((32, width), jnp.bfloat16)
    lane16 = lanes((16, width))
    away = {s: lane16 < s if s > 0 else lane16 >= width + s for s in range(-3, 4) if s}

    def halves(block):
        low_rows = block[:16, :].astype(jnp.bfloat16)
        return low_rows, jnp.concatenate([block[16:, :], blank], axis=0).astype(jnp.bfloat16)

    for g in range(groups):
        both = received(g)
        for j in range(8):
            c = channel_of(channels, g, j)
            near = strips[c * 24 : c * 24 + 24, :]
            far = pltpu.roll(near, width - 2 * HALO, 1)
            change = update_ref[c * 24 : c * 24 + 24, :]
            change = jnp.where(low, near, jnp.where(high, far, change))
            own = field_ref[c].astype(jnp.float32)
            halo = halo_ref[c].astype(jnp.float32)[:8, :]
            main = halves(main_mask * (jnp.concatenate([own, halo], axis=0) + change))
            main_ref[c] = main[0]
            change = jnp.where(high, near, far)
            beside = halves(side_mask * (beside_of(both, j) + change))
            stack = []
            for s in range(-3, 4):
                for part, other in zip(main, beside):
                    if s:
                        part = pltpu.roll(jnp.where(away[s], other, part), (-s) % width, 1)
                    stack.append(part)
            stack = jnp.concatenate(stack + [ones], axis=0)
            matrix = matrix_ref[c * 16 : c * 16 + 16, :]
            result = jnp.dot(matrix, stack, preferred_element_type=jnp.float32)
            conv[pl.ds(c, 16, stride=channels), :] = result

    mask = mask_ref[...].astype(jnp.float32)
    changes = []

    def put(n, change):
        changes.append(change)
        if n < rows - 1:
            return
        for c in range(0, channels, 8):
            parts = []
            for half in range(0, rows, 8):
                part = [changes[i][c : c + 8, :] for i in range(half, half + 8)]
                parts.append(jnp.swapaxes(jnp.stack(part, axis=0), 0, 1))
            change = jnp.concatenate(parts, axis=1)
            old = main_ref[c : c + 8].astype(jnp.float32)
            out_ref[c : c + 8] = (mask[None] * (old + change)).astype(jnp.bfloat16)

    blocks = [conv_row(conv, channels, i) for i in range(rows)]
    mlp(rows_ref, expand_ref, reduce_ref, 1, blocks, normed, inner, put)


def per_device(
    nlat,
    nlon,
    field,
    land_mask,
    depth_kernel,
    depth_bias,
    norm_gain,
    norm_bias,
    w_expand,
    b_expand,
    w_reduce,
    b_reduce,
):
    channels, rows, width = field.shape
    layers, hidden = b_expand.shape
    bf16, f32 = jnp.bfloat16, jnp.float32
    edge = HALO * channels + 16

    def buffers(count):
        return [
            pltpu.VMEM((channels + 16, count * width), bf16),
            pltpu.VMEM((hidden, count * width), bf16),
        ]

    def pack(upper_if_even, after):
        return pl.pallas_call(
            functools.partial(pack_rows, upper_if_even),
            out_shape=jax.ShapeDtypeStruct((edge, width), bf16),
            in_specs=vmem(2) + [pl.BlockSpec(memory_space=pl.ANY)],
            out_specs=pl.BlockSpec(memory_space=pltpu.VMEM),
            scratch_shapes=[
                pltpu.VMEM((channels * rows, width), f32),
                pltpu.VMEM((rows, width), f32),
            ],
            compiler_params=params(),
            cost_estimate=cost(4e9),
        )(field, land_mask, after)

    begun = pl.pallas_call(
        first_step,
        out_shape=jax.ShapeDtypeStruct((8, 128), f32),
        out_specs=pl.BlockSpec(memory_space=pltpu.VMEM),
        compiler_params=params(),
        cost_estimate=cost(4e9),
    )()
    first = pack(True, begun)
    second_sent = pack(False, first)

    alone = nlat == 2

    def at(d, lat):
        return d * nlat + lat

    pairs = []
    for d in range(nlon):
        for low in range(1, nlat - 1, 2):
            pairs += [(at(d, low), at(d, low + 1)), (at(d, low + 1), at(d, low))]
        pairs.append((at(d, nlat - 1), at(nlon - 1 - d, nlat - 1)))
        pairs.append((at(d, 0), at(d ^ 1, 0)))
    second = lax.ppermute(second_sent, ("lon", "lat"), pairs)
    pairs = []
    for low in range(0, nlat - 1, 2):
        pairs += [(low, low + 1), (low + 1, low)]
    first = lax.ppermute(first, "lat", pairs)

    kernel = depth_kernel.transpose(2, 3, 0, 1).reshape(49, layers, channels)
    matrix_one, matrix_two, by_channel, expand = pl.pallas_call(
        weights,
        out_shape=[
            jax.ShapeDtypeStruct((channels * 24, 256), bf16),
            jax.ShapeDtypeStruct((channels * 16, 256), bf16),
            jax.ShapeDtypeStruct((layers, 3, channels, 128), f32),
            jax.ShapeDtypeStruct((layers, hidden, channels + 16), bf16),
        ],
        in_specs=vmem(7),
        out_specs=vmem(4),
        scratch_shapes=[
            pltpu.VMEM((channels * 24, 128), f32),
            pltpu.VMEM((channels * 24, 128), f32),
            pltpu.VMEM((128, 128), f32),
            pltpu.VMEM((128, hidden), f32),
        ],
        compiler_params=params(),
        cost_estimate=cost(2e9),
    )(
        kernel,
        depth_bias,
        norm_gain,
        norm_bias,
        w_expand.transpose(0, 2, 1),
        b_expand,
        b_reduce,
    )
    update = pl.pallas_call(
        inner_rows,
        out_shape=jax.ShapeDtypeStruct((channels * 24, width), f32),
        in_specs=vmem(5),
        out_specs=pl.BlockSpec(memory_space=pltpu.VMEM),
        scratch_shapes=[pltpu.VMEM((channels * 16, width), f32)] + buffers(len(INNER)),
        compiler_params=params(),
        cost_estimate=cost(4e9),
    )(field, matrix_one, by_channel, expand, w_reduce)

    groups = channels // 8 + 1
    sent_rows = (channels // 16 + 1) * 32
    near_halo, near_mask, own_ends, wrap = pl.pallas_call(
        near_rows,
        out_shape=[
            jax.ShapeDtypeStruct((channels, 16, width), bf16),
            jax.ShapeDtypeStruct((16, width), f32),
            jax.ShapeDtypeStruct((groups * 16, width), bf16),
            jax.ShapeDtypeStruct((sent_rows, width), bf16),
        ],
        in_specs=vmem(3),
        out_specs=vmem(4),
        scratch_shapes=[
            pltpu.VMEM((channels * 16, width), f32),
            pltpu.VMEM((groups * 32, width), bf16),
        ],
        compiler_params=params(),
        cost_estimate=cost(1e9),
    )(field, land_mask, first)
    if alone:
        pairs = []
        for lat in range(nlat):
            pairs += [(lat, at(nlon - 1, lat)), (at(nlon - 1, lat), lat)]
            pairs += [(at(d, lat), at(d, 1 - lat)) for d in range(1, nlon - 1)]
        wrap = lax.ppermute(wrap, ("lon", "lat"), pairs)
    else:
        wrap = jnp.zeros_like(wrap)
    halo, halo_mask, ends, cross, own = pl.pallas_call(
        functools.partial(far_rows, alone),
        out_shape=[
            jax.ShapeDtypeStruct((channels, 16, width), bf16),
            jax.ShapeDtypeStruct((16, width), f32),
            jax.ShapeDtypeStruct((groups * 32, width), bf16),
            jax.ShapeDtypeStruct((sent_rows, width), bf16),
            jax.ShapeDtypeStruct((sent_rows, width), bf16),
        ],
        in_specs=vmem(5) + [pl.BlockSpec(memory_space=pl.ANY)],
        out_specs=vmem(5),
        scratch_shapes=[
            pltpu.VMEM((channels * 16, width), f32),
            pltpu.VMEM((16, width), f32),
        ],
        compiler_params=params(),
    )(second, second_sent, near_halo, near_mask, own_ends, update)
    core = pl.pallas_call(
        core_columns,
        out_shape=jax.ShapeDtypeStruct((sent_rows, width), bf16),
        in_specs=vmem(1) + [pl.BlockSpec(memory_space=pl.ANY)],
        out_specs=pl.BlockSpec(memory_space=pltpu.VMEM),
        compiler_params=params(),
    )(ends, cross)

    pairs = []
    for low in range(0, nlon, 2):
        pairs += [(low, low + 1), (low + 1, low)]
    core = lax.ppermute(core, "lon", pairs)
    pairs = []
    for lat in range(nlat):
        for low in range(1, nlon, 2):
            after = (low + 1) % nlon
            if after or not alone:
                pairs += [(at(low, lat), at(after, lat)), (at(after, lat), at(low, lat))]
            else:
                pairs += [(at(low, lat), at(low, 1 - lat)), (at(after, lat), at(after, 1 - lat))]
    cross = lax.ppermute(cross, ("lon", "lat"), pairs)

    update = pl.pallas_call(
        edge_rows,
        out_shape=jax.ShapeDtypeStruct((channels * 24, width), f32),
        in_specs=vmem(7),
        out_specs=pl.BlockSpec(memory_space=pltpu.VMEM),
        scratch_shapes=[pltpu.VMEM((channels * 16, width), f32)] + buffers(len(EDGE)),
        input_output_aliases={6: 0},
        compiler_params=params(),
        cost_estimate=cost(4e9),
    )(field, halo, matrix_one, by_channel, expand, w_reduce, update)

    strips = pl.pallas_call(
        edge_columns,
        out_shape=jax.ShapeDtypeStruct((channels * 24, width), f32),
        in_specs=vmem(9),
        out_specs=pl.BlockSpec(memory_space=pltpu.VMEM),
        scratch_shapes=[pltpu.VMEM((channels * 24, width), f32)] + buffers(3),
        compiler_params=params(),
    )(core, cross, wrap, own, ends, matrix_one, by_channel, expand, w_reduce)

    return pl.pallas_call(
        second_layer,
        out_shape=jax.ShapeDtypeStruct((channels, rows, width), bf16),
        in_specs=vmem(14),
        out_specs=pl.BlockSpec(memory_space=pltpu.VMEM),
        scratch_shapes=[
            pltpu.VMEM((channels, rows, width), bf16),
            pltpu.VMEM((channels * 16, width), f32),
        ]
        + buffers(rows),
        compiler_params=params(),
    )(
        field,
        land_mask,
        halo,
        halo_mask,
        core,
        cross,
        wrap,
        own,
        strips,
        update,
        matrix_two,
        by_channel,
        expand,
        w_reduce,
    )


def solution(mesh):
    placed = (P(None, "lat", "lon"), P("lat", "lon"), P(), P(), P(), P(), P(), P(), P(), P())
    return jax.shard_map(
        functools.partial(per_device, mesh.shape["lat"], mesh.shape["lon"]),
        mesh=mesh,
        in_specs=placed,
        out_specs=P(None, "lat", "lon"),
        check_vma=False,
    )
```

```python
import functools

import jax
import jax.numpy as jnp
from jax import lax
from jax.experimental import pallas as pl
from jax.experimental.pallas import tpu as pltpu
from jax.sharding import PartitionSpec as P


HALO = 6
VMEM_LIMIT = 20 * 1024 * 1024


def pitch(channels):
    return channels + 8


def params():
    return pltpu.CompilerParams(vmem_limit_bytes=VMEM_LIMIT)


def cost(flops):
    return pl.CostEstimate(flops=int(flops), bytes_accessed=1 << 20, transcendentals=0)


def vmem(count):
    return [pl.BlockSpec(memory_space=pltpu.VMEM)] * count


def lanes(shape):
    return lax.broadcasted_iota(jnp.int32, shape, len(shape) - 1)


def first_step(out_ref):
    out_ref[...] = jnp.zeros_like(out_ref)


def pack_rows(upper_if_even, field_ref, mask_ref, after_ref, out_ref, wide, wide_mask):
    del after_ref
    kept = 1.0 if upper_if_even else (lax.axis_index("lat") > 0).astype(jnp.float32)
    channels, rows, width = field_ref.shape
    even = lax.rem(lax.axis_index("lat"), 2) == 0
    take_upper = even if upper_if_even else jnp.logical_not(even)
    wide[...] = field_ref[...].astype(jnp.float32).reshape(channels * rows, width)
    wide_mask[...] = mask_ref[...].astype(jnp.float32)
    for k in range(HALO):
        lower = wide[pl.ds(k, channels, stride=rows), :]
        upper = wide[pl.ds(rows - HALO + k, channels, stride=rows), :]
        at = pl.ds(k * channels, channels)
        out_ref[at, :] = (kept * jnp.where(take_upper, upper, lower)).astype(jnp.bfloat16)
    pad = jnp.zeros((16 - HALO, width), jnp.float32)
    lower = jnp.concatenate([wide_mask[0:HALO, :], pad], axis=0)
    upper = jnp.concatenate([wide_mask[rows - HALO : rows, :], pad], axis=0)
    at = pl.ds(HALO * channels, 16)
    out_ref[at, :] = (kept * jnp.where(take_upper, upper, lower)).astype(jnp.bfloat16)


def north_place(row):
    return jnp.where(row < 3, 4 + row, 9 + row)


def south_place(k):
    return k - 3 if k >= 3 else 8 + k


def place_rows(received_ref, is_north, turned, wide, mask_rows, channels):
    width = received_ref.shape[1]
    wide[...] = jnp.zeros_like(wide)
    mask_rows[...] = jnp.zeros_like(mask_rows)
    turn = None
    if turned is not None:
        sub = lax.broadcasted_iota(jnp.int32, (width, width), 0)
        target = lanes((width, width))
        turn = sub == jnp.where(turned, width - 1 - target, target)
        turn = turn.astype(jnp.float32).astype(jnp.bfloat16)

    def rows_at(start, count):
        block = received_ref[start : start + count, :]
        if turn is None:
            return block.astype(jnp.float32)
        return jnp.dot(block, turn, preferred_element_type=jnp.float32)

    masks = rows_at(HALO * channels, 16)
    for k in range(HALO):
        row = k if turned is None else jnp.where(turned, HALO - 1 - k, k)
        place = jnp.where(is_north, north_place(row), south_place(k))
        wide[pl.ds(place, channels, stride=16), :] = rows_at(k * channels, channels)
        mask_rows[pl.ds(place, 1), :] = masks[k : k + 1, :]


def pack_ends(blocks):
    rows, width = blocks[0].shape
    slot = lanes((rows, width)) // 16
    packed = jnp.zeros((rows, width), jnp.bfloat16)
    for j, block in enumerate(blocks):
        packed = jnp.where(slot == j, pltpu.roll(block, 16 * j + HALO, 1), packed)
    return packed


def channel_of(channels, group, slot):
    return slot // 2 * (channels // 4) + group * 2 + slot % 2


def over_wrap():
    lon = lax.axis_index("lon")
    return (lon == 0) | (lon == lax.axis_size("lon") - 1)


def near_rows(
    field_ref, mask_ref, first_ref, halo_ref, mask_rows, ends_ref, wrap_ref, wide, all_ends
):
    channels, rows, width = field_ref.shape
    even = lax.rem(lax.axis_index("lat"), 2) == 0
    place_rows(first_ref, even, None, wide, mask_rows, channels)
    halo_ref[...] = wide[...].astype(jnp.bfloat16).reshape(channels, 16, width)
    groups = channels // 8
    for g in range(groups):
        blocks = [field_ref[channel_of(channels, g, j)] for j in range(8)]
        ends_ref[g * 16 : g * 16 + 16, :] = pack_ends(blocks)
    mask = mask_ref[...].astype(jnp.float32).astype(jnp.bfloat16)
    ends_ref[groups * 16 :, :] = pack_ends([mask])
    wrap_ref[...] = jnp.zeros_like(wrap_ref)

    @pl.when(over_wrap())
    def _():
        join_ends(ends_ref, halo_ref, mask_rows, all_ends)
        pack_side(all_ends, wrap_ref, lax.rem(lax.axis_index("lon"), 2) == 1)


def join_ends(own_ends_ref, halo_ref, mask_rows, ends_ref):
    channels = halo_ref.shape[0]
    groups = channels // 8
    for g in range(groups + 1):
        if g < groups:
            blocks = [halo_ref[channel_of(channels, g, j)] for j in range(8)]
        else:
            blocks = [mask_rows[...].astype(jnp.bfloat16)]
        own = jnp.zeros((16, halo_ref.shape[2]), jnp.bfloat16)
        if own_ends_ref is not None:
            own = own_ends_ref[g * 16 : g * 16 + 16, :]
        ends_ref[g * 32 : g * 32 + 16, :] = own
        ends_ref[g * 32 + 16 : g * 32 + 32, :] = pack_ends(blocks)


def pack_side(ends_ref, out_ref, to_east):
    width = ends_ref.shape[1]
    groups = ends_ref.shape[0] // 32 - 1
    lower = lanes((32, width)) % 16 < 8
    for m in range(groups // 2 + 1):
        n = m if m < groups // 2 else groups
        one = ends_ref[n * 32 : n * 32 + 32, :]
        one = jnp.where(to_east, one, pltpu.roll(one, width - HALO, 1))
        if n < groups:
            two = ends_ref[(n + groups // 2) * 32 : (n + groups // 2) * 32 + 32, :]
            two = jnp.where(to_east, pltpu.roll(two, 8, 1), pltpu.roll(two, 8 - HALO, 1))
            one = jnp.where(lower, one, two)
        out_ref[m * 32 : m * 32 + 32, :] = one


def far_rows(
    mirrored,
    second_ref,
    sent_ref,
    near_halo_ref,
    near_mask_ref,
    own_ends_ref,
    after_ref,
    halo_ref,
    halo_mask_ref,
    ends_ref,
    cross_ref,
    own_ref,
    wide,
    mask_rows,
):
    del after_ref
    channels, _, width = halo_ref.shape
    lat = lax.axis_index("lat")
    odd = lax.rem(lat, 2) == 1
    lon_odd = lax.rem(lax.axis_index("lon"), 2) == 1
    folded = lat == lax.axis_size("lat") - 1
    own_ref[...] = jnp.zeros_like(own_ref)
    if mirrored:

        @pl.when(folded & over_wrap())
        def _():
            place_rows(sent_ref, odd, folded, wide, mask_rows, channels)
            halo_ref[...] = wide[...].astype(jnp.bfloat16).reshape(channels, 16, width)
            join_ends(None, halo_ref, mask_rows, ends_ref)
            pack_side(ends_ref, own_ref, jnp.logical_not(lon_odd))

    place_rows(second_ref, odd, folded, wide, mask_rows, channels)
    far = wide[...].astype(jnp.bfloat16).reshape(channels, 16, width)
    halo_ref[...] = near_halo_ref[...] + far
    halo_mask_ref[...] = near_mask_ref[...] + mask_rows[...]
    join_ends(own_ends_ref, halo_ref, halo_mask_ref, ends_ref)
    pack_side(ends_ref, cross_ref, lon_odd)
    if mirrored:

        @pl.when(over_wrap())
        def _():
            cross_ref[...] = jnp.zeros_like(cross_ref)


def core_columns(ends_ref, after_ref, core_ref):
    del after_ref
    pack_side(ends_ref, core_ref, lax.rem(lax.axis_index("lon"), 2) == 0)


def in_row(place, first_layer):
    none = jnp.full_like(place, 1000)
    row = jnp.where(place < 16, place, none)
    row = jnp.where((place >= 16) & (place < 19), place - 19, row)
    row = jnp.where((place >= 20) & (place < 23), place - 4, row)
    if first_layer:
        row = jnp.where((place >= 24) & (place < 27), place - 30, row)
        row = jnp.where((place >= 28) & (place < 31), place - 9, row)
    return row


EDGE = (-3, -2, -1, 16, 17, 18, 0, 1, 2, 13, 14, 15)
INNER = (3, 4, 5, 6, 7, 8, 9, 10, 11, 12)


def place_of(row):
    if row < 0:
        return row + 19
    return row if row < 16 else row + 4


def conv_matrices(table, out_ref, left, right, row, rows_out):
    channels, taps = table.shape
    count = len(rows_out)
    folded = lax.axis_index("lat") == lax.axis_size("lat") - 1
    k = lanes((1, 256))
    shift = k // 32
    place = k - shift * 32
    tap = lax.broadcasted_iota(jnp.int32, (taps, 256), 0)
    row = row(place)
    for i, here in enumerate(rows_out):
        if here is None:
            wanted = jnp.full_like(k, -1)
        else:
            a = row - here + 3
            inside = (a >= 0) & (a <= 6) & (shift < 7)
            wanted = a * 7 + shift
            if here > 15:
                wanted = jnp.where(folded, 48 - wanted, wanted)
            wanted = jnp.where(inside, wanted, -1)
            wanted = jnp.where((shift == 7) & (place < 3), 49 + place, wanted)
        picks = (tap == wanted).astype(jnp.float32).astype(jnp.bfloat16)
        matrix = jnp.dot(table, picks, preferred_element_type=jnp.float32)
        left[pl.ds(i, channels, stride=count), :] = matrix[:, :128]
        right[pl.ds(i, channels, stride=count), :] = matrix[:, 128:]
    size = channels * count
    out_ref[:, :128] = left[:size, :].astype(jnp.bfloat16)
    out_ref[:, 128:] = right[:size, :].astype(jnp.bfloat16)


def split_bias(bias):
    high = bias.astype(jnp.bfloat16).astype(jnp.float32)
    rest = bias - high
    mid = rest.astype(jnp.bfloat16).astype(jnp.float32)
    return high, mid, rest - mid


def weights(
    kernel_ref,
    bias_ref,
    gain_ref,
    norm_bias_ref,
    expand_ref,
    expand_bias_ref,
    reduce_bias_ref,
    one_ref,
    two_ref,
    rows_ref,
    expand_out_ref,
    left,
    right,
    turn,
    tall,
):
    taps, layers, channels = kernel_ref.shape
    hidden = expand_ref.shape[2]
    turn[...] = jnp.zeros_like(turn)
    tall[...] = jnp.zeros_like(tall)
    for layer in range(layers):
        for tap in range(taps):
            turn[tap : tap + 1, :channels] = kernel_ref[tap, layer : layer + 1, :]
        parts = split_bias(bias_ref[layer : layer + 1, :])
        for n, part in enumerate(parts):
            turn[taps + n : taps + n + 1, :channels] = part
        table = turn[...].T[:channels, :64].astype(jnp.bfloat16)
        if layer == 0:
            every = EDGE + INNER + (None,) * 2
            row = functools.partial(in_row, first_layer=True)
            conv_matrices(table, one_ref, left, right, row, every)
        else:
            row = functools.partial(in_row, first_layer=False)
            conv_matrices(table, two_ref, left, right, row, tuple(range(16)))
    for layer in range(layers):
        for n, ref in enumerate((gain_ref, norm_bias_ref, reduce_bias_ref)):
            turn[:, :channels] = jnp.broadcast_to(ref[layer : layer + 1, :], (128, channels))
            rows_ref[layer, n] = turn[...].T[:channels, :]
        tall[:channels, :] = expand_ref[layer].astype(jnp.float32) * 0.5
        parts = split_bias(expand_bias_ref[layer : layer + 1, :] * 0.5)
        for n, part in enumerate(parts):
            tall[channels + n : channels + n + 1, :] = part
        for n in range(hidden // 128):
            piece = tall[:, n * 128 : (n + 1) * 128].T
            at = pl.ds(n * 128, 128)
            expand_out_ref[layer, at, :] = piece[:, : channels + 16].astype(jnp.bfloat16)


ERF = (7.97869712e-01, 3.63922860e-02, -8.78263977e-05, -3.66934787e-05, 1.42500782e-06)


def gelu_of_double(half):
    square = half * half
    total = jnp.full_like(half, 2.0 * 4.0 ** (len(ERF) - 1) * ERF[-1])
    for power in range(len(ERF) - 2, -1, -1):
        total = total * square + jnp.full_like(half, 2.0 * 4.0**power * ERF[power])
    return half * jnp.tanh(half * total) + half


def norm(rows_ref, layer, cells):
    average = jnp.mean(cells, axis=0, keepdims=True)
    centered = cells - average
    variance = jnp.mean(centered * centered, axis=0, keepdims=True)
    scaled = centered * lax.rsqrt(variance + 1e-06)
    return (scaled * rows_ref[layer, 0] + rows_ref[layer, 1]).astype(jnp.bfloat16)


def mlp(rows_ref, expand_ref, reduce_ref, layer, blocks, normed_ref, inner_ref, put):
    count = len(blocks)
    channels, width = rows_ref.shape[2:]
    hidden = inner_ref.shape[0]
    wide = count * width
    normed_ref[channels:, :wide] = jnp.ones((16, wide), jnp.bfloat16)
    for n, block in enumerate(blocks):
        at = slice(n * width, (n + 1) * width)
        normed_ref[:channels, at] = norm(rows_ref, layer, block())
    tiles = [slice(n, min(n + 2 * width, wide)) for n in range(0, wide, 2 * width)]
    for at in tiles:
        normed = normed_ref[:, at]
        for part in range(0, hidden, 128):
            matrix = expand_ref[layer, part : part + 128, :]
            half = jnp.dot(matrix, normed, preferred_element_type=jnp.float32)
            for k in range(0, 128, 16):
                values = gelu_of_double(half[k : k + 16, :].astype(jnp.bfloat16))
                inner_ref[part + k : part + k + 16, at] = values
    extra = rows_ref[layer, 2]
    for t, at in enumerate(tiles):
        change = jnp.dot(reduce_ref[layer], inner_ref[:, at], preferred_element_type=jnp.float32)
        for n in range((at.stop - at.start) // width):
            put(t * 2 + n, change[:, n * width : (n + 1) * width] + extra)


def columns_stack(block, ones):
    width = block.shape[1]
    stack = [block if s == 0 else pltpu.roll(block, (-s) % width, 1) for s in range(-3, 4)]
    return jnp.concatenate(stack + [ones], axis=0)


def conv_rows(matrix_ref, stack_of, conv, channels, stride, first, count):
    ones = jnp.ones((matrix_ref.shape[1] // 8, 128), jnp.bfloat16)

    def step(c, carry):
        matrix = matrix_ref[pl.ds(pl.multiple_of(c * stride + first, 8), count), :]
        result = jnp.dot(matrix, stack_of(c, ones), preferred_element_type=jnp.float32)
        conv[pl.ds(c, count, stride=pitch(channels)), :] = result
        return carry

    lax.fori_loop(0, channels, step, 0, unroll=channels)


def conv_row(conv, channels, i):
    start = i * pitch(channels)
    return lambda: conv[start : start + channels, :]


def inner_rows(
    field_ref, matrix_ref, rows_ref, expand_ref, reduce_ref, update_ref, conv, normed, inner
):
    channels, rows, width = field_ref.shape
    none = jnp.zeros((16, width), jnp.bfloat16)

    def stack_of(c, ones):
        return columns_stack(jnp.concatenate([field_ref[c], none], axis=0), ones)

    conv_rows(matrix_ref, stack_of, conv, channels, 24, 8, 16)

    def put(n, change):
        update_ref[pl.ds(INNER[n], channels, stride=24), :] = change

    blocks = [conv_row(conv, channels, i + len(EDGE) - 8) for i in range(len(INNER))]
    mlp(rows_ref, expand_ref, reduce_ref, 0, blocks, normed, inner, put)


def edge_rows(
    field_ref,
    halo_ref,
    matrix_ref,
    rows_ref,
    expand_ref,
    reduce_ref,
    old_ref,
    update_ref,
    conv,
    normed,
    inner,
):
    del old_ref
    channels, _, width = field_ref.shape

    def stack_of(c, ones):
        return columns_stack(jnp.concatenate([field_ref[c], halo_ref[c]], axis=0), ones)

    conv_rows(matrix_ref, stack_of, conv, channels, 24, 0, 16)
    for empty in (19, 23):
        update_ref[pl.ds(empty, channels, stride=24), :] = jnp.zeros((channels, width), jnp.float32)

    def put(n, change):
        update_ref[pl.ds(place_of(EDGE[n]), channels, stride=24), :] = change

    blocks = [conv_row(conv, channels, i) for i in range(len(EDGE))]
    mlp(rows_ref, expand_ref, reduce_ref, 0, blocks, normed, inner, put)


def neighbours(core_ref, cross_refs, group, groups):
    width = core_ref.shape[1]
    half = groups // 2
    m, upper = (half, 0) if group == groups else (group % half, group // half)
    core = core_ref[m * 32 : m * 32 + 32, :]
    cross = sum(ref[m * 32 : m * 32 + 32, :] for ref in cross_refs)
    lon_even = lax.rem(lax.axis_index("lon"), 2) == 0
    east = jnp.where(lon_even, core, cross)
    west = jnp.where(lon_even, cross, core)
    east = pltpu.roll(east, (HALO - 8 * upper) % width, 1)
    return east, pltpu.roll(west, width - 8, 1) if upper else west


def edge_columns(
    core_ref,
    cross_ref,
    wrap_ref,
    own_ref,
    ends_ref,
    matrix_ref,
    rows_ref,
    expand_ref,
    reduce_ref,
    strips,
    conv,
    normed,
    inner,
):
    channels, width = rows_ref.shape[2:]
    quarter = channels // 4
    groups = channels // 8
    lane32 = lanes((32, width))
    first_six = lane32 % 16 < HALO
    first_twelve = lane32 % 32 < 2 * HALO
    ones = jnp.ones((32, width), jnp.bfloat16)
    for g in range(groups):
        at = slice(g * 32, g * 32 + 32)
        east, west = neighbours(core_ref, (cross_ref, wrap_ref, own_ref), g, groups)
        own = ends_ref[at, :]
        at_west = jnp.where(first_six, west, own)
        at_east = jnp.where(first_six, own, east)
        for t in range(2):
            left = pltpu.roll(at_west, width - 16, 1) if t else at_west
            right = pltpu.roll(at_east, (2 * HALO - 16 * t) % width, 1)
            block = jnp.where(first_twelve, left, right)
            some = [channel_of(channels, g, 2 * n + t) for n in range(4)]
            matrix = jnp.concatenate(
                [matrix_ref[c * 24 : c * 24 + 24, :] for c in some], axis=0
            )
            stack = columns_stack(block, ones)
            result = jnp.dot(matrix, stack, preferred_element_type=jnp.float32)
            for n, c in enumerate(some):
                conv[pl.ds(c, 24, stride=pitch(channels)), :] = result[n * 24 : n * 24 + 24, :]

    order = {place_of(row): i for i, row in enumerate(EDGE + INNER)}
    lane = lanes((quarter, width))
    starts = [32 * (q // 2) + 6 * (q % 2) for q in range(8)]
    inside = [
        ((lane >= s + 3) & (lane < s + 9)) | ((lane >= s + 15) & (lane < s + 21)) for s in starts
    ]
    packs = []
    for p in range(3):
        parts = []
        for n in range(4):
            packed = jnp.zeros((quarter, width), jnp.float32)
            for q, start in enumerate(starts):
                if p * 8 + q in order:
                    row = order[p * 8 + q] * pitch(channels) + n * quarter
                    block = conv[row : row + quarter, :]
                    block = pltpu.roll(block, (start - 32 * n) % width, 1)
                    packed = jnp.where(inside[q], block, packed)
            parts.append(packed)
        packs.append(jnp.concatenate(parts, axis=0))

    def put(p, change):
        for q, start in enumerate(starts):
            near = pltpu.roll(change, (width - 6 - start) % width, 1)
            strips[pl.ds(p * 8 + q, channels, stride=24), :] = near

    blocks = [functools.partial(lambda block: block, packed) for packed in packs]
    mlp(rows_ref, expand_ref, reduce_ref, 0, blocks, normed, inner, put)


def second_layer(
    field_ref,
    mask_ref,
    halo_ref,
    halo_mask_ref,
    core_ref,
    cross_ref,
    wrap_ref,
    own_ref,
    strips,
    update_ref,
    matrix_ref,
    rows_ref,
    expand_ref,
    reduce_ref,
    out_ref,
    main_ref,
    conv,
    normed,
    inner,
):
    channels, rows, width = out_ref.shape
    groups = channels // 8
    lane32 = lanes((32, width))
    lane24 = lanes((24, width))
    first_six = lane32 % 16 < HALO

    def beside_of(received, slot):
        beside = pltpu.roll(received, (width - HALO - 16 * slot) % width, 1)
        return beside.astype(jnp.float32)[0:24, :]

    def received(g):
        east, west = neighbours(core_ref, (cross_ref, wrap_ref, own_ref), g, groups)
        return jnp.where(first_six, west, east)

    main_mask = jnp.concatenate(
        [mask_ref[...].astype(jnp.float32), halo_mask_ref[0:8, :]], axis=0
    )
    side_mask = beside_of(received(groups), 0)
    low = lane24 < 3
    high = lane24 >= width - 3
    blank = jnp.zeros((8, width), jnp.float32)
    ones = jnp.ones((32, width), jnp.bfloat16)
    lane16 = lanes((16, width))
    away = {s: lane16 < s if s > 0 else lane16 >= width + s for s in range(-3, 4) if s}

    def halves(block):
        low_rows = block[:16, :].astype(jnp.bfloat16)
        return low_rows, jnp.concatenate([block[16:, :], blank], axis=0).astype(jnp.bfloat16)

    for g in range(groups):
        both = received(g)
        for j in range(8):
            c = channel_of(channels, g, j)
            near = strips[c * 24 : c * 24 + 24, :]
            far = pltpu.roll(near, width - 2 * HALO, 1)
            change = update_ref[c * 24 : c * 24 + 24, :]
            change = jnp.where(low, near, jnp.where(high, far, change))
            own = field_ref[c].astype(jnp.float32)
            halo = halo_ref[c].astype(jnp.float32)[:8, :]
            main = halves(main_mask * (jnp.concatenate([own, halo], axis=0) + change))
            main_ref[c] = main[0]
            change = jnp.where(high, near, far)
            beside = halves(side_mask * (beside_of(both, j) + change))
            stack = []
            for s in range(-3, 4):
                for part, other in zip(main, beside):
                    if s:
                        part = pltpu.roll(jnp.where(away[s], other, part), (-s) % width, 1)
                    stack.append(part)
            stack = jnp.concatenate(stack + [ones], axis=0)
            matrix = matrix_ref[c * 16 : c * 16 + 16, :]
            result = jnp.dot(matrix, stack, preferred_element_type=jnp.float32)
            conv[pl.ds(c, 16, stride=pitch(channels)), :] = result

    mask = mask_ref[...].astype(jnp.float32)
    changes = []

    def put(n, change):
        changes.append(change)
        if n < rows - 1:
            return
        for c in range(0, channels, 8):
            parts = []
            for half in range(0, rows, 8):
                part = [changes[i][c : c + 8, :] for i in range(half, half + 8)]
                parts.append(jnp.swapaxes(jnp.stack(part, axis=0), 0, 1))
            change = jnp.concatenate(parts, axis=1)
            old = main_ref[c : c + 8].astype(jnp.float32)
            out_ref[c : c + 8] = (mask[None] * (old + change)).astype(jnp.bfloat16)

    blocks = [conv_row(conv, channels, i) for i in range(rows)]
    mlp(rows_ref, expand_ref, reduce_ref, 1, blocks, normed, inner, put)


def per_device(
    nlat,
    nlon,
    field,
    land_mask,
    depth_kernel,
    depth_bias,
    norm_gain,
    norm_bias,
    w_expand,
    b_expand,
    w_reduce,
    b_reduce,
):
    channels, rows, width = field.shape
    layers, hidden = b_expand.shape
    bf16, f32 = jnp.bfloat16, jnp.float32
    edge = HALO * channels + 16

    def buffers(count):
        return [
            pltpu.VMEM((channels + 16, count * width), bf16),
            pltpu.VMEM((hidden, count * width), bf16),
        ]

    def pack(upper_if_even, after):
        return pl.pallas_call(
            functools.partial(pack_rows, upper_if_even),
            out_shape=jax.ShapeDtypeStruct((edge, width), bf16),
            in_specs=vmem(2) + [pl.BlockSpec(memory_space=pl.ANY)],
            out_specs=pl.BlockSpec(memory_space=pltpu.VMEM),
            scratch_shapes=[
                pltpu.VMEM((channels * rows, width), f32),
                pltpu.VMEM((rows, width), f32),
            ],
            compiler_params=params(),
            cost_estimate=cost(4e9),
        )(field, land_mask, after)

    begun = pl.pallas_call(
        first_step,
        out_shape=jax.ShapeDtypeStruct((8, 128), f32),
        out_specs=pl.BlockSpec(memory_space=pltpu.VMEM),
        compiler_params=params(),
        cost_estimate=cost(4e9),
    )()
    first = pack(True, begun)
    second_sent = pack(False, first)

    alone = nlat == 2

    def at(d, lat):
        return d * nlat + lat

    pairs = []
    for d in range(nlon):
        for low in range(1, nlat - 1, 2):
            pairs += [(at(d, low), at(d, low + 1)), (at(d, low + 1), at(d, low))]
        pairs.append((at(d, nlat - 1), at(nlon - 1 - d, nlat - 1)))
        pairs.append((at(d, 0), at(d ^ 1, 0)))
    second = lax.ppermute(second_sent, ("lon", "lat"), pairs)
    pairs = []
    for low in range(0, nlat - 1, 2):
        pairs += [(low, low + 1), (low + 1, low)]
    first = lax.ppermute(first, "lat", pairs)

    kernel = depth_kernel.transpose(2, 3, 0, 1).reshape(49, layers, channels)
    matrix_one, matrix_two, by_channel, expand = pl.pallas_call(
        weights,
        out_shape=[
            jax.ShapeDtypeStruct((channels * 24, 256), bf16),
            jax.ShapeDtypeStruct((channels * 16, 256), bf16),
            jax.ShapeDtypeStruct((layers, 3, channels, 128), f32),
            jax.ShapeDtypeStruct((layers, hidden, channels + 16), bf16),
        ],
        in_specs=vmem(7),
        out_specs=vmem(4),
        scratch_shapes=[
            pltpu.VMEM((channels * 24, 128), f32),
            pltpu.VMEM((channels * 24, 128), f32),
            pltpu.VMEM((128, 128), f32),
            pltpu.VMEM((128, hidden), f32),
        ],
        compiler_params=params(),
        cost_estimate=cost(2e9),
    )(
        kernel,
        depth_bias,
        norm_gain,
        norm_bias,
        w_expand.transpose(0, 2, 1),
        b_expand,
        b_reduce,
    )
    update = pl.pallas_call(
        inner_rows,
        out_shape=jax.ShapeDtypeStruct((channels * 24, width), f32),
        in_specs=vmem(5),
        out_specs=pl.BlockSpec(memory_space=pltpu.VMEM),
        scratch_shapes=[pltpu.VMEM((pitch(channels) * 16, width), f32)] + buffers(len(INNER)),
        compiler_params=params(),
        cost_estimate=cost(4e9),
    )(field, matrix_one, by_channel, expand, w_reduce)

    groups = channels // 8 + 1
    sent_rows = (channels // 16 + 1) * 32
    near_halo, near_mask, own_ends, wrap = pl.pallas_call(
        near_rows,
        out_shape=[
            jax.ShapeDtypeStruct((channels, 16, width), bf16),
            jax.ShapeDtypeStruct((16, width), f32),
            jax.ShapeDtypeStruct((groups * 16, width), bf16),
            jax.ShapeDtypeStruct((sent_rows, width), bf16),
        ],
        in_specs=vmem(3),
        out_specs=vmem(4),
        scratch_shapes=[
            pltpu.VMEM((channels * 16, width), f32),
            pltpu.VMEM((groups * 32, width), bf16),
        ],
        compiler_params=params(),
        cost_estimate=cost(1e9),
    )(field, land_mask, first)
    if alone:
        pairs = []
        for lat in range(nlat):
            pairs += [(lat, at(nlon - 1, lat)), (at(nlon - 1, lat), lat)]
            pairs += [(at(d, lat), at(d, 1 - lat)) for d in range(1, nlon - 1)]
        wrap = lax.ppermute(wrap, ("lon", "lat"), pairs)
    else:
        wrap = jnp.zeros_like(wrap)
    halo, halo_mask, ends, cross, own = pl.pallas_call(
        functools.partial(far_rows, alone),
        out_shape=[
            jax.ShapeDtypeStruct((channels, 16, width), bf16),
            jax.ShapeDtypeStruct((16, width), f32),
            jax.ShapeDtypeStruct((groups * 32, width), bf16),
            jax.ShapeDtypeStruct((sent_rows, width), bf16),
            jax.ShapeDtypeStruct((sent_rows, width), bf16),
        ],
        in_specs=vmem(5) + [pl.BlockSpec(memory_space=pl.ANY)],
        out_specs=vmem(5),
        scratch_shapes=[
            pltpu.VMEM((channels * 16, width), f32),
            pltpu.VMEM((16, width), f32),
        ],
        compiler_params=params(),
    )(second, second_sent, near_halo, near_mask, own_ends, update)
    core = pl.pallas_call(
        core_columns,
        out_shape=jax.ShapeDtypeStruct((sent_rows, width), bf16),
        in_specs=vmem(1) + [pl.BlockSpec(memory_space=pl.ANY)],
        out_specs=pl.BlockSpec(memory_space=pltpu.VMEM),
        compiler_params=params(),
    )(ends, cross)

    pairs = []
    for low in range(0, nlon, 2):
        pairs += [(low, low + 1), (low + 1, low)]
    core = lax.ppermute(core, "lon", pairs)
    pairs = []
    for lat in range(nlat):
        for low in range(1, nlon, 2):
            after = (low + 1) % nlon
            if after or not alone:
                pairs += [(at(low, lat), at(after, lat)), (at(after, lat), at(low, lat))]
            else:
                pairs += [(at(low, lat), at(low, 1 - lat)), (at(after, lat), at(after, 1 - lat))]
    cross = lax.ppermute(cross, ("lon", "lat"), pairs)

    update = pl.pallas_call(
        edge_rows,
        out_shape=jax.ShapeDtypeStruct((channels * 24, width), f32),
        in_specs=vmem(7),
        out_specs=pl.BlockSpec(memory_space=pltpu.VMEM),
        scratch_shapes=[pltpu.VMEM((pitch(channels) * 16, width), f32)] + buffers(len(EDGE)),
        input_output_aliases={6: 0},
        compiler_params=params(),
        cost_estimate=cost(4e9),
    )(field, halo, matrix_one, by_channel, expand, w_reduce, update)

    strips = pl.pallas_call(
        edge_columns,
        out_shape=jax.ShapeDtypeStruct((channels * 24, width), f32),
        in_specs=vmem(9),
        out_specs=pl.BlockSpec(memory_space=pltpu.VMEM),
        scratch_shapes=[pltpu.VMEM((pitch(channels) * 24, width), f32)] + buffers(3),
        compiler_params=params(),
    )(core, cross, wrap, own, ends, matrix_one, by_channel, expand, w_reduce)

    return pl.pallas_call(
        second_layer,
        out_shape=jax.ShapeDtypeStruct((channels, rows, width), bf16),
        in_specs=vmem(14),
        out_specs=pl.BlockSpec(memory_space=pltpu.VMEM),
        scratch_shapes=[
            pltpu.VMEM((channels, rows, width), bf16),
            pltpu.VMEM((pitch(channels) * 16, width), f32),
        ]
        + buffers(rows),
        compiler_params=params(),
    )(
        field,
        land_mask,
        halo,
        halo_mask,
        core,
        cross,
        wrap,
        own,
        strips,
        update,
        matrix_two,
        by_channel,
        expand,
        w_reduce,
    )


def solution(mesh):
    placed = (P(None, "lat", "lon"), P("lat", "lon"), P(), P(), P(), P(), P(), P(), P(), P())
    return jax.shard_map(
        functools.partial(per_device, mesh.shape["lat"], mesh.shape["lon"]),
        mesh=mesh,
        in_specs=placed,
        out_specs=P(None, "lat", "lon"),
        check_vma=False,
    )
```

```python
import functools

import jax
import jax.numpy as jnp
from jax import lax
from jax.experimental import pallas as pl
from jax.experimental.pallas import tpu as pltpu
from jax.sharding import PartitionSpec as P


HALO = 6
APART = 24
VMEM_LIMIT = 20 * 1024 * 1024


def pitch(channels):
    return channels + 8


def params():
    return pltpu.CompilerParams(vmem_limit_bytes=VMEM_LIMIT)


def cost(flops):
    return pl.CostEstimate(flops=int(flops), bytes_accessed=1 << 20, transcendentals=0)


def vmem(count):
    return [pl.BlockSpec(memory_space=pltpu.VMEM)] * count


def lanes(shape):
    return lax.broadcasted_iota(jnp.int32, shape, len(shape) - 1)


def first_step(out_ref):
    out_ref[...] = jnp.zeros_like(out_ref)


def pack_rows(upper_if_even, field_ref, mask_ref, after_ref, out_ref, wide, wide_mask):
    del after_ref
    kept = 1.0 if upper_if_even else (lax.axis_index("lat") > 0).astype(jnp.float32)
    channels, rows, width = field_ref.shape
    even = lax.rem(lax.axis_index("lat"), 2) == 0
    take_upper = even if upper_if_even else jnp.logical_not(even)
    for c in range(channels):
        wide[c * APART : c * APART + rows, :] = field_ref[c].astype(jnp.float32)
    wide_mask[...] = mask_ref[...].astype(jnp.float32)
    for k in range(HALO):
        lower = wide[pl.ds(k, channels, stride=APART), :]
        upper = wide[pl.ds(rows - HALO + k, channels, stride=APART), :]
        at = pl.ds(k * channels, channels)
        out_ref[at, :] = (kept * jnp.where(take_upper, upper, lower)).astype(jnp.bfloat16)
    pad = jnp.zeros((16 - HALO, width), jnp.float32)
    lower = jnp.concatenate([wide_mask[0:HALO, :], pad], axis=0)
    upper = jnp.concatenate([wide_mask[rows - HALO : rows, :], pad], axis=0)
    at = pl.ds(HALO * channels, 16)
    out_ref[at, :] = (kept * jnp.where(take_upper, upper, lower)).astype(jnp.bfloat16)


def north_place(row):
    return jnp.where(row < 3, 4 + row, 9 + row)


def south_place(k):
    return k - 3 if k >= 3 else 8 + k


def place_rows(received_ref, is_north, turned, wide, mask_rows, channels):
    width = received_ref.shape[1]
    wide[...] = jnp.zeros_like(wide)
    mask_rows[...] = jnp.zeros_like(mask_rows)
    turn = None
    if turned is not None:
        sub = lax.broadcasted_iota(jnp.int32, (width, width), 0)
        target = lanes((width, width))
        turn = sub == jnp.where(turned, width - 1 - target, target)
        turn = turn.astype(jnp.float32).astype(jnp.bfloat16)

    def rows_at(start, count):
        block = received_ref[start : start + count, :]
        if turn is None:
            return block.astype(jnp.float32)
        return jnp.dot(block, turn, preferred_element_type=jnp.float32)

    masks = rows_at(HALO * channels, 16)
    for k in range(HALO):
        row = k if turned is None else jnp.where(turned, HALO - 1 - k, k)
        place = jnp.where(is_north, north_place(row), south_place(k))
        wide[pl.ds(place, channels, stride=APART), :] = rows_at(k * channels, channels)
        mask_rows[pl.ds(place, 1), :] = masks[k : k + 1, :]


def placed(wide, channels):
    blocks = wide[...].reshape(channels, APART, wide.shape[1])
    return blocks[:, :16, :].astype(jnp.bfloat16)


def pack_ends(blocks):
    rows, width = blocks[0].shape
    slot = lanes((rows, width)) // 16
    packed = jnp.zeros((rows, width), jnp.bfloat16)
    for j, block in enumerate(blocks):
        packed = jnp.where(slot == j, pltpu.roll(block, 16 * j + HALO, 1), packed)
    return packed


def channel_of(channels, group, slot):
    return slot // 2 * (channels // 4) + group * 2 + slot % 2


def over_wrap():
    lon = lax.axis_index("lon")
    return (lon == 0) | (lon == lax.axis_size("lon") - 1)


def near_rows(
    field_ref, mask_ref, first_ref, halo_ref, mask_rows, ends_ref, wrap_ref, wide, all_ends
):
    channels, rows, width = field_ref.shape
    even = lax.rem(lax.axis_index("lat"), 2) == 0
    place_rows(first_ref, even, None, wide, mask_rows, channels)
    halo_ref[...] = placed(wide, channels)
    groups = channels // 8
    for g in range(groups):
        blocks = [field_ref[channel_of(channels, g, j)] for j in range(8)]
        ends_ref[g * 16 : g * 16 + 16, :] = pack_ends(blocks)
    mask = mask_ref[...].astype(jnp.float32).astype(jnp.bfloat16)
    ends_ref[groups * 16 :, :] = pack_ends([mask])
    wrap_ref[...] = jnp.zeros_like(wrap_ref)

    @pl.when(over_wrap())
    def _():
        join_ends(ends_ref, halo_ref, mask_rows, all_ends)
        pack_side(all_ends, wrap_ref, lax.rem(lax.axis_index("lon"), 2) == 1)


def join_ends(own_ends_ref, halo_ref, mask_rows, ends_ref):
    channels = halo_ref.shape[0]
    groups = channels // 8
    for g in range(groups + 1):
        if g < groups:
            blocks = [halo_ref[channel_of(channels, g, j)] for j in range(8)]
        else:
            blocks = [mask_rows[...].astype(jnp.bfloat16)]
        own = jnp.zeros((16, halo_ref.shape[2]), jnp.bfloat16)
        if own_ends_ref is not None:
            own = own_ends_ref[g * 16 : g * 16 + 16, :]
        ends_ref[g * 32 : g * 32 + 16, :] = own
        ends_ref[g * 32 + 16 : g * 32 + 32, :] = pack_ends(blocks)


def pack_side(ends_ref, out_ref, to_east):
    width = ends_ref.shape[1]
    groups = ends_ref.shape[0] // 32 - 1
    lower = lanes((32, width)) % 16 < 8
    for m in range(groups // 2 + 1):
        n = m if m < groups // 2 else groups
        one = ends_ref[n * 32 : n * 32 + 32, :]
        one = jnp.where(to_east, one, pltpu.roll(one, width - HALO, 1))
        if n < groups:
            two = ends_ref[(n + groups // 2) * 32 : (n + groups // 2) * 32 + 32, :]
            two = jnp.where(to_east, pltpu.roll(two, 8, 1), pltpu.roll(two, 8 - HALO, 1))
            one = jnp.where(lower, one, two)
        out_ref[m * 32 : m * 32 + 32, :] = one


def far_rows(
    mirrored,
    second_ref,
    sent_ref,
    near_halo_ref,
    near_mask_ref,
    own_ends_ref,
    after_ref,
    halo_ref,
    halo_mask_ref,
    ends_ref,
    cross_ref,
    own_ref,
    wide,
    mask_rows,
):
    del after_ref
    channels, _, width = halo_ref.shape
    lat = lax.axis_index("lat")
    odd = lax.rem(lat, 2) == 1
    lon_odd = lax.rem(lax.axis_index("lon"), 2) == 1
    folded = lat == lax.axis_size("lat") - 1
    own_ref[...] = jnp.zeros_like(own_ref)
    if mirrored:

        @pl.when(folded & over_wrap())
        def _():
            place_rows(sent_ref, odd, folded, wide, mask_rows, channels)
            halo_ref[...] = placed(wide, channels)
            join_ends(None, halo_ref, mask_rows, ends_ref)
            pack_side(ends_ref, own_ref, jnp.logical_not(lon_odd))

    place_rows(second_ref, odd, folded, wide, mask_rows, channels)
    far = placed(wide, channels)
    halo_ref[...] = near_halo_ref[...] + far
    halo_mask_ref[...] = near_mask_ref[...] + mask_rows[...]
    join_ends(own_ends_ref, halo_ref, halo_mask_ref, ends_ref)
    pack_side(ends_ref, cross_ref, lon_odd)
    if mirrored:

        @pl.when(over_wrap())
        def _():
            cross_ref[...] = jnp.zeros_like(cross_ref)


def core_columns(ends_ref, after_ref, core_ref):
    del after_ref
    pack_side(ends_ref, core_ref, lax.rem(lax.axis_index("lon"), 2) == 0)


def in_row(place, first_layer):
    none = jnp.full_like(place, 1000)
    row = jnp.where(place < 16, place, none)
    row = jnp.where((place >= 16) & (place < 19), place - 19, row)
    row = jnp.where((place >= 20) & (place < 23), place - 4, row)
    if first_layer:
        row = jnp.where((place >= 24) & (place < 27), place - 30, row)
        row = jnp.where((place >= 28) & (place < 31), place - 9, row)
    return row


EDGE = (-3, -2, -1, 16, 17, 18, 0, 1, 2, 13, 14, 15)
INNER = (3, 4, 5, 6, 7, 8, 9, 10, 11, 12)


def place_of(row):
    if row < 0:
        return row + 19
    return row if row < 16 else row + 4


def conv_matrices(table, out_ref, left, right, row, rows_out):
    channels, taps = table.shape
    count = len(rows_out)
    folded = lax.axis_index("lat") == lax.axis_size("lat") - 1
    k = lanes((1, 256))
    shift = k // 32
    place = k - shift * 32
    tap = lax.broadcasted_iota(jnp.int32, (taps, 256), 0)
    row = row(place)
    for i, here in enumerate(rows_out):
        if here is None:
            wanted = jnp.full_like(k, -1)
        else:
            a = row - here + 3
            inside = (a >= 0) & (a <= 6) & (shift < 7)
            wanted = a * 7 + shift
            if here > 15:
                wanted = jnp.where(folded, 48 - wanted, wanted)
            wanted = jnp.where(inside, wanted, -1)
            wanted = jnp.where((shift == 7) & (place < 3), 49 + place, wanted)
        picks = (tap == wanted).astype(jnp.float32).astype(jnp.bfloat16)
        matrix = jnp.dot(table, picks, preferred_element_type=jnp.float32)
        left[pl.ds(i, channels, stride=count), :] = matrix[:, :128]
        right[pl.ds(i, channels, stride=count), :] = matrix[:, 128:]
    size = channels * count
    out_ref[:, :128] = left[:size, :].astype(jnp.bfloat16)
    out_ref[:, 128:] = right[:size, :].astype(jnp.bfloat16)


def split_bias(bias):
    high = bias.astype(jnp.bfloat16).astype(jnp.float32)
    rest = bias - high
    mid = rest.astype(jnp.bfloat16).astype(jnp.float32)
    return high, mid, rest - mid


def weights(
    kernel_ref,
    bias_ref,
    gain_ref,
    norm_bias_ref,
    expand_ref,
    expand_bias_ref,
    reduce_bias_ref,
    one_ref,
    two_ref,
    rows_ref,
    expand_out_ref,
    left,
    right,
    turn,
    tall,
):
    taps, layers, channels = kernel_ref.shape
    hidden = expand_ref.shape[2]
    turn[...] = jnp.zeros_like(turn)
    tall[...] = jnp.zeros_like(tall)
    for layer in range(layers):
        for tap in range(taps):
            turn[tap : tap + 1, :channels] = kernel_ref[tap, layer : layer + 1, :]
        parts = split_bias(bias_ref[layer : layer + 1, :])
        for n, part in enumerate(parts):
            turn[taps + n : taps + n + 1, :channels] = part
        table = turn[...].T[:channels, :64].astype(jnp.bfloat16)
        if layer == 0:
            every = EDGE + INNER + (None,) * 2
            row = functools.partial(in_row, first_layer=True)
            conv_matrices(table, one_ref, left, right, row, every)
        else:
            row = functools.partial(in_row, first_layer=False)
            conv_matrices(table, two_ref, left, right, row, tuple(range(16)))
    for layer in range(layers):
        for n, ref in enumerate((gain_ref, norm_bias_ref, reduce_bias_ref)):
            turn[:, :channels] = jnp.broadcast_to(ref[layer : layer + 1, :], (128, channels))
            rows_ref[layer, n] = turn[...].T[:channels, :]
        tall[:channels, :] = expand_ref[layer].astype(jnp.float32) * 0.5
        parts = split_bias(expand_bias_ref[layer : layer + 1, :] * 0.5)
        for n, part in enumerate(parts):
            tall[channels + n : channels + n + 1, :] = part
        for n in range(hidden // 128):
            piece = tall[:, n * 128 : (n + 1) * 128].T
            at = pl.ds(n * 128, 128)
            expand_out_ref[layer, at, :] = piece[:, : channels + 16].astype(jnp.bfloat16)


ERF = (7.97869712e-01, 3.63922860e-02, -8.78263977e-05, -3.66934787e-05, 1.42500782e-06)


def gelu_of_double(half):
    square = half * half
    total = jnp.full_like(half, 2.0 * 4.0 ** (len(ERF) - 1) * ERF[-1])
    for power in range(len(ERF) - 2, -1, -1):
        total = total * square + jnp.full_like(half, 2.0 * 4.0**power * ERF[power])
    return half * jnp.tanh(half * total) + half


def norm(rows_ref, layer, cells):
    average = jnp.mean(cells, axis=0, keepdims=True)
    centered = cells - average
    variance = jnp.mean(centered * centered, axis=0, keepdims=True)
    scaled = centered * lax.rsqrt(variance + 1e-06)
    return (scaled * rows_ref[layer, 0] + rows_ref[layer, 1]).astype(jnp.bfloat16)


def mlp(rows_ref, expand_ref, reduce_ref, layer, blocks, normed_ref, inner_ref, put):
    count = len(blocks)
    channels, width = rows_ref.shape[2:]
    hidden = inner_ref.shape[0]
    wide = count * width
    normed_ref[channels:, :wide] = jnp.ones((16, wide), jnp.bfloat16)
    for n, block in enumerate(blocks):
        at = slice(n * width, (n + 1) * width)
        normed_ref[:channels, at] = norm(rows_ref, layer, block())
    tiles = [slice(n, min(n + 2 * width, wide)) for n in range(0, wide, 2 * width)]
    for at in tiles:
        normed = normed_ref[:, at]
        for part in range(0, hidden, 128):
            matrix = expand_ref[layer, part : part + 128, :]
            half = jnp.dot(matrix, normed, preferred_element_type=jnp.float32)
            for k in range(0, 128, 16):
                values = gelu_of_double(half[k : k + 16, :].astype(jnp.bfloat16))
                inner_ref[part + k : part + k + 16, at] = values
    extra = rows_ref[layer, 2]
    for t, at in enumerate(tiles):
        change = jnp.dot(reduce_ref[layer], inner_ref[:, at], preferred_element_type=jnp.float32)
        for n in range((at.stop - at.start) // width):
            put(t * 2 + n, change[:, n * width : (n + 1) * width] + extra)


def columns_stack(block, ones):
    width = block.shape[1]
    stack = [block if s == 0 else pltpu.roll(block, (-s) % width, 1) for s in range(-3, 4)]
    return jnp.concatenate(stack + [ones], axis=0)


def conv_rows(matrix_ref, stack_of, conv, channels, stride, first, count):
    ones = jnp.ones((matrix_ref.shape[1] // 8, 128), jnp.bfloat16)

    def step(c, carry):
        matrix = matrix_ref[pl.ds(pl.multiple_of(c * stride + first, 8), count), :]
        result = jnp.dot(matrix, stack_of(c, ones), preferred_element_type=jnp.float32)
        conv[pl.ds(c, count, stride=pitch(channels)), :] = result
        return carry

    lax.fori_loop(0, channels, step, 0, unroll=channels)


def conv_row(conv, channels, i):
    start = i * pitch(channels)
    return lambda: conv[start : start + channels, :]


def inner_rows(
    field_ref, matrix_ref, rows_ref, expand_ref, reduce_ref, update_ref, conv, normed, inner
):
    channels, rows, width = field_ref.shape
    none = jnp.zeros((16, width), jnp.bfloat16)

    def stack_of(c, ones):
        return columns_stack(jnp.concatenate([field_ref[c], none], axis=0), ones)

    conv_rows(matrix_ref, stack_of, conv, channels, 24, 8, 16)

    def put(n, change):
        update_ref[pl.ds(INNER[n], channels, stride=24), :] = change

    blocks = [conv_row(conv, channels, i + len(EDGE) - 8) for i in range(len(INNER))]
    mlp(rows_ref, expand_ref, reduce_ref, 0, blocks, normed, inner, put)


def edge_rows(
    field_ref,
    halo_ref,
    matrix_ref,
    rows_ref,
    expand_ref,
    reduce_ref,
    old_ref,
    update_ref,
    conv,
    normed,
    inner,
):
    del old_ref
    channels, _, width = field_ref.shape

    def stack_of(c, ones):
        return columns_stack(jnp.concatenate([field_ref[c], halo_ref[c]], axis=0), ones)

    conv_rows(matrix_ref, stack_of, conv, channels, 24, 0, 16)
    for empty in (19, 23):
        update_ref[pl.ds(empty, channels, stride=24), :] = jnp.zeros((channels, width), jnp.float32)

    def put(n, change):
        update_ref[pl.ds(place_of(EDGE[n]), channels, stride=24), :] = change

    blocks = [conv_row(conv, channels, i) for i in range(len(EDGE))]
    mlp(rows_ref, expand_ref, reduce_ref, 0, blocks, normed, inner, put)


def neighbours(core_ref, cross_refs, group, groups):
    width = core_ref.shape[1]
    half = groups // 2
    m, upper = (half, 0) if group == groups else (group % half, group // half)
    core = core_ref[m * 32 : m * 32 + 32, :]
    cross = sum(ref[m * 32 : m * 32 + 32, :] for ref in cross_refs)
    lon_even = lax.rem(lax.axis_index("lon"), 2) == 0
    east = jnp.where(lon_even, core, cross)
    west = jnp.where(lon_even, cross, core)
    east = pltpu.roll(east, (HALO - 8 * upper) % width, 1)
    return east, pltpu.roll(west, width - 8, 1) if upper else west


def edge_columns(
    core_ref,
    cross_ref,
    wrap_ref,
    own_ref,
    ends_ref,
    matrix_ref,
    rows_ref,
    expand_ref,
    reduce_ref,
    strips,
    conv,
    normed,
    inner,
):
    channels, width = rows_ref.shape[2:]
    quarter = channels // 4
    groups = channels // 8
    lane32 = lanes((32, width))
    first_six = lane32 % 16 < HALO
    first_twelve = lane32 % 32 < 2 * HALO
    ones = jnp.ones((32, width), jnp.bfloat16)
    for g in range(groups):
        at = slice(g * 32, g * 32 + 32)
        east, west = neighbours(core_ref, (cross_ref, wrap_ref, own_ref), g, groups)
        own = ends_ref[at, :]
        at_west = jnp.where(first_six, west, own)
        at_east = jnp.where(first_six, own, east)
        for t in range(2):
            left = pltpu.roll(at_west, width - 16, 1) if t else at_west
            right = pltpu.roll(at_east, (2 * HALO - 16 * t) % width, 1)
            block = jnp.where(first_twelve, left, right)
            some = [channel_of(channels, g, 2 * n + t) for n in range(4)]
            matrix = jnp.concatenate(
                [matrix_ref[c * 24 : c * 24 + 24, :] for c in some], axis=0
            )
            stack = columns_stack(block, ones)
            result = jnp.dot(matrix, stack, preferred_element_type=jnp.float32)
            for n, c in enumerate(some):
                conv[pl.ds(c, 24, stride=pitch(channels)), :] = result[n * 24 : n * 24 + 24, :]

    order = {place_of(row): i for i, row in enumerate(EDGE + INNER)}
    lane = lanes((quarter, width))
    starts = [32 * (q // 2) + 6 * (q % 2) for q in range(8)]
    inside = [
        ((lane >= s + 3) & (lane < s + 9)) | ((lane >= s + 15) & (lane < s + 21)) for s in starts
    ]
    packs = []
    for p in range(3):
        parts = []
        for n in range(4):
            packed = jnp.zeros((quarter, width), jnp.float32)
            for q, start in enumerate(starts):
                if p * 8 + q in order:
                    row = order[p * 8 + q] * pitch(channels) + n * quarter
                    block = conv[row : row + quarter, :]
                    block = pltpu.roll(block, (start - 32 * n) % width, 1)
                    packed = jnp.where(inside[q], block, packed)
            parts.append(packed)
        packs.append(jnp.concatenate(parts, axis=0))

    def put(p, change):
        for q, start in enumerate(starts):
            near = pltpu.roll(change, (width - 6 - start) % width, 1)
            strips[pl.ds(p * 8 + q, channels, stride=24), :] = near

    blocks = [functools.partial(lambda block: block, packed) for packed in packs]
    mlp(rows_ref, expand_ref, reduce_ref, 0, blocks, normed, inner, put)


def second_layer(
    field_ref,
    mask_ref,
    halo_ref,
    halo_mask_ref,
    core_ref,
    cross_ref,
    wrap_ref,
    own_ref,
    strips,
    update_ref,
    matrix_ref,
    rows_ref,
    expand_ref,
    reduce_ref,
    out_ref,
    main_ref,
    conv,
    changes,
    normed,
    inner,
):
    channels, rows, width = out_ref.shape
    groups = channels // 8
    lane32 = lanes((32, width))
    lane24 = lanes((24, width))
    first_six = lane32 % 16 < HALO

    def beside_of(received, slot):
        beside = pltpu.roll(received, (width - HALO - 16 * slot) % width, 1)
        return beside.astype(jnp.float32)[0:24, :]

    def received(g):
        east, west = neighbours(core_ref, (cross_ref, wrap_ref, own_ref), g, groups)
        return jnp.where(first_six, west, east)

    main_mask = jnp.concatenate(
        [mask_ref[...].astype(jnp.float32), halo_mask_ref[0:8, :]], axis=0
    )
    side_mask = beside_of(received(groups), 0)
    low = lane24 < 3
    high = lane24 >= width - 3
    blank = jnp.zeros((8, width), jnp.float32)
    ones = jnp.ones((32, width), jnp.bfloat16)
    lane16 = lanes((16, width))
    away = {s: lane16 < s if s > 0 else lane16 >= width + s for s in range(-3, 4) if s}

    def halves(block):
        low_rows = block[:16, :].astype(jnp.bfloat16)
        return low_rows, jnp.concatenate([block[16:, :], blank], axis=0).astype(jnp.bfloat16)

    for g in range(groups):
        both = received(g)
        for j in range(8):
            c = channel_of(channels, g, j)
            near = strips[c * 24 : c * 24 + 24, :]
            far = pltpu.roll(near, width - 2 * HALO, 1)
            change = update_ref[c * 24 : c * 24 + 24, :]
            change = jnp.where(low, near, jnp.where(high, far, change))
            own = field_ref[c].astype(jnp.float32)
            halo = halo_ref[c].astype(jnp.float32)[:8, :]
            main = halves(main_mask * (jnp.concatenate([own, halo], axis=0) + change))
            main_ref[c] = main[0]
            change = jnp.where(high, near, far)
            beside = halves(side_mask * (beside_of(both, j) + change))
            stack = []
            for s in range(-3, 4):
                for part, other in zip(main, beside):
                    if s:
                        part = pltpu.roll(jnp.where(away[s], other, part), (-s) % width, 1)
                    stack.append(part)
            stack = jnp.concatenate(stack + [ones], axis=0)
            matrix = matrix_ref[c * 16 : c * 16 + 16, :]
            result = jnp.dot(matrix, stack, preferred_element_type=jnp.float32)
            conv[pl.ds(c, 16, stride=pitch(channels)), :] = result

    def put(n, change):
        changes[pl.ds(n, channels, stride=APART), :] = change

    blocks = [conv_row(conv, channels, i) for i in range(rows)]
    mlp(rows_ref, expand_ref, reduce_ref, 1, blocks, normed, inner, put)
    mask = main_mask[:rows, :]
    for c in range(channels):
        change = changes[c * APART : c * APART + rows, :]
        out_ref[c] = (mask * (main_ref[c].astype(jnp.float32) + change)).astype(jnp.bfloat16)


def per_device(
    nlat,
    nlon,
    field,
    land_mask,
    depth_kernel,
    depth_bias,
    norm_gain,
    norm_bias,
    w_expand,
    b_expand,
    w_reduce,
    b_reduce,
):
    channels, rows, width = field.shape
    layers, hidden = b_expand.shape
    bf16, f32 = jnp.bfloat16, jnp.float32
    edge = HALO * channels + 16

    def buffers(count):
        return [
            pltpu.VMEM((channels + 16, count * width), bf16),
            pltpu.VMEM((hidden, count * width), bf16),
        ]

    def pack(upper_if_even, after):
        return pl.pallas_call(
            functools.partial(pack_rows, upper_if_even),
            out_shape=jax.ShapeDtypeStruct((edge, width), bf16),
            in_specs=vmem(2) + [pl.BlockSpec(memory_space=pl.ANY)],
            out_specs=pl.BlockSpec(memory_space=pltpu.VMEM),
            scratch_shapes=[
                pltpu.VMEM((channels * APART, width), f32),
                pltpu.VMEM((rows, width), f32),
            ],
            compiler_params=params(),
            cost_estimate=cost(4e9),
        )(field, land_mask, after)

    begun = pl.pallas_call(
        first_step,
        out_shape=jax.ShapeDtypeStruct((8, 128), f32),
        out_specs=pl.BlockSpec(memory_space=pltpu.VMEM),
        compiler_params=params(),
        cost_estimate=cost(4e9),
    )()
    first = pack(True, begun)
    second_sent = pack(False, first)

    alone = nlat == 2

    def at(d, lat):
        return d * nlat + lat

    pairs = []
    for d in range(nlon):
        for low in range(1, nlat - 1, 2):
            pairs += [(at(d, low), at(d, low + 1)), (at(d, low + 1), at(d, low))]
        pairs.append((at(d, nlat - 1), at(nlon - 1 - d, nlat - 1)))
        pairs.append((at(d, 0), at(d ^ 1, 0)))
    second = lax.ppermute(second_sent, ("lon", "lat"), pairs)
    pairs = []
    for low in range(0, nlat - 1, 2):
        pairs += [(low, low + 1), (low + 1, low)]
    first = lax.ppermute(first, "lat", pairs)

    kernel = depth_kernel.transpose(2, 3, 0, 1).reshape(49, layers, channels)
    matrix_one, matrix_two, by_channel, expand = pl.pallas_call(
        weights,
        out_shape=[
            jax.ShapeDtypeStruct((channels * 24, 256), bf16),
            jax.ShapeDtypeStruct((channels * 16, 256), bf16),
            jax.ShapeDtypeStruct((layers, 3, channels, 128), f32),
            jax.ShapeDtypeStruct((layers, hidden, channels + 16), bf16),
        ],
        in_specs=vmem(7),
        out_specs=vmem(4),
        scratch_shapes=[
            pltpu.VMEM((channels * 24, 128), f32),
            pltpu.VMEM((channels * 24, 128), f32),
            pltpu.VMEM((128, 128), f32),
            pltpu.VMEM((128, hidden), f32),
        ],
        compiler_params=params(),
        cost_estimate=cost(2e9),
    )(
        kernel,
        depth_bias,
        norm_gain,
        norm_bias,
        w_expand.transpose(0, 2, 1),
        b_expand,
        b_reduce,
    )
    update = pl.pallas_call(
        inner_rows,
        out_shape=jax.ShapeDtypeStruct((channels * 24, width), f32),
        in_specs=vmem(5),
        out_specs=pl.BlockSpec(memory_space=pltpu.VMEM),
        scratch_shapes=[pltpu.VMEM((pitch(channels) * 16, width), f32)] + buffers(len(INNER)),
        compiler_params=params(),
        cost_estimate=cost(4e9),
    )(field, matrix_one, by_channel, expand, w_reduce)

    groups = channels // 8 + 1
    sent_rows = (channels // 16 + 1) * 32
    near_halo, near_mask, own_ends, wrap = pl.pallas_call(
        near_rows,
        out_shape=[
            jax.ShapeDtypeStruct((channels, 16, width), bf16),
            jax.ShapeDtypeStruct((16, width), f32),
            jax.ShapeDtypeStruct((groups * 16, width), bf16),
            jax.ShapeDtypeStruct((sent_rows, width), bf16),
        ],
        in_specs=vmem(3),
        out_specs=vmem(4),
        scratch_shapes=[
            pltpu.VMEM((channels * APART, width), f32),
            pltpu.VMEM((groups * 32, width), bf16),
        ],
        compiler_params=params(),
        cost_estimate=cost(1e9),
    )(field, land_mask, first)
    if alone:
        pairs = []
        for lat in range(nlat):
            pairs += [(lat, at(nlon - 1, lat)), (at(nlon - 1, lat), lat)]
            pairs += [(at(d, lat), at(d, 1 - lat)) for d in range(1, nlon - 1)]
        wrap = lax.ppermute(wrap, ("lon", "lat"), pairs)
    else:
        wrap = jnp.zeros_like(wrap)
    halo, halo_mask, ends, cross, own = pl.pallas_call(
        functools.partial(far_rows, alone),
        out_shape=[
            jax.ShapeDtypeStruct((channels, 16, width), bf16),
            jax.ShapeDtypeStruct((16, width), f32),
            jax.ShapeDtypeStruct((groups * 32, width), bf16),
            jax.ShapeDtypeStruct((sent_rows, width), bf16),
            jax.ShapeDtypeStruct((sent_rows, width), bf16),
        ],
        in_specs=vmem(5) + [pl.BlockSpec(memory_space=pl.ANY)],
        out_specs=vmem(5),
        scratch_shapes=[
            pltpu.VMEM((channels * APART, width), f32),
            pltpu.VMEM((16, width), f32),
        ],
        compiler_params=params(),
    )(second, second_sent, near_halo, near_mask, own_ends, update)
    core = pl.pallas_call(
        core_columns,
        out_shape=jax.ShapeDtypeStruct((sent_rows, width), bf16),
        in_specs=vmem(1) + [pl.BlockSpec(memory_space=pl.ANY)],
        out_specs=pl.BlockSpec(memory_space=pltpu.VMEM),
        compiler_params=params(),
    )(ends, cross)

    pairs = []
    for low in range(0, nlon, 2):
        pairs += [(low, low + 1), (low + 1, low)]
    core = lax.ppermute(core, "lon", pairs)
    pairs = []
    for lat in range(nlat):
        for low in range(1, nlon, 2):
            after = (low + 1) % nlon
            if after or not alone:
                pairs += [(at(low, lat), at(after, lat)), (at(after, lat), at(low, lat))]
            else:
                pairs += [(at(low, lat), at(low, 1 - lat)), (at(after, lat), at(after, 1 - lat))]
    cross = lax.ppermute(cross, ("lon", "lat"), pairs)

    update = pl.pallas_call(
        edge_rows,
        out_shape=jax.ShapeDtypeStruct((channels * 24, width), f32),
        in_specs=vmem(7),
        out_specs=pl.BlockSpec(memory_space=pltpu.VMEM),
        scratch_shapes=[pltpu.VMEM((pitch(channels) * 16, width), f32)] + buffers(len(EDGE)),
        input_output_aliases={6: 0},
        compiler_params=params(),
        cost_estimate=cost(4e9),
    )(field, halo, matrix_one, by_channel, expand, w_reduce, update)

    strips = pl.pallas_call(
        edge_columns,
        out_shape=jax.ShapeDtypeStruct((channels * 24, width), f32),
        in_specs=vmem(9),
        out_specs=pl.BlockSpec(memory_space=pltpu.VMEM),
        scratch_shapes=[pltpu.VMEM((pitch(channels) * 24, width), f32)] + buffers(3),
        compiler_params=params(),
    )(core, cross, wrap, own, ends, matrix_one, by_channel, expand, w_reduce)

    return pl.pallas_call(
        second_layer,
        out_shape=jax.ShapeDtypeStruct((channels, rows, width), bf16),
        in_specs=vmem(14),
        out_specs=pl.BlockSpec(memory_space=pltpu.VMEM),
        scratch_shapes=[
            pltpu.VMEM((channels, rows, width), bf16),
            pltpu.VMEM((pitch(channels) * 16, width), f32),
            pltpu.VMEM((channels * APART, width), f32),
        ]
        + buffers(rows),
        compiler_params=params(),
    )(
        field,
        land_mask,
        halo,
        halo_mask,
        core,
        cross,
        wrap,
        own,
        strips,
        update,
        matrix_two,
        by_channel,
        expand,
        w_reduce,
    )


def solution(mesh):
    placed = (P(None, "lat", "lon"), P("lat", "lon"), P(), P(), P(), P(), P(), P(), P(), P())
    return jax.shard_map(
        functools.partial(per_device, mesh.shape["lat"], mesh.shape["lon"]),
        mesh=mesh,
        in_specs=placed,
        out_specs=P(None, "lat", "lon"),
        check_vma=False,
    )
```

```python
import functools

import jax
import jax.numpy as jnp
from jax import lax
from jax.experimental import pallas as pl
from jax.experimental.pallas import tpu as pltpu
from jax.sharding import PartitionSpec as P


HALO = 6
APART = 24
VMEM_LIMIT = 20 * 1024 * 1024


def pitch(channels):
    return channels + 8


def params():
    return pltpu.CompilerParams(vmem_limit_bytes=VMEM_LIMIT)


def cost(flops):
    return pl.CostEstimate(flops=int(flops), bytes_accessed=1 << 20, transcendentals=0)


def vmem(count):
    return [pl.BlockSpec(memory_space=pltpu.VMEM)] * count


def lanes(shape):
    return lax.broadcasted_iota(jnp.int32, shape, len(shape) - 1)


def first_step(out_ref):
    out_ref[...] = jnp.zeros_like(out_ref)


def pack_rows(upper_if_even, field_ref, mask_ref, after_ref, out_ref, wide, wide_mask):
    del after_ref
    kept = 1.0 if upper_if_even else (lax.axis_index("lat") > 0).astype(jnp.float32)
    channels, rows, width = field_ref.shape
    even = lax.rem(lax.axis_index("lat"), 2) == 0
    take_upper = even if upper_if_even else jnp.logical_not(even)
    for c in range(channels):
        wide[c * APART : c * APART + rows, :] = field_ref[c].astype(jnp.float32)
    wide_mask[...] = mask_ref[...].astype(jnp.float32)
    for k in range(HALO):
        lower = wide[pl.ds(k, channels, stride=APART), :]
        upper = wide[pl.ds(rows - HALO + k, channels, stride=APART), :]
        at = pl.ds(k * channels, channels)
        out_ref[at, :] = (kept * jnp.where(take_upper, upper, lower)).astype(jnp.bfloat16)
    pad = jnp.zeros((16 - HALO, width), jnp.float32)
    lower = jnp.concatenate([wide_mask[0:HALO, :], pad], axis=0)
    upper = jnp.concatenate([wide_mask[rows - HALO : rows, :], pad], axis=0)
    at = pl.ds(HALO * channels, 16)
    out_ref[at, :] = (kept * jnp.where(take_upper, upper, lower)).astype(jnp.bfloat16)


def north_place(row):
    return jnp.where(row < 3, 4 + row, 9 + row)


def south_place(k):
    return k - 3 if k >= 3 else 8 + k


def place_rows(received_ref, is_north, turned, wide, mask_rows, channels):
    width = received_ref.shape[1]
    wide[...] = jnp.zeros_like(wide)
    mask_rows[...] = jnp.zeros_like(mask_rows)
    turn = None
    if turned is not None:
        sub = lax.broadcasted_iota(jnp.int32, (width, width), 0)
        target = lanes((width, width))
        turn = sub == jnp.where(turned, width - 1 - target, target)
        turn = turn.astype(jnp.float32).astype(jnp.bfloat16)

    def rows_at(start, count):
        block = received_ref[start : start + count, :]
        if turn is None:
            return block.astype(jnp.float32)
        return jnp.dot(block, turn, preferred_element_type=jnp.float32)

    masks = rows_at(HALO * channels, 16)
    for k in range(HALO):
        row = k if turned is None else jnp.where(turned, HALO - 1 - k, k)
        place = jnp.where(is_north, north_place(row), south_place(k))
        wide[pl.ds(place, channels, stride=APART), :] = rows_at(k * channels, channels)
        mask_rows[pl.ds(place, 1), :] = masks[k : k + 1, :]


def placed(wide, channels):
    blocks = wide[...].reshape(channels, APART, wide.shape[1])
    return blocks[:, :16, :].astype(jnp.bfloat16)


def pack_ends(blocks):
    rows, width = blocks[0].shape
    slot = lanes((rows, width)) // 16
    packed = jnp.zeros((rows, width), jnp.bfloat16)
    for j, block in enumerate(blocks):
        packed = jnp.where(slot == j, pltpu.roll(block, 16 * j + HALO, 1), packed)
    return packed


def channel_of(channels, group, slot):
    return slot // 2 * (channels // 4) + group * 2 + slot % 2


def over_wrap():
    lon = lax.axis_index("lon")
    return (lon == 0) | (lon == lax.axis_size("lon") - 1)


def near_rows(
    field_ref, mask_ref, first_ref, halo_ref, mask_rows, ends_ref, wrap_ref, wide, all_ends
):
    channels, rows, width = field_ref.shape
    even = lax.rem(lax.axis_index("lat"), 2) == 0
    place_rows(first_ref, even, None, wide, mask_rows, channels)
    halo_ref[...] = placed(wide, channels)
    groups = channels // 8
    for g in range(groups):
        blocks = [field_ref[channel_of(channels, g, j)] for j in range(8)]
        ends_ref[g * 16 : g * 16 + 16, :] = pack_ends(blocks)
    mask = mask_ref[...].astype(jnp.float32).astype(jnp.bfloat16)
    ends_ref[groups * 16 :, :] = pack_ends([mask])
    wrap_ref[...] = jnp.zeros_like(wrap_ref)

    @pl.when(over_wrap())
    def _():
        join_ends(ends_ref, halo_ref, mask_rows, all_ends)
        pack_side(all_ends, wrap_ref, lax.rem(lax.axis_index("lon"), 2) == 1)


def join_ends(own_ends_ref, halo_ref, mask_rows, ends_ref):
    channels = halo_ref.shape[0]
    groups = channels // 8
    for g in range(groups + 1):
        if g < groups:
            blocks = [halo_ref[channel_of(channels, g, j)] for j in range(8)]
        else:
            blocks = [mask_rows[...].astype(jnp.bfloat16)]
        own = jnp.zeros((16, halo_ref.shape[2]), jnp.bfloat16)
        if own_ends_ref is not None:
            own = own_ends_ref[g * 16 : g * 16 + 16, :]
        ends_ref[g * 32 : g * 32 + 16, :] = own
        ends_ref[g * 32 + 16 : g * 32 + 32, :] = pack_ends(blocks)


def pack_side(ends_ref, out_ref, to_east):
    width = ends_ref.shape[1]
    groups = ends_ref.shape[0] // 32 - 1
    lower = lanes((32, width)) % 16 < 8
    for m in range(groups // 2 + 1):
        n = m if m < groups // 2 else groups
        one = ends_ref[n * 32 : n * 32 + 32, :]
        one = jnp.where(to_east, one, pltpu.roll(one, width - HALO, 1))
        if n < groups:
            two = ends_ref[(n + groups // 2) * 32 : (n + groups // 2) * 32 + 32, :]
            two = jnp.where(to_east, pltpu.roll(two, 8, 1), pltpu.roll(two, 8 - HALO, 1))
            one = jnp.where(lower, one, two)
        out_ref[m * 32 : m * 32 + 32, :] = one


def far_rows(
    alone,
    second_ref,
    near_halo_ref,
    near_mask_ref,
    own_ends_ref,
    after_ref,
    halo_ref,
    halo_mask_ref,
    ends_ref,
    cross_ref,
    wide,
    mask_rows,
):
    del after_ref
    channels = halo_ref.shape[0]
    lat = lax.axis_index("lat")
    odd = lax.rem(lat, 2) == 1
    lon_odd = lax.rem(lax.axis_index("lon"), 2) == 1
    folded = lat == lax.axis_size("lat") - 1
    place_rows(second_ref, odd, folded, wide, mask_rows, channels)
    halo_ref[...] = near_halo_ref[...] + placed(wide, channels)
    halo_mask_ref[...] = near_mask_ref[...] + mask_rows[...]
    join_ends(own_ends_ref, halo_ref, halo_mask_ref, ends_ref)
    pack_side(ends_ref, cross_ref, lon_odd)
    if alone:

        @pl.when(over_wrap())
        def _():
            cross_ref[...] = jnp.zeros_like(cross_ref)


def mirrored_columns(alone, sent_ref, after_ref, own_ref, wide, mask_rows, halo, ends):
    del after_ref
    channels = halo.shape[0]
    lat = lax.axis_index("lat")
    folded = lat == lax.axis_size("lat") - 1
    own_ref[...] = jnp.zeros_like(own_ref)
    if alone:

        @pl.when(folded & over_wrap())
        def _():
            odd = lax.rem(lat, 2) == 1
            place_rows(sent_ref, odd, folded, wide, mask_rows, channels)
            halo[...] = placed(wide, channels)
            join_ends(None, halo, mask_rows, ends)
            pack_side(ends, own_ref, lax.rem(lax.axis_index("lon"), 2) == 0)


def core_columns(ends_ref, after_ref, core_ref):
    del after_ref
    pack_side(ends_ref, core_ref, lax.rem(lax.axis_index("lon"), 2) == 0)


def in_row(place, first_layer):
    none = jnp.full_like(place, 1000)
    row = jnp.where(place < 16, place, none)
    row = jnp.where((place >= 16) & (place < 19), place - 19, row)
    row = jnp.where((place >= 20) & (place < 23), place - 4, row)
    if first_layer:
        row = jnp.where((place >= 24) & (place < 27), place - 30, row)
        row = jnp.where((place >= 28) & (place < 31), place - 9, row)
    return row


EDGE = (-3, -2, -1, 16, 17, 18, 0, 1, 2, 13, 14, 15)
INNER = (3, 4, 5, 6, 7, 8, 9, 10, 11, 12)


def place_of(row):
    if row < 0:
        return row + 19
    return row if row < 16 else row + 4


def conv_matrices(table, out_ref, left, right, row, rows_out):
    channels, taps = table.shape
    count = len(rows_out)
    folded = lax.axis_index("lat") == lax.axis_size("lat") - 1
    k = lanes((1, 256))
    shift = k // 32
    place = k - shift * 32
    tap = lax.broadcasted_iota(jnp.int32, (taps, 256), 0)
    row = row(place)
    for i, here in enumerate(rows_out):
        if here is None:
            wanted = jnp.full_like(k, -1)
        else:
            a = row - here + 3
            inside = (a >= 0) & (a <= 6) & (shift < 7)
            wanted = a * 7 + shift
            if here > 15:
                wanted = jnp.where(folded, 48 - wanted, wanted)
            wanted = jnp.where(inside, wanted, -1)
            wanted = jnp.where((shift == 7) & (place < 3), 49 + place, wanted)
        picks = (tap == wanted).astype(jnp.float32).astype(jnp.bfloat16)
        matrix = jnp.dot(table, picks, preferred_element_type=jnp.float32)
        left[pl.ds(i, channels, stride=count), :] = matrix[:, :128]
        right[pl.ds(i, channels, stride=count), :] = matrix[:, 128:]
    size = channels * count
    out_ref[:, :128] = left[:size, :].astype(jnp.bfloat16)
    out_ref[:, 128:] = right[:size, :].astype(jnp.bfloat16)


def split_bias(bias):
    high = bias.astype(jnp.bfloat16).astype(jnp.float32)
    rest = bias - high
    mid = rest.astype(jnp.bfloat16).astype(jnp.float32)
    return high, mid, rest - mid


def weights(
    kernel_ref,
    bias_ref,
    gain_ref,
    norm_bias_ref,
    expand_ref,
    expand_bias_ref,
    reduce_bias_ref,
    one_ref,
    two_ref,
    rows_ref,
    expand_out_ref,
    left,
    right,
    turn,
    tall,
):
    taps, layers, channels = kernel_ref.shape
    hidden = expand_ref.shape[2]
    turn[...] = jnp.zeros_like(turn)
    tall[...] = jnp.zeros_like(tall)
    for layer in range(layers):
        for tap in range(taps):
            turn[tap : tap + 1, :channels] = kernel_ref[tap, layer : layer + 1, :]
        parts = split_bias(bias_ref[layer : layer + 1, :])
        for n, part in enumerate(parts):
            turn[taps + n : taps + n + 1, :channels] = part
        table = turn[...].T[:channels, :64].astype(jnp.bfloat16)
        if layer == 0:
            every = EDGE + INNER + (None,) * 2
            row = functools.partial(in_row, first_layer=True)
            conv_matrices(table, one_ref, left, right, row, every)
        else:
            row = functools.partial(in_row, first_layer=False)
            conv_matrices(table, two_ref, left, right, row, tuple(range(16)))
    for layer in range(layers):
        for n, ref in enumerate((gain_ref, norm_bias_ref, reduce_bias_ref)):
            turn[:, :channels] = jnp.broadcast_to(ref[layer : layer + 1, :], (128, channels))
            rows_ref[layer, n] = turn[...].T[:channels, :]
        tall[:channels, :] = expand_ref[layer].astype(jnp.float32) * 0.5
        parts = split_bias(expand_bias_ref[layer : layer + 1, :] * 0.5)
        for n, part in enumerate(parts):
            tall[channels + n : channels + n + 1, :] = part
        for n in range(hidden // 128):
            piece = tall[:, n * 128 : (n + 1) * 128].T
            at = pl.ds(n * 128, 128)
            expand_out_ref[layer, at, :] = piece[:, : channels + 16].astype(jnp.bfloat16)


ERF = (7.97869712e-01, 3.63922860e-02, -8.78263977e-05, -3.66934787e-05, 1.42500782e-06)


def gelu_of_double(half):
    square = half * half
    total = jnp.full_like(half, 2.0 * 4.0 ** (len(ERF) - 1) * ERF[-1])
    for power in range(len(ERF) - 2, -1, -1):
        total = total * square + jnp.full_like(half, 2.0 * 4.0**power * ERF[power])
    return half * jnp.tanh(half * total) + half


def norm(rows_ref, layer, cells):
    average = jnp.mean(cells, axis=0, keepdims=True)
    centered = cells - average
    variance = jnp.mean(centered * centered, axis=0, keepdims=True)
    scaled = centered * lax.rsqrt(variance + 1e-06)
    return (scaled * rows_ref[layer, 0] + rows_ref[layer, 1]).astype(jnp.bfloat16)


def mlp(rows_ref, expand_ref, reduce_ref, layer, blocks, normed_ref, inner_ref, put):
    count = len(blocks)
    channels, width = rows_ref.shape[2:]
    hidden = inner_ref.shape[0]
    wide = count * width
    normed_ref[channels:, :wide] = jnp.ones((16, wide), jnp.bfloat16)
    for n, block in enumerate(blocks):
        at = slice(n * width, (n + 1) * width)
        normed_ref[:channels, at] = norm(rows_ref, layer, block())
    tiles = [slice(n, min(n + 2 * width, wide)) for n in range(0, wide, 2 * width)]
    for at in tiles:
        normed = normed_ref[:, at]
        for part in range(0, hidden, 128):
            matrix = expand_ref[layer, part : part + 128, :]
            half = jnp.dot(matrix, normed, preferred_element_type=jnp.float32)
            for k in range(0, 128, 16):
                values = gelu_of_double(half[k : k + 16, :].astype(jnp.bfloat16))
                inner_ref[part + k : part + k + 16, at] = values
    extra = rows_ref[layer, 2]
    for t, at in enumerate(tiles):
        change = jnp.dot(reduce_ref[layer], inner_ref[:, at], preferred_element_type=jnp.float32)
        for n in range((at.stop - at.start) // width):
            put(t * 2 + n, change[:, n * width : (n + 1) * width] + extra)


def columns_stack(block, ones):
    width = block.shape[1]
    stack = [block if s == 0 else pltpu.roll(block, (-s) % width, 1) for s in range(-3, 4)]
    return jnp.concatenate(stack + [ones], axis=0)


def conv_rows(matrix_ref, stack_of, conv, channels, stride, first, count):
    ones = jnp.ones((matrix_ref.shape[1] // 8, 128), jnp.bfloat16)

    def step(c, carry):
        matrix = matrix_ref[pl.ds(pl.multiple_of(c * stride + first, 8), count), :]
        result = jnp.dot(matrix, stack_of(c, ones), preferred_element_type=jnp.float32)
        conv[pl.ds(c, count, stride=pitch(channels)), :] = result
        return carry

    lax.fori_loop(0, channels, step, 0, unroll=channels)


def conv_row(conv, channels, i):
    start = i * pitch(channels)
    return lambda: conv[start : start + channels, :]


def inner_rows(
    field_ref, matrix_ref, rows_ref, expand_ref, reduce_ref, update_ref, conv, normed, inner
):
    channels, rows, width = field_ref.shape
    none = jnp.zeros((16, width), jnp.bfloat16)

    def stack_of(c, ones):
        return columns_stack(jnp.concatenate([field_ref[c], none], axis=0), ones)

    conv_rows(matrix_ref, stack_of, conv, channels, 24, 8, 16)

    def put(n, change):
        update_ref[pl.ds(INNER[n], channels, stride=24), :] = change

    blocks = [conv_row(conv, channels, i + len(EDGE) - 8) for i in range(len(INNER))]
    mlp(rows_ref, expand_ref, reduce_ref, 0, blocks, normed, inner, put)


def edge_rows(
    field_ref,
    halo_ref,
    matrix_ref,
    rows_ref,
    expand_ref,
    reduce_ref,
    old_ref,
    update_ref,
    conv,
    normed,
    inner,
):
    del old_ref
    channels, _, width = field_ref.shape

    def stack_of(c, ones):
        return columns_stack(jnp.concatenate([field_ref[c], halo_ref[c]], axis=0), ones)

    conv_rows(matrix_ref, stack_of, conv, channels, 24, 0, 16)
    for empty in (19, 23):
        update_ref[pl.ds(empty, channels, stride=24), :] = jnp.zeros((channels, width), jnp.float32)

    def put(n, change):
        update_ref[pl.ds(place_of(EDGE[n]), channels, stride=24), :] = change

    blocks = [conv_row(conv, channels, i) for i in range(len(EDGE))]
    mlp(rows_ref, expand_ref, reduce_ref, 0, blocks, normed, inner, put)


def neighbours(core_ref, cross_refs, group, groups):
    width = core_ref.shape[1]
    half = groups // 2
    m, upper = (half, 0) if group == groups else (group % half, group // half)
    core = core_ref[m * 32 : m * 32 + 32, :]
    cross = sum(ref[m * 32 : m * 32 + 32, :] for ref in cross_refs)
    lon_even = lax.rem(lax.axis_index("lon"), 2) == 0
    east = jnp.where(lon_even, core, cross)
    west = jnp.where(lon_even, cross, core)
    east = pltpu.roll(east, (HALO - 8 * upper) % width, 1)
    return east, pltpu.roll(west, width - 8, 1) if upper else west


def edge_columns(
    core_ref,
    cross_ref,
    wrap_ref,
    own_ref,
    ends_ref,
    matrix_ref,
    rows_ref,
    expand_ref,
    reduce_ref,
    strips,
    conv,
    normed,
    inner,
):
    channels, width = rows_ref.shape[2:]
    quarter = channels // 4
    groups = channels // 8
    lane32 = lanes((32, width))
    first_six = lane32 % 16 < HALO
    first_twelve = lane32 % 32 < 2 * HALO
    ones = jnp.ones((32, width), jnp.bfloat16)
    for g in range(groups):
        at = slice(g * 32, g * 32 + 32)
        east, west = neighbours(core_ref, (cross_ref, wrap_ref, own_ref), g, groups)
        own = ends_ref[at, :]
        at_west = jnp.where(first_six, west, own)
        at_east = jnp.where(first_six, own, east)
        for t in range(2):
            left = pltpu.roll(at_west, width - 16, 1) if t else at_west
            right = pltpu.roll(at_east, (2 * HALO - 16 * t) % width, 1)
            block = jnp.where(first_twelve, left, right)
            some = [channel_of(channels, g, 2 * n + t) for n in range(4)]
            matrix = jnp.concatenate(
                [matrix_ref[c * 24 : c * 24 + 24, :] for c in some], axis=0
            )
            stack = columns_stack(block, ones)
            result = jnp.dot(matrix, stack, preferred_element_type=jnp.float32)
            for n, c in enumerate(some):
                conv[pl.ds(c, 24, stride=pitch(channels)), :] = result[n * 24 : n * 24 + 24, :]

    order = {place_of(row): i for i, row in enumerate(EDGE + INNER)}
    lane = lanes((quarter, width))
    starts = [32 * (q // 2) + 6 * (q % 2) for q in range(8)]
    inside = [
        ((lane >= s + 3) & (lane < s + 9)) | ((lane >= s + 15) & (lane < s + 21)) for s in starts
    ]
    packs = []
    for p in range(3):
        parts = []
        for n in range(4):
            packed = jnp.zeros((quarter, width), jnp.float32)
            for q, start in enumerate(starts):
                if p * 8 + q in order:
                    row = order[p * 8 + q] * pitch(channels) + n * quarter
                    block = conv[row : row + quarter, :]
                    block = pltpu.roll(block, (start - 32 * n) % width, 1)
                    packed = jnp.where(inside[q], block, packed)
            parts.append(packed)
        packs.append(jnp.concatenate(parts, axis=0))

    def put(p, change):
        for q, start in enumerate(starts):
            near = pltpu.roll(change, (width - 6 - start) % width, 1)
            strips[pl.ds(p * 8 + q, channels, stride=24), :] = near

    blocks = [functools.partial(lambda block: block, packed) for packed in packs]
    mlp(rows_ref, expand_ref, reduce_ref, 0, blocks, normed, inner, put)


def second_layer(
    field_ref,
    mask_ref,
    halo_ref,
    halo_mask_ref,
    core_ref,
    cross_ref,
    wrap_ref,
    own_ref,
    strips,
    update_ref,
    matrix_ref,
    rows_ref,
    expand_ref,
    reduce_ref,
    out_ref,
    main_ref,
    conv,
    changes,
    normed,
    inner,
):
    channels, rows, width = out_ref.shape
    groups = channels // 8
    lane32 = lanes((32, width))
    lane24 = lanes((24, width))
    first_six = lane32 % 16 < HALO

    def beside_of(received, slot):
        beside = pltpu.roll(received, (width - HALO - 16 * slot) % width, 1)
        return beside.astype(jnp.float32)[0:24, :]

    def received(g):
        east, west = neighbours(core_ref, (cross_ref, wrap_ref, own_ref), g, groups)
        return jnp.where(first_six, west, east)

    main_mask = jnp.concatenate(
        [mask_ref[...].astype(jnp.float32), halo_mask_ref[0:8, :]], axis=0
    )
    side_mask = beside_of(received(groups), 0)
    low = lane24 < 3
    high = lane24 >= width - 3
    blank = jnp.zeros((8, width), jnp.float32)
    ones = jnp.ones((32, width), jnp.bfloat16)
    lane16 = lanes((16, width))
    away = {s: lane16 < s if s > 0 else lane16 >= width + s for s in range(-3, 4) if s}

    def halves(block):
        low_rows = block[:16, :].astype(jnp.bfloat16)
        return low_rows, jnp.concatenate([block[16:, :], blank], axis=0).astype(jnp.bfloat16)

    for g in range(groups):
        both = received(g)
        for j in range(8):
            c = channel_of(channels, g, j)
            near = strips[c * 24 : c * 24 + 24, :]
            far = pltpu.roll(near, width - 2 * HALO, 1)
            change = update_ref[c * 24 : c * 24 + 24, :]
            change = jnp.where(low, near, jnp.where(high, far, change))
            own = field_ref[c].astype(jnp.float32)
            halo = halo_ref[c].astype(jnp.float32)[:8, :]
            main = halves(main_mask * (jnp.concatenate([own, halo], axis=0) + change))
            main_ref[c] = main[0]
            change = jnp.where(high, near, far)
            beside = halves(side_mask * (beside_of(both, j) + change))
            stack = []
            for s in range(-3, 4):
                for part, other in zip(main, beside):
                    if s:
                        part = pltpu.roll(jnp.where(away[s], other, part), (-s) % width, 1)
                    stack.append(part)
            stack = jnp.concatenate(stack + [ones], axis=0)
            matrix = matrix_ref[c * 16 : c * 16 + 16, :]
            result = jnp.dot(matrix, stack, preferred_element_type=jnp.float32)
            conv[pl.ds(c, 16, stride=pitch(channels)), :] = result

    def put(n, change):
        changes[pl.ds(n, channels, stride=APART), :] = change

    blocks = [conv_row(conv, channels, i) for i in range(rows)]
    mlp(rows_ref, expand_ref, reduce_ref, 1, blocks, normed, inner, put)
    mask = main_mask[:rows, :]
    for c in range(channels):
        change = changes[c * APART : c * APART + rows, :]
        out_ref[c] = (mask * (main_ref[c].astype(jnp.float32) + change)).astype(jnp.bfloat16)


def per_device(
    nlat,
    nlon,
    field,
    land_mask,
    depth_kernel,
    depth_bias,
    norm_gain,
    norm_bias,
    w_expand,
    b_expand,
    w_reduce,
    b_reduce,
):
    channels, rows, width = field.shape
    layers, hidden = b_expand.shape
    bf16, f32 = jnp.bfloat16, jnp.float32
    edge = HALO * channels + 16

    def buffers(count):
        return [
            pltpu.VMEM((channels + 16, count * width), bf16),
            pltpu.VMEM((hidden, count * width), bf16),
        ]

    def pack(upper_if_even, after):
        return pl.pallas_call(
            functools.partial(pack_rows, upper_if_even),
            out_shape=jax.ShapeDtypeStruct((edge, width), bf16),
            in_specs=vmem(2) + [pl.BlockSpec(memory_space=pl.ANY)],
            out_specs=pl.BlockSpec(memory_space=pltpu.VMEM),
            scratch_shapes=[
                pltpu.VMEM((channels * APART, width), f32),
                pltpu.VMEM((rows, width), f32),
            ],
            compiler_params=params(),
            cost_estimate=cost(4e9),
        )(field, land_mask, after)

    begun = pl.pallas_call(
        first_step,
        out_shape=jax.ShapeDtypeStruct((8, 128), f32),
        out_specs=pl.BlockSpec(memory_space=pltpu.VMEM),
        compiler_params=params(),
        cost_estimate=cost(4e9),
    )()
    first = pack(True, begun)
    second_sent = pack(False, first)

    alone = nlat == 2

    def at(d, lat):
        return d * nlat + lat

    pairs = []
    for d in range(nlon):
        for low in range(1, nlat - 1, 2):
            pairs += [(at(d, low), at(d, low + 1)), (at(d, low + 1), at(d, low))]
        pairs.append((at(d, nlat - 1), at(nlon - 1 - d, nlat - 1)))
        pairs.append((at(d, 0), at(d ^ 1, 0)))
    second = lax.ppermute(second_sent, ("lon", "lat"), pairs)
    pairs = []
    for low in range(0, nlat - 1, 2):
        pairs += [(low, low + 1), (low + 1, low)]
    first = lax.ppermute(first, "lat", pairs)

    kernel = depth_kernel.transpose(2, 3, 0, 1).reshape(49, layers, channels)
    matrix_one, matrix_two, by_channel, expand = pl.pallas_call(
        weights,
        out_shape=[
            jax.ShapeDtypeStruct((channels * 24, 256), bf16),
            jax.ShapeDtypeStruct((channels * 16, 256), bf16),
            jax.ShapeDtypeStruct((layers, 3, channels, 128), f32),
            jax.ShapeDtypeStruct((layers, hidden, channels + 16), bf16),
        ],
        in_specs=vmem(7),
        out_specs=vmem(4),
        scratch_shapes=[
            pltpu.VMEM((channels * 24, 128), f32),
            pltpu.VMEM((channels * 24, 128), f32),
            pltpu.VMEM((128, 128), f32),
            pltpu.VMEM((128, hidden), f32),
        ],
        compiler_params=params(),
        cost_estimate=cost(2e9),
    )(
        kernel,
        depth_bias,
        norm_gain,
        norm_bias,
        w_expand.transpose(0, 2, 1),
        b_expand,
        b_reduce,
    )
    update = pl.pallas_call(
        inner_rows,
        out_shape=jax.ShapeDtypeStruct((channels * 24, width), f32),
        in_specs=vmem(5),
        out_specs=pl.BlockSpec(memory_space=pltpu.VMEM),
        scratch_shapes=[pltpu.VMEM((pitch(channels) * 16, width), f32)] + buffers(len(INNER)),
        compiler_params=params(),
        cost_estimate=cost(4e9),
    )(field, matrix_one, by_channel, expand, w_reduce)

    groups = channels // 8 + 1
    sent_rows = (channels // 16 + 1) * 32
    near_halo, near_mask, own_ends, wrap = pl.pallas_call(
        near_rows,
        out_shape=[
            jax.ShapeDtypeStruct((channels, 16, width), bf16),
            jax.ShapeDtypeStruct((16, width), f32),
            jax.ShapeDtypeStruct((groups * 16, width), bf16),
            jax.ShapeDtypeStruct((sent_rows, width), bf16),
        ],
        in_specs=vmem(3),
        out_specs=vmem(4),
        scratch_shapes=[
            pltpu.VMEM((channels * APART, width), f32),
            pltpu.VMEM((groups * 32, width), bf16),
        ],
        compiler_params=params(),
        cost_estimate=cost(1e9),
    )(field, land_mask, first)
    if alone:
        pairs = []
        for lat in range(nlat):
            pairs += [(lat, at(nlon - 1, lat)), (at(nlon - 1, lat), lat)]
            pairs += [(at(d, lat), at(d, 1 - lat)) for d in range(1, nlon - 1)]
        wrap = lax.ppermute(wrap, ("lon", "lat"), pairs)
    else:
        wrap = jnp.zeros_like(wrap)
    halo, halo_mask, ends, cross = pl.pallas_call(
        functools.partial(far_rows, alone),
        out_shape=[
            jax.ShapeDtypeStruct((channels, 16, width), bf16),
            jax.ShapeDtypeStruct((16, width), f32),
            jax.ShapeDtypeStruct((groups * 32, width), bf16),
            jax.ShapeDtypeStruct((sent_rows, width), bf16),
        ],
        in_specs=vmem(4) + [pl.BlockSpec(memory_space=pl.ANY)],
        out_specs=vmem(4),
        scratch_shapes=[
            pltpu.VMEM((channels * APART, width), f32),
            pltpu.VMEM((16, width), f32),
        ],
        compiler_params=params(),
    )(second, near_halo, near_mask, own_ends, update)
    core = pl.pallas_call(
        core_columns,
        out_shape=jax.ShapeDtypeStruct((sent_rows, width), bf16),
        in_specs=vmem(1) + [pl.BlockSpec(memory_space=pl.ANY)],
        out_specs=pl.BlockSpec(memory_space=pltpu.VMEM),
        compiler_params=params(),
    )(ends, cross)

    own = pl.pallas_call(
        functools.partial(mirrored_columns, alone),
        out_shape=jax.ShapeDtypeStruct((sent_rows, width), bf16),
        in_specs=vmem(1) + [pl.BlockSpec(memory_space=pl.ANY)],
        out_specs=pl.BlockSpec(memory_space=pltpu.VMEM),
        scratch_shapes=[
            pltpu.VMEM((channels * APART, width), f32),
            pltpu.VMEM((16, width), f32),
            pltpu.VMEM((channels, 16, width), bf16),
            pltpu.VMEM((groups * 32, width), bf16),
        ],
        compiler_params=params(),
    )(second_sent, core)

    pairs = []
    for low in range(0, nlon, 2):
        pairs += [(low, low + 1), (low + 1, low)]
    core = lax.ppermute(core, "lon", pairs)
    pairs = []
    for lat in range(nlat):
        for low in range(1, nlon, 2):
            after = (low + 1) % nlon
            if after or not alone:
                pairs += [(at(low, lat), at(after, lat)), (at(after, lat), at(low, lat))]
            else:
                pairs += [(at(low, lat), at(low, 1 - lat)), (at(after, lat), at(after, 1 - lat))]
    cross = lax.ppermute(cross, ("lon", "lat"), pairs)

    update = pl.pallas_call(
        edge_rows,
        out_shape=jax.ShapeDtypeStruct((channels * 24, width), f32),
        in_specs=vmem(7),
        out_specs=pl.BlockSpec(memory_space=pltpu.VMEM),
        scratch_shapes=[pltpu.VMEM((pitch(channels) * 16, width), f32)] + buffers(len(EDGE)),
        input_output_aliases={6: 0},
        compiler_params=params(),
        cost_estimate=cost(4e9),
    )(field, halo, matrix_one, by_channel, expand, w_reduce, update)

    strips = pl.pallas_call(
        edge_columns,
        out_shape=jax.ShapeDtypeStruct((channels * 24, width), f32),
        in_specs=vmem(9),
        out_specs=pl.BlockSpec(memory_space=pltpu.VMEM),
        scratch_shapes=[pltpu.VMEM((pitch(channels) * 24, width), f32)] + buffers(3),
        compiler_params=params(),
    )(core, cross, wrap, own, ends, matrix_one, by_channel, expand, w_reduce)

    return pl.pallas_call(
        second_layer,
        out_shape=jax.ShapeDtypeStruct((channels, rows, width), bf16),
        in_specs=vmem(14),
        out_specs=pl.BlockSpec(memory_space=pltpu.VMEM),
        scratch_shapes=[
            pltpu.VMEM((channels, rows, width), bf16),
            pltpu.VMEM((pitch(channels) * 16, width), f32),
            pltpu.VMEM((channels * APART, width), f32),
        ]
        + buffers(rows),
        compiler_params=params(),
    )(
        field,
        land_mask,
        halo,
        halo_mask,
        core,
        cross,
        wrap,
        own,
        strips,
        update,
        matrix_two,
        by_channel,
        expand,
        w_reduce,
    )


def solution(mesh):
    placed = (P(None, "lat", "lon"), P("lat", "lon"), P(), P(), P(), P(), P(), P(), P(), P())
    return jax.shard_map(
        functools.partial(per_device, mesh.shape["lat"], mesh.shape["lon"]),
        mesh=mesh,
        in_specs=placed,
        out_specs=P(None, "lat", "lon"),
        check_vma=False,
    )
```

```python
import functools

import jax
import jax.numpy as jnp
from jax import lax
from jax.experimental import pallas as pl
from jax.experimental.pallas import tpu as pltpu
from jax.sharding import PartitionSpec as P


HALO = 6
APART = 24
VMEM_LIMIT = 20 * 1024 * 1024


def pitch(channels):
    return channels + 8


def params():
    return pltpu.CompilerParams(vmem_limit_bytes=VMEM_LIMIT)


def cost(flops):
    return pl.CostEstimate(flops=int(flops), bytes_accessed=1 << 20, transcendentals=0)


def vmem(count):
    return [pl.BlockSpec(memory_space=pltpu.VMEM)] * count


def lanes(shape):
    return lax.broadcasted_iota(jnp.int32, shape, len(shape) - 1)


def first_step(out_ref):
    out_ref[...] = jnp.zeros_like(out_ref)


def pack_rows(upper_if_even, field_ref, mask_ref, after_ref, out_ref, wide, wide_mask):
    del after_ref
    kept = 1.0 if upper_if_even else (lax.axis_index("lat") > 0).astype(jnp.float32)
    channels, rows, width = field_ref.shape
    even = lax.rem(lax.axis_index("lat"), 2) == 0
    take_upper = even if upper_if_even else jnp.logical_not(even)
    for c in range(channels):
        wide[c * APART : c * APART + rows, :] = field_ref[c].astype(jnp.float32)
    wide_mask[...] = mask_ref[...].astype(jnp.float32)
    for k in range(HALO):
        lower = wide[pl.ds(k, channels, stride=APART), :]
        upper = wide[pl.ds(rows - HALO + k, channels, stride=APART), :]
        at = pl.ds(k * channels, channels)
        out_ref[at, :] = (kept * jnp.where(take_upper, upper, lower)).astype(jnp.bfloat16)
    pad = jnp.zeros((16 - HALO, width), jnp.float32)
    lower = jnp.concatenate([wide_mask[0:HALO, :], pad], axis=0)
    upper = jnp.concatenate([wide_mask[rows - HALO : rows, :], pad], axis=0)
    at = pl.ds(HALO * channels, 16)
    out_ref[at, :] = (kept * jnp.where(take_upper, upper, lower)).astype(jnp.bfloat16)


def north_place(row):
    return jnp.where(row < 3, 4 + row, 9 + row)


def south_place(k):
    return k - 3 if k >= 3 else 8 + k


def place_rows(received_ref, is_north, turned, wide, mask_rows, channels):
    width = received_ref.shape[1]
    wide[...] = jnp.zeros_like(wide)
    mask_rows[...] = jnp.zeros_like(mask_rows)
    turn = None
    if turned is not None:
        sub = lax.broadcasted_iota(jnp.int32, (width, width), 0)
        target = lanes((width, width))
        turn = sub == jnp.where(turned, width - 1 - target, target)
        turn = turn.astype(jnp.float32).astype(jnp.bfloat16)

    def rows_at(start, count):
        block = received_ref[start : start + count, :]
        if turn is None:
            return block.astype(jnp.float32)
        return jnp.dot(block, turn, preferred_element_type=jnp.float32)

    masks = rows_at(HALO * channels, 16)
    for k in range(HALO):
        row = k if turned is None else jnp.where(turned, HALO - 1 - k, k)
        place = jnp.where(is_north, north_place(row), south_place(k))
        wide[pl.ds(place, channels, stride=APART), :] = rows_at(k * channels, channels)
        mask_rows[pl.ds(place, 1), :] = masks[k : k + 1, :]


def placed(wide, channels):
    blocks = wide[: channels * APART, :].reshape(channels, APART, wide.shape[1])
    return blocks[:, :16, :].astype(jnp.bfloat16)


def pack_ends(blocks):
    rows, width = blocks[0].shape
    slot = lanes((rows, width)) // 16
    packed = jnp.zeros((rows, width), jnp.bfloat16)
    for j, block in enumerate(blocks):
        packed = jnp.where(slot == j, pltpu.roll(block, 16 * j + HALO, 1), packed)
    return packed


def channel_of(channels, group, slot):
    return slot // 2 * (channels // 4) + group * 2 + slot % 2


def over_wrap():
    lon = lax.axis_index("lon")
    return (lon == 0) | (lon == lax.axis_size("lon") - 1)


def near_rows(
    field_ref, mask_ref, first_ref, halo_ref, mask_rows, ends_ref, wrap_ref, wide, all_ends
):
    channels, rows, width = field_ref.shape
    even = lax.rem(lax.axis_index("lat"), 2) == 0
    place_rows(first_ref, even, None, wide, mask_rows, channels)
    halo_ref[...] = placed(wide, channels)
    groups = channels // 8
    for g in range(groups):
        blocks = [field_ref[channel_of(channels, g, j)] for j in range(8)]
        ends_ref[g * 16 : g * 16 + 16, :] = pack_ends(blocks)
    mask = mask_ref[...].astype(jnp.float32).astype(jnp.bfloat16)
    ends_ref[groups * 16 :, :] = pack_ends([mask])
    wrap_ref[...] = jnp.zeros_like(wrap_ref)

    @pl.when(over_wrap())
    def _():
        join_ends(ends_ref, halo_ref, mask_rows, all_ends)
        pack_side(all_ends, wrap_ref, lax.rem(lax.axis_index("lon"), 2) == 1)


def join_ends(own_ends_ref, halo_ref, mask_rows, ends_ref):
    channels = halo_ref.shape[0]
    groups = channels // 8
    for g in range(groups + 1):
        if g < groups:
            blocks = [halo_ref[channel_of(channels, g, j)] for j in range(8)]
        else:
            blocks = [mask_rows[...].astype(jnp.bfloat16)]
        own = jnp.zeros((16, halo_ref.shape[2]), jnp.bfloat16)
        if own_ends_ref is not None:
            own = own_ends_ref[g * 16 : g * 16 + 16, :]
        ends_ref[g * 32 : g * 32 + 16, :] = own
        ends_ref[g * 32 + 16 : g * 32 + 32, :] = pack_ends(blocks)


def pack_side(ends_ref, out_ref, to_east):
    width = ends_ref.shape[1]
    groups = ends_ref.shape[0] // 32 - 1
    lower = lanes((32, width)) % 16 < 8
    for m in range(groups // 2 + 1):
        n = m if m < groups // 2 else groups
        one = ends_ref[n * 32 : n * 32 + 32, :]
        one = jnp.where(to_east, one, pltpu.roll(one, width - HALO, 1))
        if n < groups:
            two = ends_ref[(n + groups // 2) * 32 : (n + groups // 2) * 32 + 32, :]
            two = jnp.where(to_east, pltpu.roll(two, 8, 1), pltpu.roll(two, 8 - HALO, 1))
            one = jnp.where(lower, one, two)
        out_ref[m * 32 : m * 32 + 32, :] = one


def far_rows(
    alone,
    second_ref,
    near_halo_ref,
    near_mask_ref,
    own_ends_ref,
    after_ref,
    halo_ref,
    halo_mask_ref,
    ends_ref,
    cross_ref,
    wide,
    mask_rows,
):
    del after_ref
    channels = halo_ref.shape[0]
    lat = lax.axis_index("lat")
    odd = lax.rem(lat, 2) == 1
    lon_odd = lax.rem(lax.axis_index("lon"), 2) == 1
    folded = lat == lax.axis_size("lat") - 1
    place_rows(second_ref, odd, folded, wide, mask_rows, channels)
    halo_ref[...] = near_halo_ref[...] + placed(wide, channels)
    halo_mask_ref[...] = near_mask_ref[...] + mask_rows[...]
    join_ends(own_ends_ref, halo_ref, halo_mask_ref, ends_ref)
    pack_side(ends_ref, cross_ref, lon_odd)
    if alone:

        @pl.when(over_wrap())
        def _():
            cross_ref[...] = jnp.zeros_like(cross_ref)


def mirrored_columns(alone, sent_ref, after_ref, own_ref, wide, mask_rows, halo, ends):
    del after_ref
    channels = halo.shape[0]
    lat = lax.axis_index("lat")
    folded = lat == lax.axis_size("lat") - 1
    own_ref[...] = jnp.zeros_like(own_ref)
    if alone:

        @pl.when(folded & over_wrap())
        def _():
            odd = lax.rem(lat, 2) == 1
            place_rows(sent_ref, odd, folded, wide, mask_rows, channels)
            halo[...] = placed(wide, channels)
            join_ends(None, halo, mask_rows, ends)
            pack_side(ends, own_ref, lax.rem(lax.axis_index("lon"), 2) == 0)


def core_columns(ends_ref, after_ref, core_ref):
    del after_ref
    pack_side(ends_ref, core_ref, lax.rem(lax.axis_index("lon"), 2) == 0)


def in_row(place, first_layer):
    none = jnp.full_like(place, 1000)
    row = jnp.where(place < 16, place, none)
    row = jnp.where((place >= 16) & (place < 19), place - 19, row)
    row = jnp.where((place >= 20) & (place < 23), place - 4, row)
    if first_layer:
        row = jnp.where((place >= 24) & (place < 27), place - 30, row)
        row = jnp.where((place >= 28) & (place < 31), place - 9, row)
    return row


EDGE = (-3, -2, -1, 16, 17, 18, 0, 1, 2, 13, 14, 15)
INNER = (3, 4, 5, 6, 7, 8, 9, 10, 11, 12)


def place_of(row):
    if row < 0:
        return row + 19
    return row if row < 16 else row + 4


def conv_matrices(table, out_ref, left, right, row, rows_out):
    channels, taps = table.shape
    count = len(rows_out)
    folded = lax.axis_index("lat") == lax.axis_size("lat") - 1
    k = lanes((1, 256))
    shift = k // 32
    place = k - shift * 32
    tap = lax.broadcasted_iota(jnp.int32, (taps, 256), 0)
    row = row(place)
    for i, here in enumerate(rows_out):
        if here is None:
            wanted = jnp.full_like(k, -1)
        else:
            a = row - here + 3
            inside = (a >= 0) & (a <= 6) & (shift < 7)
            wanted = a * 7 + shift
            if here > 15:
                wanted = jnp.where(folded, 48 - wanted, wanted)
            wanted = jnp.where(inside, wanted, -1)
            wanted = jnp.where((shift == 7) & (place < 3), 49 + place, wanted)
        picks = (tap == wanted).astype(jnp.float32).astype(jnp.bfloat16)
        matrix = jnp.dot(table, picks, preferred_element_type=jnp.float32)
        left[pl.ds(i, channels, stride=count), :] = matrix[:, :128]
        right[pl.ds(i, channels, stride=count), :] = matrix[:, 128:]
    size = channels * count
    out_ref[:, :128] = left[:size, :].astype(jnp.bfloat16)
    out_ref[:, 128:] = right[:size, :].astype(jnp.bfloat16)


def split_bias(bias):
    high = bias.astype(jnp.bfloat16).astype(jnp.float32)
    rest = bias - high
    mid = rest.astype(jnp.bfloat16).astype(jnp.float32)
    return high, mid, rest - mid


def weights(
    kernel_ref,
    bias_ref,
    gain_ref,
    norm_bias_ref,
    expand_ref,
    expand_bias_ref,
    reduce_bias_ref,
    one_ref,
    two_ref,
    rows_ref,
    expand_out_ref,
    left,
    right,
    turn,
    tall,
):
    taps, layers, channels = kernel_ref.shape
    hidden = expand_ref.shape[2]
    turn[...] = jnp.zeros_like(turn)
    tall[...] = jnp.zeros_like(tall)
    for layer in range(layers):
        for tap in range(taps):
            turn[tap : tap + 1, :channels] = kernel_ref[tap, layer : layer + 1, :]
        parts = split_bias(bias_ref[layer : layer + 1, :])
        for n, part in enumerate(parts):
            turn[taps + n : taps + n + 1, :channels] = part
        table = turn[...].T[:channels, :64].astype(jnp.bfloat16)
        if layer == 0:
            every = EDGE + INNER + (None,) * 2
            row = functools.partial(in_row, first_layer=True)
            conv_matrices(table, one_ref, left, right, row, every)
        else:
            row = functools.partial(in_row, first_layer=False)
            conv_matrices(table, two_ref, left, right, row, tuple(range(16)))
    for layer in range(layers):
        for n, ref in enumerate((gain_ref, norm_bias_ref, reduce_bias_ref)):
            turn[:, :channels] = jnp.broadcast_to(ref[layer : layer + 1, :], (128, channels))
            rows_ref[layer, n] = turn[...].T[:channels, :]
        tall[:channels, :] = expand_ref[layer].astype(jnp.float32) * 0.5
        parts = split_bias(expand_bias_ref[layer : layer + 1, :] * 0.5)
        for n, part in enumerate(parts):
            tall[channels + n : channels + n + 1, :] = part
        for n in range(hidden // 128):
            piece = tall[:, n * 128 : (n + 1) * 128].T
            at = pl.ds(n * 128, 128)
            expand_out_ref[layer, at, :] = piece[:, : channels + 16].astype(jnp.bfloat16)


ERF = (7.97869712e-01, 3.63922860e-02, -8.78263977e-05, -3.66934787e-05, 1.42500782e-06)


def gelu_of_double(half):
    square = half * half
    total = jnp.full_like(half, 2.0 * 4.0 ** (len(ERF) - 1) * ERF[-1])
    for power in range(len(ERF) - 2, -1, -1):
        total = total * square + jnp.full_like(half, 2.0 * 4.0**power * ERF[power])
    return half * jnp.tanh(half * total) + half


def norm(rows_ref, layer, cells):
    average = jnp.mean(cells, axis=0, keepdims=True)
    centered = cells - average
    variance = jnp.mean(centered * centered, axis=0, keepdims=True)
    scaled = centered * lax.rsqrt(variance + 1e-06)
    return (scaled * rows_ref[layer, 0] + rows_ref[layer, 1]).astype(jnp.bfloat16)


def mlp(rows_ref, expand_ref, reduce_ref, layer, blocks, normed_ref, inner_ref, put):
    count = len(blocks)
    channels, width = rows_ref.shape[2:]
    hidden = inner_ref.shape[0]
    wide = count * width
    normed_ref[channels:, :wide] = jnp.ones((16, wide), jnp.bfloat16)
    for n, block in enumerate(blocks):
        at = slice(n * width, (n + 1) * width)
        normed_ref[:channels, at] = norm(rows_ref, layer, block())
    tiles = [slice(n, min(n + 2 * width, wide)) for n in range(0, wide, 2 * width)]
    for at in tiles:
        normed = normed_ref[:, at]
        for part in range(0, hidden, 128):
            matrix = expand_ref[layer, part : part + 128, :]
            half = jnp.dot(matrix, normed, preferred_element_type=jnp.float32)
            for k in range(0, 128, 16):
                values = gelu_of_double(half[k : k + 16, :].astype(jnp.bfloat16))
                inner_ref[part + k : part + k + 16, at] = values
    extra = rows_ref[layer, 2]
    for t, at in enumerate(tiles):
        change = jnp.dot(reduce_ref[layer], inner_ref[:, at], preferred_element_type=jnp.float32)
        for n in range((at.stop - at.start) // width):
            put(t * 2 + n, change[:, n * width : (n + 1) * width] + extra)


def columns_stack(block, ones):
    width = block.shape[1]
    stack = [block if s == 0 else pltpu.roll(block, (-s) % width, 1) for s in range(-3, 4)]
    return jnp.concatenate(stack + [ones], axis=0)


def conv_rows(matrix_ref, stack_of, conv, channels, stride, first, count):
    ones = jnp.ones((matrix_ref.shape[1] // 8, 128), jnp.bfloat16)

    def step(c, carry):
        matrix = matrix_ref[pl.ds(pl.multiple_of(c * stride + first, 8), count), :]
        result = jnp.dot(matrix, stack_of(c, ones), preferred_element_type=jnp.float32)
        conv[pl.ds(c, count, stride=pitch(channels)), :] = result
        return carry

    lax.fori_loop(0, channels, step, 0, unroll=channels)


def conv_row(conv, channels, i):
    start = i * pitch(channels)
    return lambda: conv[start : start + channels, :]


def inner_rows(
    field_ref, matrix_ref, rows_ref, expand_ref, reduce_ref, update_ref, conv, normed, inner
):
    channels, rows, width = field_ref.shape
    none = jnp.zeros((16, width), jnp.bfloat16)

    def stack_of(c, ones):
        return columns_stack(jnp.concatenate([field_ref[c], none], axis=0), ones)

    conv_rows(matrix_ref, stack_of, conv, channels, 24, 8, 16)

    def put(n, change):
        update_ref[pl.ds(INNER[n], channels, stride=24), :] = change

    blocks = [conv_row(conv, channels, i + len(EDGE) - 8) for i in range(len(INNER))]
    mlp(rows_ref, expand_ref, reduce_ref, 0, blocks, normed, inner, put)


def edge_rows(
    field_ref,
    halo_ref,
    matrix_ref,
    rows_ref,
    expand_ref,
    reduce_ref,
    old_ref,
    update_ref,
    conv,
    normed,
    inner,
):
    del old_ref
    channels, _, width = field_ref.shape

    def stack_of(c, ones):
        return columns_stack(jnp.concatenate([field_ref[c], halo_ref[c]], axis=0), ones)

    conv_rows(matrix_ref, stack_of, conv, channels, 24, 0, 16)
    for empty in (19, 23):
        update_ref[pl.ds(empty, channels, stride=24), :] = jnp.zeros((channels, width), jnp.float32)

    def put(n, change):
        update_ref[pl.ds(place_of(EDGE[n]), channels, stride=24), :] = change

    blocks = [conv_row(conv, channels, i) for i in range(len(EDGE))]
    mlp(rows_ref, expand_ref, reduce_ref, 0, blocks, normed, inner, put)


def neighbours(core_ref, cross_refs, group, groups):
    width = core_ref.shape[1]
    half = groups // 2
    m, upper = (half, 0) if group == groups else (group % half, group // half)
    core = core_ref[m * 32 : m * 32 + 32, :]
    cross = sum(ref[m * 32 : m * 32 + 32, :] for ref in cross_refs)
    lon_even = lax.rem(lax.axis_index("lon"), 2) == 0
    east = jnp.where(lon_even, core, cross)
    west = jnp.where(lon_even, cross, core)
    east = pltpu.roll(east, (HALO - 8 * upper) % width, 1)
    return east, pltpu.roll(west, width - 8, 1) if upper else west


def edge_columns(
    core_ref,
    cross_ref,
    wrap_ref,
    own_ref,
    ends_ref,
    matrix_ref,
    rows_ref,
    expand_ref,
    reduce_ref,
    strips,
    conv,
    normed,
    inner,
):
    channels, width = rows_ref.shape[2:]
    quarter = channels // 4
    groups = channels // 8
    lane32 = lanes((32, width))
    first_six = lane32 % 16 < HALO
    first_twelve = lane32 % 32 < 2 * HALO
    ones = jnp.ones((32, width), jnp.bfloat16)
    for g in range(groups):
        at = slice(g * 32, g * 32 + 32)
        east, west = neighbours(core_ref, (cross_ref, wrap_ref, own_ref), g, groups)
        own = ends_ref[at, :]
        at_west = jnp.where(first_six, west, own)
        at_east = jnp.where(first_six, own, east)
        for t in range(2):
            left = pltpu.roll(at_west, width - 16, 1) if t else at_west
            right = pltpu.roll(at_east, (2 * HALO - 16 * t) % width, 1)
            block = jnp.where(first_twelve, left, right)
            some = [channel_of(channels, g, 2 * n + t) for n in range(4)]
            matrix = jnp.concatenate(
                [matrix_ref[c * 24 : c * 24 + 24, :] for c in some], axis=0
            )
            stack = columns_stack(block, ones)
            result = jnp.dot(matrix, stack, preferred_element_type=jnp.float32)
            for n, c in enumerate(some):
                conv[pl.ds(c, 24, stride=pitch(channels)), :] = result[n * 24 : n * 24 + 24, :]

    order = {place_of(row): i for i, row in enumerate(EDGE + INNER)}
    lane = lanes((quarter, width))
    starts = [32 * (q // 2) + 6 * (q % 2) for q in range(8)]
    inside = [
        ((lane >= s + 3) & (lane < s + 9)) | ((lane >= s + 15) & (lane < s + 21)) for s in starts
    ]
    packs = []
    for p in range(3):
        parts = []
        for n in range(4):
            packed = jnp.zeros((quarter, width), jnp.float32)
            for q, start in enumerate(starts):
                if p * 8 + q in order:
                    row = order[p * 8 + q] * pitch(channels) + n * quarter
                    block = conv[row : row + quarter, :]
                    block = pltpu.roll(block, (start - 32 * n) % width, 1)
                    packed = jnp.where(inside[q], block, packed)
            parts.append(packed)
        packs.append(jnp.concatenate(parts, axis=0))

    def put(p, change):
        for q, start in enumerate(starts):
            near = pltpu.roll(change, (width - 6 - start) % width, 1)
            strips[pl.ds(p * 8 + q, channels, stride=24), :] = near

    blocks = [functools.partial(lambda block: block, packed) for packed in packs]
    mlp(rows_ref, expand_ref, reduce_ref, 0, blocks, normed, inner, put)


def second_layer(
    field_ref,
    mask_ref,
    halo_ref,
    halo_mask_ref,
    core_ref,
    cross_ref,
    wrap_ref,
    own_ref,
    strips,
    update_ref,
    matrix_ref,
    rows_ref,
    expand_ref,
    reduce_ref,
    out_ref,
    main_ref,
    conv,
    changes,
    normed,
    inner,
):
    channels, rows, width = out_ref.shape
    groups = channels // 8
    lane32 = lanes((32, width))
    lane24 = lanes((24, width))
    first_six = lane32 % 16 < HALO

    def beside_of(received, slot):
        beside = pltpu.roll(received, (width - HALO - 16 * slot) % width, 1)
        return beside.astype(jnp.float32)[0:24, :]

    def received(g):
        east, west = neighbours(core_ref, (cross_ref, wrap_ref, own_ref), g, groups)
        return jnp.where(first_six, west, east)

    main_mask = jnp.concatenate(
        [mask_ref[...].astype(jnp.float32), halo_mask_ref[0:8, :]], axis=0
    )
    side_mask = beside_of(received(groups), 0)
    low = lane24 < 3
    high = lane24 >= width - 3
    blank = jnp.zeros((8, width), jnp.float32)
    ones = jnp.ones((32, width), jnp.bfloat16)
    lane16 = lanes((16, width))
    away = {s: lane16 < s if s > 0 else lane16 >= width + s for s in range(-3, 4) if s}

    def halves(block):
        low_rows = block[:16, :].astype(jnp.bfloat16)
        return low_rows, jnp.concatenate([block[16:, :], blank], axis=0).astype(jnp.bfloat16)

    for g in range(groups):
        both = received(g)
        for j in range(8):
            c = channel_of(channels, g, j)
            near = strips[c * 24 : c * 24 + 24, :]
            far = pltpu.roll(near, width - 2 * HALO, 1)
            change = update_ref[c * 24 : c * 24 + 24, :]
            change = jnp.where(low, near, jnp.where(high, far, change))
            own = field_ref[c].astype(jnp.float32)
            halo = halo_ref[c].astype(jnp.float32)[:8, :]
            main = halves(main_mask * (jnp.concatenate([own, halo], axis=0) + change))
            main_ref[c] = main[0]
            change = jnp.where(high, near, far)
            beside = halves(side_mask * (beside_of(both, j) + change))
            stack = []
            for s in range(-3, 4):
                for part, other in zip(main, beside):
                    if s:
                        part = pltpu.roll(jnp.where(away[s], other, part), (-s) % width, 1)
                    stack.append(part)
            stack = jnp.concatenate(stack + [ones], axis=0)
            matrix = matrix_ref[c * 16 : c * 16 + 16, :]
            result = jnp.dot(matrix, stack, preferred_element_type=jnp.float32)
            conv[pl.ds(c, 16, stride=pitch(channels)), :] = result

    def put(n, change):
        changes[pl.ds(n, channels, stride=APART), :] = change

    blocks = [conv_row(conv, channels, i) for i in range(rows)]
    mlp(rows_ref, expand_ref, reduce_ref, 1, blocks, normed, inner, put)
    mask = main_mask[:rows, :]
    for c in range(channels):
        change = changes[c * APART : c * APART + rows, :]
        out_ref[c] = (mask * (main_ref[c].astype(jnp.float32) + change)).astype(jnp.bfloat16)


def per_device(
    nlat,
    nlon,
    field,
    land_mask,
    depth_kernel,
    depth_bias,
    norm_gain,
    norm_bias,
    w_expand,
    b_expand,
    w_reduce,
    b_reduce,
):
    channels, rows, width = field.shape
    layers, hidden = b_expand.shape
    bf16, f32 = jnp.bfloat16, jnp.float32
    edge = HALO * channels + 16

    def buffers(count):
        return [
            pltpu.VMEM((channels + 16, count * width), bf16),
            pltpu.VMEM((hidden, count * width), bf16),
        ]

    def pack(upper_if_even, after):
        return pl.pallas_call(
            functools.partial(pack_rows, upper_if_even),
            out_shape=jax.ShapeDtypeStruct((edge, width), bf16),
            in_specs=vmem(2) + [pl.BlockSpec(memory_space=pl.ANY)],
            out_specs=pl.BlockSpec(memory_space=pltpu.VMEM),
            scratch_shapes=[
                pltpu.VMEM(((channels + 1) * APART, width), f32),
                pltpu.VMEM((rows, width), f32),
            ],
            compiler_params=params(),
            cost_estimate=cost(4e9),
        )(field, land_mask, after)

    begun = pl.pallas_call(
        first_step,
        out_shape=jax.ShapeDtypeStruct((8, 128), f32),
        out_specs=pl.BlockSpec(memory_space=pltpu.VMEM),
        compiler_params=params(),
        cost_estimate=cost(4e9),
    )()
    first = pack(True, begun)
    second_sent = pack(False, first)

    alone = nlat == 2

    def at(d, lat):
        return d * nlat + lat

    pairs = []
    for d in range(nlon):
        for low in range(1, nlat - 1, 2):
            pairs += [(at(d, low), at(d, low + 1)), (at(d, low + 1), at(d, low))]
        pairs.append((at(d, nlat - 1), at(nlon - 1 - d, nlat - 1)))
        pairs.append((at(d, 0), at(d ^ 1, 0)))
    second = lax.ppermute(second_sent, ("lon", "lat"), pairs)
    pairs = []
    for low in range(0, nlat - 1, 2):
        pairs += [(low, low + 1), (low + 1, low)]
    first = lax.ppermute(first, "lat", pairs)

    kernel = depth_kernel.transpose(2, 3, 0, 1).reshape(49, layers, channels)
    matrix_one, matrix_two, by_channel, expand = pl.pallas_call(
        weights,
        out_shape=[
            jax.ShapeDtypeStruct((channels * 24, 256), bf16),
            jax.ShapeDtypeStruct((channels * 16, 256), bf16),
            jax.ShapeDtypeStruct((layers, 3, channels, 128), f32),
            jax.ShapeDtypeStruct((layers, hidden, channels + 16), bf16),
        ],
        in_specs=vmem(7),
        out_specs=vmem(4),
        scratch_shapes=[
            pltpu.VMEM(((channels + 1) * 24, 128), f32),
            pltpu.VMEM(((channels + 1) * 24, 128), f32),
            pltpu.VMEM((128, 128), f32),
            pltpu.VMEM((128, hidden), f32),
        ],
        compiler_params=params(),
        cost_estimate=cost(2e9),
    )(
        kernel,
        depth_bias,
        norm_gain,
        norm_bias,
        w_expand.transpose(0, 2, 1),
        b_expand,
        b_reduce,
    )
    update = pl.pallas_call(
        inner_rows,
        out_shape=jax.ShapeDtypeStruct(((channels + 1) * 24, width), f32),
        in_specs=vmem(5),
        out_specs=pl.BlockSpec(memory_space=pltpu.VMEM),
        scratch_shapes=[pltpu.VMEM((pitch(channels) * 17, width), f32)] + buffers(len(INNER)),
        compiler_params=params(),
        cost_estimate=cost(4e9),
    )(field, matrix_one, by_channel, expand, w_reduce)

    groups = channels // 8 + 1
    sent_rows = (channels // 16 + 1) * 32
    near_halo, near_mask, own_ends, wrap = pl.pallas_call(
        near_rows,
        out_shape=[
            jax.ShapeDtypeStruct((channels, 16, width), bf16),
            jax.ShapeDtypeStruct((16, width), f32),
            jax.ShapeDtypeStruct((groups * 16, width), bf16),
            jax.ShapeDtypeStruct((sent_rows, width), bf16),
        ],
        in_specs=vmem(3),
        out_specs=vmem(4),
        scratch_shapes=[
            pltpu.VMEM(((channels + 1) * APART, width), f32),
            pltpu.VMEM((groups * 32, width), bf16),
        ],
        compiler_params=params(),
        cost_estimate=cost(1e9),
    )(field, land_mask, first)
    if alone:
        pairs = []
        for lat in range(nlat):
            pairs += [(lat, at(nlon - 1, lat)), (at(nlon - 1, lat), lat)]
            pairs += [(at(d, lat), at(d, 1 - lat)) for d in range(1, nlon - 1)]
        wrap = lax.ppermute(wrap, ("lon", "lat"), pairs)
    else:
        wrap = jnp.zeros_like(wrap)
    halo, halo_mask, ends, cross = pl.pallas_call(
        functools.partial(far_rows, alone),
        out_shape=[
            jax.ShapeDtypeStruct((channels, 16, width), bf16),
            jax.ShapeDtypeStruct((16, width), f32),
            jax.ShapeDtypeStruct((groups * 32, width), bf16),
            jax.ShapeDtypeStruct((sent_rows, width), bf16),
        ],
        in_specs=vmem(4) + [pl.BlockSpec(memory_space=pl.ANY)],
        out_specs=vmem(4),
        scratch_shapes=[
            pltpu.VMEM(((channels + 1) * APART, width), f32),
            pltpu.VMEM((16, width), f32),
        ],
        compiler_params=params(),
    )(second, near_halo, near_mask, own_ends, update)
    core = pl.pallas_call(
        core_columns,
        out_shape=jax.ShapeDtypeStruct((sent_rows, width), bf16),
        in_specs=vmem(1) + [pl.BlockSpec(memory_space=pl.ANY)],
        out_specs=pl.BlockSpec(memory_space=pltpu.VMEM),
        compiler_params=params(),
    )(ends, cross)

    own = pl.pallas_call(
        functools.partial(mirrored_columns, alone),
        out_shape=jax.ShapeDtypeStruct((sent_rows, width), bf16),
        in_specs=vmem(1) + [pl.BlockSpec(memory_space=pl.ANY)],
        out_specs=pl.BlockSpec(memory_space=pltpu.VMEM),
        scratch_shapes=[
            pltpu.VMEM(((channels + 1) * APART, width), f32),
            pltpu.VMEM((16, width), f32),
            pltpu.VMEM((channels, 16, width), bf16),
            pltpu.VMEM((groups * 32, width), bf16),
        ],
        compiler_params=params(),
    )(second_sent, core)

    pairs = []
    for low in range(0, nlon, 2):
        pairs += [(low, low + 1), (low + 1, low)]
    core = lax.ppermute(core, "lon", pairs)
    pairs = []
    for lat in range(nlat):
        for low in range(1, nlon, 2):
            after = (low + 1) % nlon
            if after or not alone:
                pairs += [(at(low, lat), at(after, lat)), (at(after, lat), at(low, lat))]
            else:
                pairs += [(at(low, lat), at(low, 1 - lat)), (at(after, lat), at(after, 1 - lat))]
    cross = lax.ppermute(cross, ("lon", "lat"), pairs)

    update = pl.pallas_call(
        edge_rows,
        out_shape=jax.ShapeDtypeStruct(((channels + 1) * 24, width), f32),
        in_specs=vmem(7),
        out_specs=pl.BlockSpec(memory_space=pltpu.VMEM),
        scratch_shapes=[pltpu.VMEM((pitch(channels) * 17, width), f32)] + buffers(len(EDGE)),
        input_output_aliases={6: 0},
        compiler_params=params(),
        cost_estimate=cost(4e9),
    )(field, halo, matrix_one, by_channel, expand, w_reduce, update)

    strips = pl.pallas_call(
        edge_columns,
        out_shape=jax.ShapeDtypeStruct(((channels + 1) * 24, width), f32),
        in_specs=vmem(9),
        out_specs=pl.BlockSpec(memory_space=pltpu.VMEM),
        scratch_shapes=[pltpu.VMEM((pitch(channels) * 25, width), f32)] + buffers(3),
        compiler_params=params(),
    )(core, cross, wrap, own, ends, matrix_one, by_channel, expand, w_reduce)

    return pl.pallas_call(
        second_layer,
        out_shape=jax.ShapeDtypeStruct((channels, rows, width), bf16),
        in_specs=vmem(14),
        out_specs=pl.BlockSpec(memory_space=pltpu.VMEM),
        scratch_shapes=[
            pltpu.VMEM((channels, rows, width), bf16),
            pltpu.VMEM((pitch(channels) * 17, width), f32),
            pltpu.VMEM(((channels + 1) * APART, width), f32),
        ]
        + buffers(rows),
        compiler_params=params(),
    )(
        field,
        land_mask,
        halo,
        halo_mask,
        core,
        cross,
        wrap,
        own,
        strips,
        update,
        matrix_two,
        by_channel,
        expand,
        w_reduce,
    )


def solution(mesh):
    placed = (P(None, "lat", "lon"), P("lat", "lon"), P(), P(), P(), P(), P(), P(), P(), P())
    return jax.shard_map(
        functools.partial(per_device, mesh.shape["lat"], mesh.shape["lon"]),
        mesh=mesh,
        in_specs=placed,
        out_specs=P(None, "lat", "lon"),
        check_vma=False,
    )
```

```python
import functools

import jax
import jax.numpy as jnp
from jax import lax
from jax.experimental import pallas as pl
from jax.experimental.pallas import tpu as pltpu
from jax.sharding import PartitionSpec as P


HALO = 6
APART = 24
VMEM_LIMIT = 20 * 1024 * 1024


def pitch(channels):
    return channels + 8


def params():
    return pltpu.CompilerParams(vmem_limit_bytes=VMEM_LIMIT)


def cost(flops):
    return pl.CostEstimate(flops=int(flops), bytes_accessed=1 << 20, transcendentals=0)


def vmem(count):
    return [pl.BlockSpec(memory_space=pltpu.VMEM)] * count


def lanes(shape):
    return lax.broadcasted_iota(jnp.int32, shape, len(shape) - 1)


def first_step(out_ref):
    out_ref[...] = jnp.zeros_like(out_ref)


def pack_rows(upper_if_even, field_ref, mask_ref, after_ref, out_ref, wide, wide_mask):
    del after_ref
    kept = 1.0 if upper_if_even else (lax.axis_index("lat") > 0).astype(jnp.float32)
    channels, rows, width = field_ref.shape
    even = lax.rem(lax.axis_index("lat"), 2) == 0
    take_upper = even if upper_if_even else jnp.logical_not(even)
    for c in range(channels):
        wide[c * APART : c * APART + rows, :] = field_ref[c].astype(jnp.float32)
    wide_mask[...] = mask_ref[...].astype(jnp.float32)
    for k in range(HALO):
        lower = wide[pl.ds(k, channels, stride=APART), :]
        upper = wide[pl.ds(rows - HALO + k, channels, stride=APART), :]
        at = pl.ds(k * channels, channels)
        out_ref[at, :] = (kept * jnp.where(take_upper, upper, lower)).astype(jnp.bfloat16)
    pad = jnp.zeros((16 - HALO, width), jnp.float32)
    lower = jnp.concatenate([wide_mask[0:HALO, :], pad], axis=0)
    upper = jnp.concatenate([wide_mask[rows - HALO : rows, :], pad], axis=0)
    at = pl.ds(HALO * channels, 16)
    out_ref[at, :] = (kept * jnp.where(take_upper, upper, lower)).astype(jnp.bfloat16)


def north_place(row):
    return jnp.where(row < 3, 4 + row, 9 + row)


def south_place(k):
    return k - 3 if k >= 3 else 8 + k


def place_rows(received_ref, is_north, turned, wide, mask_rows, channels):
    width = received_ref.shape[1]
    wide[...] = jnp.zeros_like(wide)
    mask_rows[...] = jnp.zeros_like(mask_rows)
    turn = None
    if turned is not None:
        sub = lax.broadcasted_iota(jnp.int32, (width, width), 0)
        target = lanes((width, width))
        turn = sub == jnp.where(turned, width - 1 - target, target)
        turn = turn.astype(jnp.float32).astype(jnp.bfloat16)

    def rows_at(start, count):
        block = received_ref[start : start + count, :]
        if turn is None:
            return block.astype(jnp.float32)
        return jnp.dot(block, turn, preferred_element_type=jnp.float32)

    masks = rows_at(HALO * channels, 16)
    for k in range(HALO):
        row = k if turned is None else jnp.where(turned, HALO - 1 - k, k)
        place = jnp.where(is_north, north_place(row), south_place(k))
        wide[pl.ds(place, channels, stride=APART), :] = rows_at(k * channels, channels)
        mask_rows[pl.ds(place, 1), :] = masks[k : k + 1, :]


def placed(wide, channels):
    blocks = wide[: channels * APART, :].reshape(channels, APART, wide.shape[1])
    return blocks[:, :16, :].astype(jnp.bfloat16)


def pack_ends(blocks):
    rows, width = blocks[0].shape
    slot = lanes((rows, width)) // 16
    packed = jnp.zeros((rows, width), jnp.bfloat16)
    for j, block in enumerate(blocks):
        packed = jnp.where(slot == j, pltpu.roll(block, 16 * j + HALO, 1), packed)
    return packed


def channel_of(channels, group, slot):
    return slot // 2 * (channels // 4) + group * 2 + slot % 2


def over_wrap():
    lon = lax.axis_index("lon")
    return (lon == 0) | (lon == lax.axis_size("lon") - 1)


def near_rows(
    field_ref, mask_ref, first_ref, halo_ref, mask_rows, ends_ref, wrap_ref, wide, all_ends
):
    channels, rows, width = field_ref.shape
    even = lax.rem(lax.axis_index("lat"), 2) == 0
    place_rows(first_ref, even, None, wide, mask_rows, channels)
    halo_ref[...] = placed(wide, channels)
    groups = channels // 8
    for g in range(groups):
        blocks = [field_ref[channel_of(channels, g, j)] for j in range(8)]
        ends_ref[g * 16 : g * 16 + 16, :] = pack_ends(blocks)
    mask = mask_ref[...].astype(jnp.float32).astype(jnp.bfloat16)
    ends_ref[groups * 16 :, :] = pack_ends([mask])
    wrap_ref[...] = jnp.zeros_like(wrap_ref)

    @pl.when(over_wrap())
    def _():
        join_ends(ends_ref, halo_ref, mask_rows, all_ends)
        pack_side(all_ends, wrap_ref, lax.rem(lax.axis_index("lon"), 2) == 1)


def join_ends(own_ends_ref, halo_ref, mask_rows, ends_ref):
    channels = halo_ref.shape[0]
    groups = channels // 8
    for g in range(groups + 1):
        if g < groups:
            blocks = [halo_ref[channel_of(channels, g, j)] for j in range(8)]
        else:
            blocks = [mask_rows[...].astype(jnp.bfloat16)]
        own = jnp.zeros((16, halo_ref.shape[2]), jnp.bfloat16)
        if own_ends_ref is not None:
            own = own_ends_ref[g * 16 : g * 16 + 16, :]
        ends_ref[g * 32 : g * 32 + 16, :] = own
        ends_ref[g * 32 + 16 : g * 32 + 32, :] = pack_ends(blocks)


def pack_side(ends_ref, out_ref, to_east):
    width = ends_ref.shape[1]
    groups = ends_ref.shape[0] // 32 - 1
    lower = lanes((32, width)) % 16 < 8
    for m in range(groups // 2 + 1):
        n = m if m < groups // 2 else groups
        one = ends_ref[n * 32 : n * 32 + 32, :]
        one = jnp.where(to_east, one, pltpu.roll(one, width - HALO, 1))
        if n < groups:
            two = ends_ref[(n + groups // 2) * 32 : (n + groups // 2) * 32 + 32, :]
            two = jnp.where(to_east, pltpu.roll(two, 8, 1), pltpu.roll(two, 8 - HALO, 1))
            one = jnp.where(lower, one, two)
        out_ref[m * 32 : m * 32 + 32, :] = one


def far_rows(
    alone,
    second_ref,
    near_halo_ref,
    near_mask_ref,
    own_ends_ref,
    after_ref,
    halo_ref,
    halo_mask_ref,
    ends_ref,
    cross_ref,
    wide,
    mask_rows,
):
    del after_ref
    channels = halo_ref.shape[0]
    lat = lax.axis_index("lat")
    odd = lax.rem(lat, 2) == 1
    lon_odd = lax.rem(lax.axis_index("lon"), 2) == 1
    folded = lat == lax.axis_size("lat") - 1
    place_rows(second_ref, odd, folded, wide, mask_rows, channels)
    halo_ref[...] = near_halo_ref[...] + placed(wide, channels)
    halo_mask_ref[...] = near_mask_ref[...] + mask_rows[...]
    join_ends(own_ends_ref, halo_ref, halo_mask_ref, ends_ref)
    pack_side(ends_ref, cross_ref, lon_odd)
    if alone:

        @pl.when(over_wrap())
        def _():
            cross_ref[...] = jnp.zeros_like(cross_ref)


def mirrored_columns(alone, sent_ref, after_ref, own_ref, wide, mask_rows, halo, ends):
    del after_ref
    channels = halo.shape[0]
    lat = lax.axis_index("lat")
    folded = lat == lax.axis_size("lat") - 1
    own_ref[...] = jnp.zeros_like(own_ref)
    if alone:

        @pl.when(folded & over_wrap())
        def _():
            odd = lax.rem(lat, 2) == 1
            place_rows(sent_ref, odd, folded, wide, mask_rows, channels)
            halo[...] = placed(wide, channels)
            join_ends(None, halo, mask_rows, ends)
            pack_side(ends, own_ref, lax.rem(lax.axis_index("lon"), 2) == 0)


def core_columns(ends_ref, after_ref, core_ref):
    del after_ref
    pack_side(ends_ref, core_ref, lax.rem(lax.axis_index("lon"), 2) == 0)


def in_row(place, first_layer):
    none = jnp.full_like(place, 1000)
    row = jnp.where(place < 16, place, none)
    row = jnp.where((place >= 16) & (place < 19), place - 19, row)
    row = jnp.where((place >= 20) & (place < 23), place - 4, row)
    if first_layer:
        row = jnp.where((place >= 24) & (place < 27), place - 30, row)
        row = jnp.where((place >= 28) & (place < 31), place - 9, row)
    return row


EDGE = (-3, -2, -1, 16, 17, 18, 0, 1, 2, 13, 14, 15)
INNER = (3, 4, 5, 6, 7, 8, 9, 10, 11, 12)


def place_of(row):
    if row < 0:
        return row + 19
    return row if row < 16 else row + 4


def conv_matrices(table, out_ref, left, right, row, rows_out):
    channels, taps = table.shape
    count = len(rows_out)
    folded = lax.axis_index("lat") == lax.axis_size("lat") - 1
    k = lanes((1, 256))
    shift = k // 32
    place = k - shift * 32
    tap = lax.broadcasted_iota(jnp.int32, (taps, 256), 0)
    row = row(place)
    for i, here in enumerate(rows_out):
        if here is None:
            wanted = jnp.full_like(k, -1)
        else:
            a = row - here + 3
            inside = (a >= 0) & (a <= 6) & (shift < 7)
            wanted = a * 7 + shift
            if here > 15:
                wanted = jnp.where(folded, 48 - wanted, wanted)
            wanted = jnp.where(inside, wanted, -1)
            wanted = jnp.where((shift == 7) & (place < 3), 49 + place, wanted)
        picks = (tap == wanted).astype(jnp.float32).astype(jnp.bfloat16)
        matrix = jnp.dot(table, picks, preferred_element_type=jnp.float32)
        left[pl.ds(i, channels, stride=count), :] = matrix[:, :128]
        right[pl.ds(i, channels, stride=count), :] = matrix[:, 128:]
    size = channels * count
    out_ref[:, :128] = left[:size, :].astype(jnp.bfloat16)
    out_ref[:, 128:] = right[:size, :].astype(jnp.bfloat16)


def split_bias(bias):
    high = bias.astype(jnp.bfloat16).astype(jnp.float32)
    rest = bias - high
    mid = rest.astype(jnp.bfloat16).astype(jnp.float32)
    return high, mid, rest - mid


def weights(
    kernel_ref,
    bias_ref,
    gain_ref,
    norm_bias_ref,
    expand_ref,
    expand_bias_ref,
    reduce_bias_ref,
    one_ref,
    two_ref,
    rows_ref,
    expand_out_ref,
    left,
    right,
    turn,
    tall,
):
    taps, layers, channels = kernel_ref.shape
    hidden = expand_ref.shape[2]
    turn[...] = jnp.zeros_like(turn)
    tall[...] = jnp.zeros_like(tall)
    for layer in range(layers):
        for tap in range(taps):
            turn[tap : tap + 1, :channels] = kernel_ref[tap, layer : layer + 1, :]
        parts = split_bias(bias_ref[layer : layer + 1, :])
        for n, part in enumerate(parts):
            turn[taps + n : taps + n + 1, :channels] = part
        table = turn[...].T[:channels, :64].astype(jnp.bfloat16)
        if layer == 0:
            every = EDGE + INNER + (None,) * 2
            row = functools.partial(in_row, first_layer=True)
            conv_matrices(table, one_ref, left, right, row, every)
        else:
            row = functools.partial(in_row, first_layer=False)
            conv_matrices(table, two_ref, left, right, row, tuple(range(16)))
    for layer in range(layers):
        for n, ref in enumerate((gain_ref, norm_bias_ref, reduce_bias_ref)):
            turn[:, :channels] = jnp.broadcast_to(ref[layer : layer + 1, :], (128, channels))
            rows_ref[layer, n] = turn[...].T[:channels, :]
        tall[:channels, :] = expand_ref[layer].astype(jnp.float32) * 0.5
        parts = split_bias(expand_bias_ref[layer : layer + 1, :] * 0.5)
        for n, part in enumerate(parts):
            tall[channels + n : channels + n + 1, :] = part
        for n in range(hidden // 128):
            piece = tall[:, n * 128 : (n + 1) * 128].T
            at = pl.ds(n * 128, 128)
            expand_out_ref[layer, at, :] = piece[:, : channels + 16].astype(jnp.bfloat16)


ERF = (7.97869712e-01, 3.63922860e-02, -8.78263977e-05, -3.66934787e-05, 1.42500782e-06)


def gelu_of_double(half):
    square = half * half
    total = jnp.full_like(half, 2.0 * 4.0 ** (len(ERF) - 1) * ERF[-1])
    for power in range(len(ERF) - 2, -1, -1):
        total = total * square + jnp.full_like(half, 2.0 * 4.0**power * ERF[power])
    return half * jnp.tanh(half * total) + half


def norm(rows_ref, layer, cells):
    average = jnp.mean(cells, axis=0, keepdims=True)
    centered = cells - average
    variance = jnp.mean(centered * centered, axis=0, keepdims=True)
    scaled = centered * lax.rsqrt(variance + 1e-06)
    return (scaled * rows_ref[layer, 0] + rows_ref[layer, 1]).astype(jnp.bfloat16)


def mlp(rows_ref, expand_ref, reduce_ref, layer, blocks, normed_ref, inner_ref, put):
    count = len(blocks)
    channels, width = rows_ref.shape[2:]
    hidden = inner_ref.shape[0]
    wide = count * width
    normed_ref[channels:, :wide] = jnp.ones((16, wide), jnp.bfloat16)
    for n, block in enumerate(blocks):
        at = slice(n * width, (n + 1) * width)
        normed_ref[:channels, at] = norm(rows_ref, layer, block())
    step = 2 if count % 2 == 0 else 3
    tiles = [slice(n, min(n + step * width, wide)) for n in range(0, wide, step * width)]
    for at in tiles:
        normed = normed_ref[:, at]
        for part in range(0, hidden, 128):
            matrix = expand_ref[layer, part : part + 128, :]
            half = jnp.dot(matrix, normed, preferred_element_type=jnp.float32)
            for k in range(0, 128, 16):
                values = gelu_of_double(half[k : k + 16, :].astype(jnp.bfloat16))
                inner_ref[part + k : part + k + 16, at] = values
    extra = rows_ref[layer, 2]
    for t, at in enumerate(tiles):
        change = jnp.dot(reduce_ref[layer], inner_ref[:, at], preferred_element_type=jnp.float32)
        for n in range((at.stop - at.start) // width):
            put(t * step + n, change[:, n * width : (n + 1) * width] + extra)


def columns_stack(block, ones):
    width = block.shape[1]
    stack = [block if s == 0 else pltpu.roll(block, (-s) % width, 1) for s in range(-3, 4)]
    return jnp.concatenate(stack + [ones], axis=0)


def conv_rows(matrix_ref, stack_of, conv, channels, stride, first, count):
    ones = jnp.ones((matrix_ref.shape[1] // 8, 128), jnp.bfloat16)

    def step(c, carry):
        matrix = matrix_ref[pl.ds(pl.multiple_of(c * stride + first, 8), count), :]
        result = jnp.dot(matrix, stack_of(c, ones), preferred_element_type=jnp.float32)
        conv[pl.ds(c, count, stride=pitch(channels)), :] = result
        return carry

    lax.fori_loop(0, channels, step, 0, unroll=channels)


def conv_row(conv, channels, i):
    start = i * pitch(channels)
    return lambda: conv[start : start + channels, :]


def inner_rows(
    field_ref, matrix_ref, rows_ref, expand_ref, reduce_ref, update_ref, conv, normed, inner
):
    channels, rows, width = field_ref.shape
    none = jnp.zeros((16, width), jnp.bfloat16)

    def stack_of(c, ones):
        return columns_stack(jnp.concatenate([field_ref[c], none], axis=0), ones)

    conv_rows(matrix_ref, stack_of, conv, channels, 24, 8, 16)

    def put(n, change):
        update_ref[pl.ds(INNER[n], channels, stride=24), :] = change

    blocks = [conv_row(conv, channels, i + len(EDGE) - 8) for i in range(len(INNER))]
    mlp(rows_ref, expand_ref, reduce_ref, 0, blocks, normed, inner, put)


def edge_rows(
    field_ref,
    halo_ref,
    matrix_ref,
    rows_ref,
    expand_ref,
    reduce_ref,
    old_ref,
    update_ref,
    conv,
    normed,
    inner,
):
    del old_ref
    channels, _, width = field_ref.shape

    def stack_of(c, ones):
        return columns_stack(jnp.concatenate([field_ref[c], halo_ref[c]], axis=0), ones)

    conv_rows(matrix_ref, stack_of, conv, channels, 24, 0, 16)
    for empty in (19, 23):
        update_ref[pl.ds(empty, channels, stride=24), :] = jnp.zeros((channels, width), jnp.float32)

    def put(n, change):
        update_ref[pl.ds(place_of(EDGE[n]), channels, stride=24), :] = change

    blocks = [conv_row(conv, channels, i) for i in range(len(EDGE))]
    mlp(rows_ref, expand_ref, reduce_ref, 0, blocks, normed, inner, put)


def neighbours(core_ref, cross_refs, group, groups):
    width = core_ref.shape[1]
    half = groups // 2
    m, upper = (half, 0) if group == groups else (group % half, group // half)
    core = core_ref[m * 32 : m * 32 + 32, :]
    cross = sum(ref[m * 32 : m * 32 + 32, :] for ref in cross_refs)
    lon_even = lax.rem(lax.axis_index("lon"), 2) == 0
    east = jnp.where(lon_even, core, cross)
    west = jnp.where(lon_even, cross, core)
    east = pltpu.roll(east, (HALO - 8 * upper) % width, 1)
    return east, pltpu.roll(west, width - 8, 1) if upper else west


def edge_columns(
    core_ref,
    cross_ref,
    wrap_ref,
    own_ref,
    ends_ref,
    matrix_ref,
    rows_ref,
    expand_ref,
    reduce_ref,
    strips,
    conv,
    normed,
    inner,
):
    channels, width = rows_ref.shape[2:]
    quarter = channels // 4
    groups = channels // 8
    lane32 = lanes((32, width))
    first_six = lane32 % 16 < HALO
    first_twelve = lane32 % 32 < 2 * HALO
    ones = jnp.ones((32, width), jnp.bfloat16)
    for g in range(groups):
        at = slice(g * 32, g * 32 + 32)
        east, west = neighbours(core_ref, (cross_ref, wrap_ref, own_ref), g, groups)
        own = ends_ref[at, :]
        at_west = jnp.where(first_six, west, own)
        at_east = jnp.where(first_six, own, east)
        for t in range(2):
            left = pltpu.roll(at_west, width - 16, 1) if t else at_west
            right = pltpu.roll(at_east, (2 * HALO - 16 * t) % width, 1)
            block = jnp.where(first_twelve, left, right)
            some = [channel_of(channels, g, 2 * n + t) for n in range(4)]
            matrix = jnp.concatenate(
                [matrix_ref[c * 24 : c * 24 + 24, :] for c in some], axis=0
            )
            stack = columns_stack(block, ones)
            result = jnp.dot(matrix, stack, preferred_element_type=jnp.float32)
            for n, c in enumerate(some):
                conv[pl.ds(c, 24, stride=pitch(channels)), :] = result[n * 24 : n * 24 + 24, :]

    order = {place_of(row): i for i, row in enumerate(EDGE + INNER)}
    lane = lanes((quarter, width))
    starts = [32 * (q // 2) + 6 * (q % 2) for q in range(8)]
    inside = [
        ((lane >= s + 3) & (lane < s + 9)) | ((lane >= s + 15) & (lane < s + 21)) for s in starts
    ]
    packs = []
    for p in range(3):
        parts = []
        for n in range(4):
            packed = jnp.zeros((quarter, width), jnp.float32)
            for q, start in enumerate(starts):
                if p * 8 + q in order:
                    row = order[p * 8 + q] * pitch(channels) + n * quarter
                    block = conv[row : row + quarter, :]
                    block = pltpu.roll(block, (start - 32 * n) % width, 1)
                    packed = jnp.where(inside[q], block, packed)
            parts.append(packed)
        packs.append(jnp.concatenate(parts, axis=0))

    def put(p, change):
        for q, start in enumerate(starts):
            near = pltpu.roll(change, (width - 6 - start) % width, 1)
            strips[pl.ds(p * 8 + q, channels, stride=24), :] = near

    blocks = [functools.partial(lambda block: block, packed) for packed in packs]
    mlp(rows_ref, expand_ref, reduce_ref, 0, blocks, normed, inner, put)


def second_layer(
    field_ref,
    mask_ref,
    halo_ref,
    halo_mask_ref,
    core_ref,
    cross_ref,
    wrap_ref,
    own_ref,
    strips,
    update_ref,
    matrix_ref,
    rows_ref,
    expand_ref,
    reduce_ref,
    out_ref,
    main_ref,
    conv,
    changes,
    normed,
    inner,
):
    channels, rows, width = out_ref.shape
    groups = channels // 8
    lane32 = lanes((32, width))
    lane24 = lanes((24, width))
    first_six = lane32 % 16 < HALO

    def beside_of(received, slot):
        beside = pltpu.roll(received, (width - HALO - 16 * slot) % width, 1)
        return beside.astype(jnp.float32)[0:24, :]

    def received(g):
        east, west = neighbours(core_ref, (cross_ref, wrap_ref, own_ref), g, groups)
        return jnp.where(first_six, west, east)

    main_mask = jnp.concatenate(
        [mask_ref[...].astype(jnp.float32), halo_mask_ref[0:8, :]], axis=0
    )
    side_mask = beside_of(received(groups), 0)
    low = lane24 < 3
    high = lane24 >= width - 3
    blank = jnp.zeros((8, width), jnp.float32)
    ones = jnp.ones((32, width), jnp.bfloat16)
    lane16 = lanes((16, width))
    away = {s: lane16 < s if s > 0 else lane16 >= width + s for s in range(-3, 4) if s}

    def halves(block):
        low_rows = block[:16, :].astype(jnp.bfloat16)
        return low_rows, jnp.concatenate([block[16:, :], blank], axis=0).astype(jnp.bfloat16)

    for g in range(groups):
        both = received(g)
        for j in range(8):
            c = channel_of(channels, g, j)
            near = strips[c * 24 : c * 24 + 24, :]
            far = pltpu.roll(near, width - 2 * HALO, 1)
            change = update_ref[c * 24 : c * 24 + 24, :]
            change = jnp.where(low, near, jnp.where(high, far, change))
            own = field_ref[c].astype(jnp.float32)
            halo = halo_ref[c].astype(jnp.float32)[:8, :]
            main = halves(main_mask * (jnp.concatenate([own, halo], axis=0) + change))
            main_ref[c] = main[0]
            change = jnp.where(high, near, far)
            beside = halves(side_mask * (beside_of(both, j) + change))
            stack = []
            for s in range(-3, 4):
                for part, other in zip(main, beside):
                    if s:
                        part = pltpu.roll(jnp.where(away[s], other, part), (-s) % width, 1)
                    stack.append(part)
            stack = jnp.concatenate(stack + [ones], axis=0)
            matrix = matrix_ref[c * 16 : c * 16 + 16, :]
            result = jnp.dot(matrix, stack, preferred_element_type=jnp.float32)
            conv[pl.ds(c, 16, stride=pitch(channels)), :] = result

    def put(n, change):
        changes[pl.ds(n, channels, stride=APART), :] = change

    blocks = [conv_row(conv, channels, i) for i in range(rows)]
    mlp(rows_ref, expand_ref, reduce_ref, 1, blocks, normed, inner, put)
    mask = main_mask[:rows, :]
    for c in range(channels):
        change = changes[c * APART : c * APART + rows, :]
        out_ref[c] = (mask * (main_ref[c].astype(jnp.float32) + change)).astype(jnp.bfloat16)


def per_device(
    nlat,
    nlon,
    field,
    land_mask,
    depth_kernel,
    depth_bias,
    norm_gain,
    norm_bias,
    w_expand,
    b_expand,
    w_reduce,
    b_reduce,
):
    channels, rows, width = field.shape
    layers, hidden = b_expand.shape
    bf16, f32 = jnp.bfloat16, jnp.float32
    edge = HALO * channels + 16

    def buffers(count):
        return [
            pltpu.VMEM((channels + 16, count * width), bf16),
            pltpu.VMEM((hidden, count * width), bf16),
        ]

    def pack(upper_if_even, after):
        return pl.pallas_call(
            functools.partial(pack_rows, upper_if_even),
            out_shape=jax.ShapeDtypeStruct((edge, width), bf16),
            in_specs=vmem(2) + [pl.BlockSpec(memory_space=pl.ANY)],
            out_specs=pl.BlockSpec(memory_space=pltpu.VMEM),
            scratch_shapes=[
                pltpu.VMEM(((channels + 1) * APART, width), f32),
                pltpu.VMEM((rows, width), f32),
            ],
            compiler_params=params(),
            cost_estimate=cost(4e9),
        )(field, land_mask, after)

    begun = pl.pallas_call(
        first_step,
        out_shape=jax.ShapeDtypeStruct((8, 128), f32),
        out_specs=pl.BlockSpec(memory_space=pltpu.VMEM),
        compiler_params=params(),
        cost_estimate=cost(4e9),
    )()
    first = pack(True, begun)
    second_sent = pack(False, first)

    alone = nlat == 2

    def at(d, lat):
        return d * nlat + lat

    pairs = []
    for d in range(nlon):
        for low in range(1, nlat - 1, 2):
            pairs += [(at(d, low), at(d, low + 1)), (at(d, low + 1), at(d, low))]
        pairs.append((at(d, nlat - 1), at(nlon - 1 - d, nlat - 1)))
        pairs.append((at(d, 0), at(d ^ 1, 0)))
    second = lax.ppermute(second_sent, ("lon", "lat"), pairs)
    pairs = []
    for low in range(0, nlat - 1, 2):
        pairs += [(low, low + 1), (low + 1, low)]
    first = lax.ppermute(first, "lat", pairs)

    kernel = depth_kernel.transpose(2, 3, 0, 1).reshape(49, layers, channels)
    matrix_one, matrix_two, by_channel, expand = pl.pallas_call(
        weights,
        out_shape=[
            jax.ShapeDtypeStruct((channels * 24, 256), bf16),
            jax.ShapeDtypeStruct((channels * 16, 256), bf16),
            jax.ShapeDtypeStruct((layers, 3, channels, 128), f32),
            jax.ShapeDtypeStruct((layers, hidden, channels + 16), bf16),
        ],
        in_specs=vmem(7),
        out_specs=vmem(4),
        scratch_shapes=[
            pltpu.VMEM(((channels + 1) * 24, 128), f32),
            pltpu.VMEM(((channels + 1) * 24, 128), f32),
            pltpu.VMEM((128, 128), f32),
            pltpu.VMEM((128, hidden), f32),
        ],
        compiler_params=params(),
        cost_estimate=cost(2e9),
    )(
        kernel,
        depth_bias,
        norm_gain,
        norm_bias,
        w_expand.transpose(0, 2, 1),
        b_expand,
        b_reduce,
    )
    update = pl.pallas_call(
        inner_rows,
        out_shape=jax.ShapeDtypeStruct(((channels + 1) * 24, width), f32),
        in_specs=vmem(5),
        out_specs=pl.BlockSpec(memory_space=pltpu.VMEM),
        scratch_shapes=[pltpu.VMEM((pitch(channels) * 17, width), f32)] + buffers(len(INNER)),
        compiler_params=params(),
        cost_estimate=cost(4e9),
    )(field, matrix_one, by_channel, expand, w_reduce)

    groups = channels // 8 + 1
    sent_rows = (channels // 16 + 1) * 32
    near_halo, near_mask, own_ends, wrap = pl.pallas_call(
        near_rows,
        out_shape=[
            jax.ShapeDtypeStruct((channels, 16, width), bf16),
            jax.ShapeDtypeStruct((16, width), f32),
            jax.ShapeDtypeStruct((groups * 16, width), bf16),
            jax.ShapeDtypeStruct((sent_rows, width), bf16),
        ],
        in_specs=vmem(3),
        out_specs=vmem(4),
        scratch_shapes=[
            pltpu.VMEM(((channels + 1) * APART, width), f32),
            pltpu.VMEM((groups * 32, width), bf16),
        ],
        compiler_params=params(),
        cost_estimate=cost(1e9),
    )(field, land_mask, first)
    if alone:
        pairs = []
        for lat in range(nlat):
            pairs += [(lat, at(nlon - 1, lat)), (at(nlon - 1, lat), lat)]
            pairs += [(at(d, lat), at(d, 1 - lat)) for d in range(1, nlon - 1)]
        wrap = lax.ppermute(wrap, ("lon", "lat"), pairs)
    else:
        wrap = jnp.zeros_like(wrap)
    halo, halo_mask, ends, cross = pl.pallas_call(
        functools.partial(far_rows, alone),
        out_shape=[
            jax.ShapeDtypeStruct((channels, 16, width), bf16),
            jax.ShapeDtypeStruct((16, width), f32),
            jax.ShapeDtypeStruct((groups * 32, width), bf16),
            jax.ShapeDtypeStruct((sent_rows, width), bf16),
        ],
        in_specs=vmem(4) + [pl.BlockSpec(memory_space=pl.ANY)],
        out_specs=vmem(4),
        scratch_shapes=[
            pltpu.VMEM(((channels + 1) * APART, width), f32),
            pltpu.VMEM((16, width), f32),
        ],
        compiler_params=params(),
    )(second, near_halo, near_mask, own_ends, update)
    core = pl.pallas_call(
        core_columns,
        out_shape=jax.ShapeDtypeStruct((sent_rows, width), bf16),
        in_specs=vmem(1) + [pl.BlockSpec(memory_space=pl.ANY)],
        out_specs=pl.BlockSpec(memory_space=pltpu.VMEM),
        compiler_params=params(),
    )(ends, cross)

    own = pl.pallas_call(
        functools.partial(mirrored_columns, alone),
        out_shape=jax.ShapeDtypeStruct((sent_rows, width), bf16),
        in_specs=vmem(1) + [pl.BlockSpec(memory_space=pl.ANY)],
        out_specs=pl.BlockSpec(memory_space=pltpu.VMEM),
        scratch_shapes=[
            pltpu.VMEM(((channels + 1) * APART, width), f32),
            pltpu.VMEM((16, width), f32),
            pltpu.VMEM((channels, 16, width), bf16),
            pltpu.VMEM((groups * 32, width), bf16),
        ],
        compiler_params=params(),
    )(second_sent, core)

    pairs = []
    for low in range(0, nlon, 2):
        pairs += [(low, low + 1), (low + 1, low)]
    core = lax.ppermute(core, "lon", pairs)
    pairs = []
    for lat in range(nlat):
        for low in range(1, nlon, 2):
            after = (low + 1) % nlon
            if after or not alone:
                pairs += [(at(low, lat), at(after, lat)), (at(after, lat), at(low, lat))]
            else:
                pairs += [(at(low, lat), at(low, 1 - lat)), (at(after, lat), at(after, 1 - lat))]
    cross = lax.ppermute(cross, ("lon", "lat"), pairs)

    update = pl.pallas_call(
        edge_rows,
        out_shape=jax.ShapeDtypeStruct(((channels + 1) * 24, width), f32),
        in_specs=vmem(7),
        out_specs=pl.BlockSpec(memory_space=pltpu.VMEM),
        scratch_shapes=[pltpu.VMEM((pitch(channels) * 17, width), f32)] + buffers(len(EDGE)),
        input_output_aliases={6: 0},
        compiler_params=params(),
        cost_estimate=cost(4e9),
    )(field, halo, matrix_one, by_channel, expand, w_reduce, update)

    strips = pl.pallas_call(
        edge_columns,
        out_shape=jax.ShapeDtypeStruct(((channels + 1) * 24, width), f32),
        in_specs=vmem(9),
        out_specs=pl.BlockSpec(memory_space=pltpu.VMEM),
        scratch_shapes=[pltpu.VMEM((pitch(channels) * 25, width), f32)] + buffers(3),
        compiler_params=params(),
    )(core, cross, wrap, own, ends, matrix_one, by_channel, expand, w_reduce)

    return pl.pallas_call(
        second_layer,
        out_shape=jax.ShapeDtypeStruct((channels, rows, width), bf16),
        in_specs=vmem(14),
        out_specs=pl.BlockSpec(memory_space=pltpu.VMEM),
        scratch_shapes=[
            pltpu.VMEM((channels, rows, width), bf16),
            pltpu.VMEM((pitch(channels) * 17, width), f32),
            pltpu.VMEM(((channels + 1) * APART, width), f32),
        ]
        + buffers(rows),
        compiler_params=params(),
    )(
        field,
        land_mask,
        halo,
        halo_mask,
        core,
        cross,
        wrap,
        own,
        strips,
        update,
        matrix_two,
        by_channel,
        expand,
        w_reduce,
    )


def solution(mesh):
    placed = (P(None, "lat", "lon"), P("lat", "lon"), P(), P(), P(), P(), P(), P(), P(), P())
    return jax.shard_map(
        functools.partial(per_device, mesh.shape["lat"], mesh.shape["lon"]),
        mesh=mesh,
        in_specs=placed,
        out_specs=P(None, "lat", "lon"),
        check_vma=False,
    )
```
